32 devices in a mesh: seq: 8 (over z, x), head: 4 (over y, core).
Axes of the slice: x: 2, y: 2, z: 4, core: 2. Of those that a mesh axis runs over, the one named last changes fastest.
Arguments:
- inputs: bfloat16 [4, 1024, 1024], P('head', 'seq'), may hold values from -6 to 6
- gain_attn: bfloat16 [1024], P(('seq', 'head')), may hold values from 0.099609375 to 1.8984375
- w_qkv: bfloat16 [1024, 3072], P(('seq', 'head')), may hold values from -0.1875 to 0.1875
- head_bias: float32 [16, 2], replicated, may hold values from -1 to 1
- w_out: bfloat16 [1024, 1024], P(('seq', 'head')), may hold values from -6 to 6
- gain_ffn: bfloat16 [1024], P(('seq', 'head')), may hold values from 0.099609375 to 1.8984375
- w_gate: bfloat16 [1024, 4096], P('seq', 'head'), may hold values from -0.1875 to 0.1875
- w_up: bfloat16 [1024, 4096], P('seq', 'head'), may hold values from -0.1875 to 0.1875
- w_down: bfloat16 [4096, 1024], P('head', 'seq'), may hold values from -0.09375 to 0.09375
- time_ids: int32 [4, 1024], replicated, may hold values from 0 to 511
- variate_ids: int32 [4, 1024], replicated, may hold values from 0 to 3
- seq_ids: int32 [4, 1024], replicated, may hold values from 0 to 11, as said below
- cotangent: bfloat16 [4, 1024, 1024], P('head', 'seq'), may hold values from -6 to 6
Outputs:
- output: bfloat16 [4, 1024, 1024], P('head', 'seq')
- grad_input: bfloat16 [4, 1024, 1024], P('head', 'seq')
- grad_gain_attn: float32 [1024], P(('seq', 'head'))
- grad_w_qkv: float32 [1024, 3072], P(('seq', 'head'))
- grad_head_bias: float32 [16, 2], replicated
- grad_w_out: float32 [1024, 1024], P(('seq', 'head'))
- grad_gain_ffn: float32 [1024], P(('seq', 'head'))
- grad_w_gate: float32 [1024, 4096], P('seq', 'head')
- grad_w_up: float32 [1024, 4096], P('seq', 'head')
- grad_w_down: float32 [4096, 1024], P('head', 'seq')
The draws below stay inside these ranges and needn't reach their ends.
Inputs may be any that keep to these rules, and one draw needn't show every extreme that they name: `seq_ids`: ids never fall along a window's 1024 positions, and no two windows hold the same id.
All inputs are finite; a program needn't handle non-finite values.
Results may differ from the reference program's by a relative error of at most 0.024.
Values may be sent and summed in bfloat16 or wider, within the bound.
No kernel may reach another device: no remote copies, remote signals or barrier semaphores. Data moves between devices by JAX's collectives and lax.ppermute only.
A program may use at most 256 MiB of HBM per device.

```python
import math
from functools import partial
import jax
import jax.numpy as jnp
from jax import lax

D = 1024
H = 16
HD = 64
FF = 4096
TOK_DEV = 128
SEQ_LEN = 1024
WINDOWS = 4


def draw_seq_ids(key, part):
    key = jax.random.fold_in(key, 7)
    head_key, tail_key = jax.random.split(key)
    leading = jax.random.randint(head_key, (WINDOWS, 1), 1, TOK_DEV)
    trailing = jax.random.randint(tail_key, (WINDOWS, 1), 1, TOK_DEV)
    places = jnp.arange(SEQ_LEN, dtype=jnp.int32)[None, :]
    within = (places >= leading).astype(jnp.int32) + (places >= SEQ_LEN - trailing).astype(jnp.int32)
    return within + 3 * jnp.arange(WINDOWS, dtype=jnp.int32)[:, None]


def place_ends(result, stream_key, smallest, top_value):
    extent = result.shape
    spot = [jax.random.randint(jax.random.fold_in(stream_key, axis), (), 0, extent[axis]) for axis in range(len(extent))]
    result = result.at[tuple(spot)].set(smallest)
    longest = extent.index(max(extent))
    spot[longest] = (spot[longest] + 1) % extent[longest]
    return result.at[tuple(spot)].set(top_value)


def block_scale(stream_key, shape, cuts, low, largest):
    loudness, own = 1.0, jax.random.fold_in(stream_key, 6)
    for dim, blocks in cuts:
        draws = jnp.exp(jax.random.uniform(jax.random.fold_in(own, dim), (blocks,), jnp.float32, low / len(cuts), largest / len(cuts)))
        loudness = loudness * jnp.repeat(draws, shape[dim] // blocks).reshape([-1 if axis == dim else 1 for axis in range(len(shape))])
    return loudness


def scatter_about(rng, shape, spread, most, cuts=(), held_as=jnp.bfloat16):
    gain = block_scale(rng, shape, cuts, -0.22, 0.18) if cuts else 1.0
    entries = jax.random.normal(rng, shape, jnp.float32) * spread * gain
    return jnp.minimum(jnp.maximum(entries, -most), most).astype(held_as)


def setup_inputs(seed: int = 0) -> dict:
    seeds = jax.random.split(jax.random.key(seed), 14)
    inputs = scatter_about(seeds[0], (WINDOWS, SEQ_LEN, D), 1.0, 6.0, ((0, 4), (1, 8)))
    gain_attn = jnp.clip(1.0 + 0.18 * jax.random.normal(seeds[1], (D,), jnp.float32), 0.099609375, 1.8984375).astype(jnp.bfloat16)
    w_qkv = scatter_about(seeds[2], (D, 3 * D), D ** -0.5, 0.1875, ((0, 32),))
    head_bias = jnp.clip(jax.random.uniform(seeds[3], (H, 2), jnp.float32, -1.0, 1.0), -1.0, 1.0)
    w_out = scatter_about(seeds[4], (D, D), (max(1, D // SEQ_LEN)) ** -0.5, 6.0, ((0, 32),))
    gain_ffn = jnp.clip(1.0 + 0.18 * jax.random.normal(seeds[5], (D,), jnp.float32), 0.099609375, 1.8984375).astype(jnp.bfloat16)
    w_gate = scatter_about(seeds[6], (D, FF), D ** -0.5, 0.1875, ((0, 8), (1, 4)))
    w_up = scatter_about(seeds[7], (D, FF), D ** -0.5, 0.1875, ((0, 8), (1, 4)))
    w_down = scatter_about(seeds[8], (FF, D), FF ** -0.5, 0.09375, ((0, 4), (1, 8)))
    time_ids = place_ends(jax.random.randint(seeds[9], (WINDOWS, SEQ_LEN), 0, 512), jax.random.fold_in(seeds[9], 1), 0, 511).astype(jnp.int32)
    variate_ids = place_ends(jax.random.randint(seeds[10], (WINDOWS, SEQ_LEN), 0, 4), jax.random.fold_in(seeds[10], 1), 0, 3).astype(jnp.int32)
    seq_ids = draw_seq_ids(jax.random.fold_in(seeds[13], 71), 0)
    cotangent = scatter_about(seeds[12], (WINDOWS, SEQ_LEN, D), 1.0, 6.0, ((0, 4), (1, 8)))
    return dict(inputs=inputs, gain_attn=gain_attn, w_qkv=w_qkv, head_bias=head_bias, w_out=w_out, gain_ffn=gain_ffn, w_gate=w_gate, w_up=w_up, w_down=w_down, time_ids=time_ids, variate_ids=variate_ids, seq_ids=seq_ids, cotangent=cotangent)


precise = lax.Precision.HIGHEST
epsilon = 1e-05

@jax.custom_vjp
def low(v):
    return lax.optimization_barrier(v.astype(jnp.bfloat16)).astype(jnp.float32)

@jax.custom_vjp
def low_back(v):
    return v

def low_keep(v):
    return (low(v), None)

def low_pass(kept, grad):
    return (grad,)

def back_keep(v):
    return (v, None)

def back_low(kept, grad):
    return (low(grad),)
low.defvjp(low_keep, low_pass)
low_back.defvjp(back_keep, back_low)

def rope_tables(stamps, dimension):
    halfway = dimension // 2
    frequency = jnp.exp(-math.log(10000.0) * jnp.arange(halfway, dtype=jnp.float32) / halfway)
    angles = stamps.astype(jnp.float32)[:, None] * frequency[None, :]
    return (jnp.cos(angles), jnp.sin(angles))

def rotate(values, cosine, sine_table):
    halfway = values.shape[-1] // 2
    leading = values[..., :halfway]
    trailing = values[..., halfway:]
    cosine = cosine[:, None, :]
    sine_table = sine_table[:, None, :]
    return jnp.concatenate([leading * cosine - trailing * sine_table, trailing * cosine + leading * sine_table], axis=-1)

def rms_scale(values, scaling):
    return values * lax.rsqrt(lax.optimization_barrier(jnp.mean(values * values, axis=-1, keepdims=True)) + epsilon) * scaling

def window_layer(params, window):
    tokens, stamps, variates, segments = window
    gain_attn, w_qkv, head_bias, w_out, gain_ffn, w_gate, w_up, w_down = params
    length = tokens.shape[0]
    normed = low(rms_scale(tokens, gain_attn))
    packed = low_back(jnp.dot(normed, w_qkv, precision=precise)).reshape(length, H, 3, HD)
    cosine, sine_table = rope_tables(stamps, HD)
    queries = low_back(low(rotate(packed[:, :, 0], cosine, sine_table)))
    key_rows = low_back(low(rotate(packed[:, :, 1], cosine, sine_table)))
    value_rows = low_back(low(packed[:, :, 2]))
    same_doc = segments[:, None] == segments[None, :]
    same_var = variates[:, None] == variates[None, :]

    def one_head(element):
        query_rows, keys_head, values_head, biases = element
        scores = jnp.dot(query_rows, keys_head.T, precision=precise) * HD ** (-0.5)
        scores = scores + jnp.where(same_var, biases[0], biases[1])
        scores = jnp.where(same_doc, low_back(scores), -1e+30)
        weights = jax.nn.softmax(scores, axis=-1)
        return jnp.dot(low(weights), values_head, precision=precise)
    attended = lax.map(jax.checkpoint(one_head), (jnp.moveaxis(queries, 1, 0), jnp.moveaxis(key_rows, 1, 0), jnp.moveaxis(value_rows, 1, 0), head_bias))
    attended = low_back(low(jnp.moveaxis(attended, 0, 1).reshape(length, H * HD)))
    middle = tokens + low_back(jnp.dot(attended, w_out, precision=precise))
    normed_two = low(rms_scale(middle, gain_ffn))
    gate_values = low_back(jnp.dot(normed_two, w_gate, precision=precise))
    up_values = low_back(jnp.dot(normed_two, w_up, precision=precise))
    hidden = low(jax.nn.silu(gate_values) * up_values)
    return middle + jnp.dot(hidden, w_down, precision=precise)

def reference(inputs, gain_attn, w_qkv, head_bias, w_out, gain_ffn, w_gate, w_up, w_down, time_ids, variate_ids, seq_ids, cotangent):
    params = tuple((weight.astype(jnp.float32) for weight in (gain_attn, w_qkv, head_bias, w_out, gain_ffn, w_gate, w_up, w_down)))

    def forward(tokens, weights):
        per_window = jax.checkpoint(partial(window_layer, weights))
        return lax.map(per_window, (tokens, time_ids, variate_ids, seq_ids))
    output, pullback = jax.vjp(forward, inputs.astype(jnp.float32), params)
    grad_input, gradients = pullback(cotangent.astype(jnp.float32))
    return (output.astype(jnp.bfloat16), grad_input.astype(jnp.bfloat16), gradients[0], gradients[1], gradients[2], gradients[3], gradients[4], gradients[5], gradients[6], gradients[7])
```

```python
import functools
import math

import jax
import jax.numpy as jnp
from jax import lax
from jax.experimental import pallas as pl
from jax.experimental.pallas import tpu as pltpu
from jax.sharding import PartitionSpec as P


epsilon = 1e-05
masked_score = -1e30
low = jnp.bfloat16
wide = jnp.float32
lanes = 128
half_lanes = 64


def dot(a, b):
    return jnp.dot(a, b, preferred_element_type=wide)


def dot_t(a, b):
    return lax.dot_general(a, b, (((1,), (1,)), ((), ())), preferred_element_type=wide)


def t_dot(a, b):
    return lax.dot_general(a, b, (((0,), (0,)), ((), ())), preferred_element_type=wide)


class Place:
    def __init__(self):
        self.seq_size = lax.axis_size("seq")
        self.head_size = lax.axis_size("head")
        self.z_size = self.seq_size // 2
        self.y_size = self.head_size // 2
        self.seq = lax.axis_index("seq")
        self.head = lax.axis_index("head")
        self.z, self.x = self.seq // 2, self.seq % 2
        self.y, self.c = self.head // 2, self.head % 2

    def along_z(self, value, step):
        return lax.ppermute(value, "seq", [(i, i ^ (2 * step)) for i in range(self.seq_size)])

    def along_x(self, value):
        return lax.ppermute(value, "seq", [(i, i ^ 1) for i in range(self.seq_size)])

    def along_c(self, value):
        return lax.ppermute(value, "head", [(i, i ^ 1) for i in range(self.head_size)])

    def along_xy(self, value, dx, dy):
        if dy == 0:
            return self.along_x(value)
        if dx == 0:
            return lax.ppermute(
                value, "head", [(i, i ^ (2 * dy)) for i in range(self.head_size)]
            )
        return lax.ppermute(
            value,
            ("seq", "head"),
            [
                (s * self.head_size + h, (s ^ dx) * self.head_size + (h ^ (2 * dy)))
                for s in range(self.seq_size)
                for h in range(self.head_size)
            ],
        )

    def turn(self, value):
        return lax.ppermute(
            value,
            ("seq", "head"),
            [
                (s * self.head_size + h, ((s & ~1) | (h & 1)) * self.head_size + ((h & ~1) | (s & 1)))
                for s in range(self.seq_size)
                for h in range(self.head_size)
            ],
        )

    def pairs(self):
        return [(dx, dy) for dy in range(self.y_size) for dx in range(2)]

    def gather_xy(self, value):
        return [value if d == (0, 0) else self.along_xy(value, *d) for d in self.pairs()]

    def scatter_xy(self, blocks):
        return [
            block if d == (0, 0) else self.along_xy(block, *d)
            for d, block in zip(self.pairs(), blocks)
        ]

    def gather_z(self, value):
        return [value if d == 0 else self.along_z(value, d) for d in range(self.z_size)]

    def scatter_z(self, blocks):
        return [block if d == 0 else self.along_z(block, d) for d, block in enumerate(blocks)]


def pick(bit, zero, one):
    return jnp.where(bit == 0, zero, one)


def xor_list(blocks, me):
    step = 1
    while step < len(blocks):
        on = (me // step) % 2
        blocks = [pick(on, blocks[i], blocks[i ^ step]) for i in range(len(blocks))]
        step *= 2
    return blocks


def reorder_kernel(me_ref, in_ref, out_ref):
    count = in_ref.shape[0]
    me = me_ref[0]

    @pl.loop(0, count)
    def _(i):
        out_ref[i] = in_ref[jnp.bitwise_xor(i, me)]


def reorder(blocks, me):
    return pl.pallas_call(
        reorder_kernel,
        out_shape=jax.ShapeDtypeStruct(blocks.shape, blocks.dtype),
        in_specs=[pl.BlockSpec(memory_space=pltpu.SMEM), pl.BlockSpec(memory_space=pltpu.VMEM)],
        out_specs=pl.BlockSpec(memory_space=pltpu.VMEM),
        compiler_params=pltpu.CompilerParams(vmem_limit_bytes=32 * 2**20),
        cost_estimate=pl.CostEstimate(flops=0, bytes_accessed=2 * blocks.size * 2, transcendentals=0),
    )(me.reshape(1).astype(jnp.int32), blocks)


def lane_ids(rows):
    return lax.broadcasted_iota(jnp.int32, (rows, lanes), 1)


def swap_halves(value):
    first = lane_ids(value.shape[0]) % half_lanes < half_lanes // 2
    return jnp.where(first, pltpu.roll(value, lanes - 32, 1), pltpu.roll(value, 32, 1))


def three_pieces(value):
    one = value.astype(low).astype(wide)
    rest = value - one
    two = rest.astype(low).astype(wide)
    return one, two, (rest - two).astype(low).astype(wide)


def attend_kernel(
    heads,
    bias_ref,
    near_ref,
    far_ref,
    w_ref,
    cosine_ref,
    sine_ref,
    kinds_ref,
    docs_col_ref,
    docs_row_ref,
    query_ref,
    key_ref,
    value_ref,
    out_ref,
):
    rows = near_ref.shape[0]
    length = 2 * rows
    step = min(rows, 256)
    padded = w_ref.shape[1] // 3
    for part, source in enumerate((near_ref, far_ref)):
        for start in range(0, rows, step):
            at = pl.ds(part * rows + start, step)
            packed = dot(source[start : start + step, :], w_ref[...])
            cosine, sine = cosine_ref[at, :], sine_ref[at, :]
            lane = lane_ids(step)
            kind = kinds_ref[at, :]
            own = (lane == 64 + kind).astype(wide)
            own_two = (lane == 68 + kind).astype(wide)
            extra_query = ((lane == 72 + kind) | (lane == 76)).astype(wide)
            extra_key = own + own_two + ((lane >= 77) & (lane < 80)).astype(wide)
            extra_value = ((lane >= 64) & (lane < 67)).astype(wide)
            for head in range(heads):
                base = head // 2 * lanes
                query = packed[:, base : base + lanes]
                key = packed[:, padded + base : padded + base + lanes]
                value = packed[:, 2 * padded + base : 2 * padded + base + lanes]
                query = (query * cosine + swap_halves(query) * sine).astype(low).astype(wide) * 0.125
                key = key * cosine + swap_halves(key) * sine
                if head % 2:
                    query, key, value = (pltpu.roll(v, half_lanes, 1) for v in (query, key, value))
                body = lane < half_lanes
                extra = extra_query + own * bias_ref[0, head] + own_two * bias_ref[1, head]
                query_ref[head, at, :] = jnp.where(body, query, extra).astype(low)
                key_ref[head, at, :] = jnp.where(body, key, extra_key).astype(low)
                value_ref[head, at, :] = jnp.where(body, value, extra_value).astype(low)
    block = min(length, 256)
    lane = lane_ids(block)

    @pl.loop(0, length // block)
    def _(i):
        at = pl.ds(pl.multiple_of(i * block, block), block)
        allowed = docs_col_ref[at, :] == docs_row_ref[...]
        done = []
        for head in range(heads):
            query = query_ref[head, at, :]
            scores = jnp.where(allowed, dot_t(query, key_ref[head]), masked_score)
            top = jnp.max(scores, axis=1, keepdims=True)
            weights = jnp.exp(scores - top).astype(low)
            summed = dot(weights, value_ref[head])
            total = summed[:, half_lanes : half_lanes + 1]
            one, two, three = three_pieces(-(top + jnp.log(total)))
            extra = jnp.where(lane == 77, one, jnp.where(lane == 78, two, jnp.where(lane == 79, three, 0.0)))
            query_ref[head, at, :] = jnp.where(lane < 77, query.astype(wide), extra).astype(low)
            done.append(summed / total)
        for base in range(0, heads, 2):
            both = done[base]
            if base + 1 < heads:
                both = jnp.where(lane < half_lanes, both, pltpu.roll(done[base + 1], half_lanes, 1))
            out_ref[at, base // 2 * lanes : (base // 2 + 1) * lanes] = both.astype(low)


def attend(bias, near, far, w, cosine, sine, kinds, docs, heads):
    length = 2 * near.shape[0]
    padded = w.shape[1] // 3
    vmem = pl.BlockSpec(memory_space=pltpu.VMEM)
    whole = jax.ShapeDtypeStruct((heads, length, lanes), low)
    flops = 2 * length * near.shape[1] * w.shape[1] + 4 * heads * length * length * lanes
    return pl.pallas_call(
        functools.partial(attend_kernel, heads),
        out_shape=(whole, whole, whole, jax.ShapeDtypeStruct((length, padded), low)),
        in_specs=[pl.BlockSpec(memory_space=pltpu.SMEM)] + [vmem] * 8,
        out_specs=(vmem, vmem, vmem, vmem),
        compiler_params=pltpu.CompilerParams(vmem_limit_bytes=48 * 2**20),
        cost_estimate=pl.CostEstimate(
            flops=flops, bytes_accessed=8 * 2**20, transcendentals=heads * length * length
        ),
    )(bias, near, far, w, cosine, sine, kinds, docs.reshape(length, 1), docs.reshape(1, length))


def attend_grad_kernel(
    heads,
    query_ref,
    key_ref,
    value_ref,
    out_ref,
    grad_out_ref,
    cosine_ref,
    sine_ref,
    kinds_ref,
    docs_col_ref,
    docs_row_ref,
    packed_ref,
    bias_ref,
    grad_query_ref,
    grad_key_ref,
    grad_value_ref,
):
    length = query_ref.shape[1]
    padded = packed_ref.shape[1] // 3
    block = min(length, 256)
    lane = lane_ids(block)
    grad_key_ref[...] = jnp.zeros_like(grad_key_ref)
    grad_value_ref[...] = jnp.zeros_like(grad_value_ref)

    @pl.loop(0, length // block)
    def _(i):
        at = pl.ds(pl.multiple_of(i * block, block), block)
        allowed = docs_col_ref[...] == docs_row_ref[:, at]
        for head in range(heads):
            columns = slice(head // 2 * lanes, (head // 2 + 1) * lanes)
            grad_out = grad_out_ref[at, columns].astype(wide)
            product = grad_out * out_ref[at, columns].astype(wide)
            mine = (lane >= half_lanes) if head % 2 else (lane < half_lanes)
            row_dot = jnp.sum(jnp.where(mine, product, 0.0), axis=1, keepdims=True)
            one, two, three = three_pieces(-row_dot)
            if head % 2:
                grad_out = pltpu.roll(grad_out, half_lanes, 1)
            extra = jnp.where(lane == 64, one, jnp.where(lane == 65, two, jnp.where(lane == 66, three, 0.0)))
            grad_out = jnp.where(lane < half_lanes, grad_out, extra).astype(low)
            query, key = query_ref[head, at, :], key_ref[head]
            weights = jnp.exp(jnp.where(allowed, dot_t(key, query), masked_score))
            grad_scores = (weights * dot_t(value_ref[head], grad_out)).astype(low)
            grad_value_ref[head] += dot(weights.astype(low), grad_out)
            grad_key_ref[head] += dot(grad_scores, query)
            grad_query_ref[head, at, :] = t_dot(grad_scores, key)

    for start in range(0, length, block):
        at = slice(start, start + block)
        cosine, sine = cosine_ref[at, :], sine_ref[at, :]
        for base in range(0, heads, 2):

            def joined(ref):
                both = ref[base, at, :]
                if base + 1 < heads:
                    both = jnp.where(lane < half_lanes, both, pltpu.roll(ref[base + 1, at, :], half_lanes, 1))
                else:
                    both = jnp.where(lane < half_lanes, both, 0.0)
                return both

            columns = base // 2 * lanes
            query = joined(grad_query_ref) * 0.125
            key = joined(grad_key_ref)
            value = joined(grad_value_ref)
            query = query * cosine - swap_halves(query) * sine
            key = key * cosine - swap_halves(key) * sine
            for part, result in enumerate((query, key, value)):
                packed_ref[at, part * padded + columns : part * padded + columns + lanes] = result.astype(low)
    every = lane_ids(length)
    kinds = kinds_ref[...]
    for head in range(heads):
        grads = grad_key_ref[head]
        same = jnp.sum(jnp.where(every == 72 + kinds, grads, 0.0))
        total = jnp.sum(jnp.where(every == 76, grads, 0.0))
        bias_ref[head, 0] = same
        bias_ref[head, 1] = total - same


def attend_grad(query, key, value, out, grad_out, cosine, sine, kinds, docs, padded):
    heads, length, _ = query.shape
    vmem = pl.BlockSpec(memory_space=pltpu.VMEM)
    scratch = pltpu.VMEM((heads, length, lanes), wide)
    return pl.pallas_call(
        functools.partial(attend_grad_kernel, heads),
        out_shape=(
            jax.ShapeDtypeStruct((length, 3 * padded), low),
            jax.ShapeDtypeStruct((heads, 2), wide),
        ),
        in_specs=[vmem] * 10,
        out_specs=(vmem, pl.BlockSpec(memory_space=pltpu.SMEM)),
        scratch_shapes=[scratch] * 3,
        compiler_params=pltpu.CompilerParams(vmem_limit_bytes=48 * 2**20),
        cost_estimate=pl.CostEstimate(
            flops=10 * heads * length * length * lanes,
            bytes_accessed=8 * 2**20,
            transcendentals=heads * length * length,
        ),
    )(query, key, value, out, grad_out, cosine, sine, kinds, docs.reshape(length, 1), docs.reshape(1, length))


def rope_tables(stamps, dimension):
    halfway = dimension // 2
    frequency = jnp.exp(-math.log(10000.0) * jnp.arange(halfway, dtype=wide) / halfway)
    repeated = jnp.tile(frequency, lanes // halfway)
    angles = stamps.astype(wide)[:, None] * repeated[None, :]
    sign = jnp.where(jnp.arange(lanes) % dimension < halfway, -1.0, 1.0)
    return (jnp.cos(angles), jnp.sin(angles) * sign[None, :])


def shards(
    inputs,
    gain_attn,
    w_qkv,
    head_bias,
    w_out,
    gain_ffn,
    w_gate,
    w_up,
    w_down,
    time_ids,
    variate_ids,
    seq_ids,
    cotangent,
):
    at = Place()
    z_size, y_size = at.z_size, at.y_size
    tokens = inputs[0].astype(wide)
    rows, width = tokens.shape
    head_count = head_bias.shape[0]
    head_dim = width // head_count
    groups = at.seq_size
    heads = head_count // groups
    padded = (heads + 1) // 2 * lanes
    share = width // (at.seq_size * at.head_size)
    group = 2 * at.z + at.c
    window = 2 * at.y + at.x

    inverse_one = lax.rsqrt(jnp.mean(tokens * tokens, axis=-1, keepdims=True) + epsilon)
    unit = tokens * inverse_one
    near = jnp.concatenate(at.gather_z(at.turn(unit.astype(low))), axis=0)
    far = at.along_c(near)

    gain_one = gain_attn.astype(wide)[:, None]
    scaled = (w_qkv.astype(wide) * gain_one).astype(low)

    def to_parts(columns):
        parts = columns.reshape(-1, groups, heads, 3, head_dim).transpose(0, 1, 3, 2, 4)
        parts = parts.reshape(-1, groups, 3, heads * head_dim)
        parts = jnp.pad(parts, ((0, 0), (0, 0), (0, 0), (0, padded - heads * head_dim)))
        return parts.reshape(-1, groups, 3 * padded)

    parts = to_parts(scaled).reshape(share, z_size, 2, 3 * padded)
    core_own = pick(at.c, parts[:, :, 0], parts[:, :, 1])
    core_other = at.along_c(pick(at.c, parts[:, :, 1], parts[:, :, 0]))
    both = jnp.stack([core_own, core_other])
    sent = [
        lax.dynamic_index_in_dim(both, jnp.bitwise_xor(at.z, d), axis=2, keepdims=False)
        for d in range(z_size)
    ]
    by_z = jnp.stack(at.scatter_z(sent))
    by_xy = jnp.stack(at.gather_xy(by_z.reshape(2 * z_size * share, 3 * padded)))
    blocks = by_xy.reshape(y_size, 2, z_size, 2, share, 3 * padded).transpose(2, 1, 0, 3, 4, 5)
    device_id = at.seq * at.head_size + at.head
    w_heads = reorder(blocks.reshape(-1, share, 3 * padded), device_id).reshape(width, 3 * padded)

    def of_window(ids):
        row = lax.dynamic_index_in_dim(ids, window, axis=0, keepdims=False).reshape(z_size, 2, rows)
        order = [
            lax.dynamic_slice(
                row, (jnp.bitwise_xor(at.z, d), jnp.bitwise_xor(at.c, e), 0), (1, 1, rows)
            ).reshape(rows)
            for e in range(2)
            for d in range(z_size)
        ]
        return jnp.concatenate(order)

    docs = of_window(seq_ids)
    kinds = of_window(variate_ids)[:, None]
    cosine, sine = rope_tables(of_window(time_ids), head_dim)
    local_bias = lax.dynamic_slice_in_dim(head_bias, group * heads, heads, 0)
    difference = local_bias[:, 0] - local_bias[:, 1]
    difference_high = difference.astype(low).astype(wide)
    bias = jnp.stack([difference_high, difference - difference_high])

    depth, units = w_gate.shape[0], w_gate.shape[1] // 2
    stacked = jnp.concatenate([w_gate, w_up, w_down.T], axis=1).reshape(depth, 3, 2, units)
    mine = pick(at.x, stacked[:, :, 0], stacked[:, :, 1]).reshape(depth, 3 * units)
    other = at.along_x(pick(at.x, stacked[:, :, 1], stacked[:, :, 0]).reshape(depth, 3 * units))
    z_block = jnp.concatenate([pick(at.x, mine, other), pick(at.x, other, mine)], axis=0)
    w_ffn = jnp.concatenate(at.gather_z(z_block), axis=0)
    w_gate_up, w_down_t = w_ffn[:, : 2 * units], w_ffn[:, 2 * units :]

    z_columns = width // z_size

    def turn_columns(value):
        pieces = [value[:, i * z_columns : (i + 1) * z_columns] for i in range(z_size)]
        return jnp.concatenate(xor_list(pieces, at.z), axis=1)

    def gather_tokens(value):
        near_rows = jnp.concatenate(at.gather_xy(value), axis=0)
        return jnp.concatenate([near_rows, at.along_c(near_rows)], axis=0)

    grad_out = cotangent[0]
    grad_out_all = gather_tokens(turn_columns(grad_out))

    out_and_gain = jnp.concatenate(
        [w_out, jnp.pad(gain_ffn[:, None], ((0, 0), (0, lanes - 1)))], axis=1
    )
    gathered = lax.all_gather(out_and_gain, ("seq", "head"), axis=0, tiled=True)
    gain_two = gathered[:, width].astype(wide)
    out_rows = reorder(gathered[:, :width].reshape(groups, -1, width), at.seq)
    out_rows = out_rows.reshape(z_size, 2, -1, width).transpose(1, 0, 2, 3).reshape(width, width)

    query, key, value, attended = attend(bias, near, far, w_heads, cosine, sine, kinds, docs, heads)

    group_width = heads * head_dim
    sent = attended[:, :group_width].reshape(2, z_size, rows, group_width)
    received = at.scatter_z([sent[:, d] for d in range(z_size)])
    kept = jnp.concatenate([block[0] for block in received], axis=1)
    passed = at.along_c(jnp.concatenate([block[1] for block in received], axis=1))
    merged = at.turn(jnp.concatenate([kept, passed], axis=1))

    middle = tokens + dot(merged, out_rows)
    inverse_two = lax.rsqrt(jnp.mean(middle * middle, axis=-1, keepdims=True) + epsilon)
    normed_two = (middle * inverse_two * gain_two).astype(low)
    normed_two_all = gather_tokens(turn_columns(normed_two))

    gate_up = dot(normed_two_all, w_gate_up)
    gate_values, up_values = gate_up[:, :units], gate_up[:, units:]
    sigmoid_gate = jax.nn.sigmoid(gate_values)
    activated = gate_values * sigmoid_gate
    hidden = (activated * up_values).astype(low)
    grad_hidden = dot(grad_out_all, w_down_t)
    grad_gate = (
        grad_hidden * up_values * sigmoid_gate * (1.0 + gate_values * (1.0 - sigmoid_gate))
    ).astype(low)
    grad_up = (grad_hidden * activated).astype(low)
    grad_gate_up = jnp.concatenate([grad_gate, grad_up], axis=1)

    def scatter_tokens(part):
        cut = part.shape[0] // 2
        kept = part[:cut] + at.along_c(part[cut:].astype(low)).astype(wide)
        received = at.scatter_xy([kept[:rows]] + [
            kept[i * rows : (i + 1) * rows].astype(low) for i in range(1, 2 * y_size)
        ])
        return turn_columns(functools.reduce(jnp.add, [block.astype(wide) for block in received]))

    upstream = scatter_tokens(dot_t(grad_gate_up, w_gate_up)) * gain_two
    grad_middle = (
        grad_out.astype(wide)
        + inverse_two * upstream
        - middle * inverse_two**3 * jnp.mean(upstream * middle, axis=-1, keepdims=True)
    )
    grad_branch = grad_middle.astype(low)
    grad_merged = dot_t(grad_branch, out_rows).astype(low)

    turned = at.turn(grad_merged)
    cut = width // 2
    kept, passed = turned[:, :cut], at.along_c(turned[:, cut:])
    sent = [
        jnp.stack([part[:, d * group_width : (d + 1) * group_width] for part in (kept, passed)])
        for d in range(z_size)
    ]
    received = jnp.stack(at.scatter_z(sent), axis=1)
    grad_attended = received.reshape(2 * z_size * rows, group_width)
    if padded > group_width:
        grad_attended = jnp.pad(grad_attended, ((0, 0), (0, padded - group_width)))
    grad_packed, bias_grad = attend_grad(
        query, key, value, attended, grad_attended, cosine, sine, kinds, docs, padded
    )

    half = near.shape[0]
    upstream_far = dot_t(grad_packed[half:], w_heads).astype(low)
    upstream_near = dot_t(grad_packed[:half], w_heads) + at.along_c(upstream_far).astype(wide)
    received = at.scatter_z([upstream_near[:rows]] + [
        upstream_near[i * rows : (i + 1) * rows].astype(low) for i in range(1, z_size)
    ])
    upstream_one = functools.reduce(jnp.add, [block.astype(wide) for block in received])
    upstream_one = at.turn(upstream_one.astype(low)).astype(wide)
    grad_input = grad_middle + inverse_one * (
        upstream_one - unit * jnp.mean(upstream_one * unit, axis=-1, keepdims=True)
    )

    grad_heads = t_dot(near, grad_packed[:half]) + t_dot(far, grad_packed[half:])
    grad_heads = grad_heads.astype(low).reshape(z_size, 2, y_size, 2, share, 3 * padded)

    def rows_of(dx, dy):
        picked = lax.dynamic_slice(
            grad_heads,
            (0, jnp.bitwise_xor(at.x, dx), jnp.bitwise_xor(at.y, dy), 0, 0, 0),
            (z_size, 1, 1, 2, share, 3 * padded),
        )
        return picked.reshape(z_size, 2, share, 3 * padded)

    received = at.scatter_xy([rows_of(*d) for d in at.pairs()])
    summed = functools.reduce(jnp.add, [block.astype(wide) for block in received]).astype(low)
    sent = [
        lax.dynamic_index_in_dim(summed, jnp.bitwise_xor(at.z, d), axis=0, keepdims=False)
        for d in range(z_size)
    ]
    received = jnp.stack(at.scatter_z(sent))
    core_own = pick(at.c, received[:, 0], received[:, 1])
    core_other = at.along_c(pick(at.c, received[:, 1], received[:, 0]))
    by_group = jnp.stack([core_own, core_other], axis=1).reshape(groups, share, 3 * padded)
    by_group = reorder(by_group, group).astype(wide).reshape(groups, share, 3, padded)
    by_group = by_group[..., :group_width].reshape(groups, share, 3, heads, head_dim)
    raw = by_group.transpose(1, 0, 3, 2, 4).reshape(share, 3 * width)
    grad_w_qkv = raw * gain_one
    grad_gain_attn = jnp.sum(raw * w_qkv.astype(wide), axis=1)

    full_bias = lax.dynamic_update_slice_in_dim(
        jnp.zeros((head_count, 2), wide), bias_grad, group * heads, 0
    )
    full_bias = full_bias + at.along_c(full_bias)
    for d in range(int(math.log2(z_size))):
        full_bias = full_bias + at.along_z(full_bias, 1 << d)
    full_bias = full_bias + at.along_x(full_bias)
    for d in range(int(math.log2(y_size))):
        full_bias = full_bias + at.along_xy(full_bias, 0, 1 << d)

    grad_out_rows = t_dot(merged, grad_branch).astype(low)
    grad_out_rows = grad_out_rows.reshape(2, z_size, -1, width).transpose(1, 0, 2, 3)
    grad_out_rows = reorder(grad_out_rows.reshape(groups, -1, width), at.seq).reshape(width, width)
    grad_w_out = lax.psum_scatter(
        grad_out_rows, ("seq", "head"), scatter_dimension=0, tiled=True
    ).astype(wide)

    sent = []
    for d in range(z_size):
        columns = slice(d * z_columns, (d + 1) * z_columns)
        sent.append(
            jnp.concatenate(
                [
                    t_dot(normed_two_all[:, columns], grad_gate_up),
                    t_dot(grad_out_all[:, columns], hidden),
                ],
                axis=1,
            )
        )
    received = at.scatter_z(sent[:1] + [block.astype(low) for block in sent[1:]])
    summed = functools.reduce(jnp.add, [block.astype(wide) for block in received])
    mine = pick(at.x, summed[:depth], summed[depth:])
    other = at.along_x(pick(at.x, summed[depth:], summed[:depth]).astype(low)).astype(wide)
    first, second = pick(at.x, mine, other), pick(at.x, other, mine)
    grad_w_gate, grad_w_up, grad_w_down_t = (
        jnp.concatenate([first[:, i * units : (i + 1) * units], second[:, i * units : (i + 1) * units]], axis=1)
        for i in range(3)
    )
    gain_part = jnp.sum(grad_w_gate * w_gate.astype(wide) + grad_w_up * w_up.astype(wide), axis=1)
    gain_part = gain_part + at.along_c(gain_part)
    for d in range(int(math.log2(y_size))):
        gain_part = gain_part + at.along_xy(gain_part, 0, 1 << d)
    grad_gain_ffn = lax.dynamic_slice_in_dim(gain_part, at.head * share, share, 0) / gain_ffn.astype(wide)

    output = middle + scatter_tokens(dot_t(hidden, w_down_t))

    return (
        output.astype(low).reshape(1, rows, width),
        grad_input.astype(low).reshape(1, rows, width),
        grad_gain_attn,
        grad_w_qkv,
        full_bias,
        grad_w_out,
        grad_gain_ffn,
        grad_w_gate,
        grad_w_up,
        grad_w_down_t.T,
    )


def solution(mesh):
    placed = (
        P("head", "seq", None),
        P(("seq", "head")),
        P(("seq", "head"), None),
        P(),
        P(("seq", "head"), None),
        P(("seq", "head")),
        P("seq", "head"),
        P("seq", "head"),
        P("head", "seq"),
        P(),
        P(),
        P(),
        P("head", "seq", None),
    )
    return jax.shard_map(
        shards,
        mesh=mesh,
        in_specs=placed,
        out_specs=(
            P("head", "seq", None),
            P("head", "seq", None),
            P(("seq", "head")),
            P(("seq", "head"), None),
            P(),
            P(("seq", "head"), None),
            P(("seq", "head")),
            P("seq", "head"),
            P("seq", "head"),
            P("head", "seq"),
        ),
        check_vma=False,
    )
```

```python
import functools
import math

import jax
import jax.numpy as jnp
from jax import lax
from jax.experimental import pallas as pl
from jax.experimental.layout import Layout, with_layout_constraint
from jax.experimental.pallas import tpu as pltpu
from jax.sharding import PartitionSpec as P


epsilon = 1e-05
masked_score = -1e30
low = jnp.bfloat16
wide = jnp.float32
lanes = 128
half_lanes = 64


def dot(a, b):
    return jnp.dot(a, b, preferred_element_type=wide)


def dot_t(a, b):
    return lax.dot_general(a, b, (((1,), (1,)), ((), ())), preferred_element_type=wide)


def t_dot(a, b):
    return lax.dot_general(a, b, (((0,), (0,)), ((), ())), preferred_element_type=wide)


class Place:
    def __init__(self):
        self.seq_size = lax.axis_size("seq")
        self.head_size = lax.axis_size("head")
        self.z_size = self.seq_size // 2
        self.y_size = self.head_size // 2
        self.seq = lax.axis_index("seq")
        self.head = lax.axis_index("head")
        self.z, self.x = self.seq // 2, self.seq % 2
        self.y, self.c = self.head // 2, self.head % 2

    def along_z(self, value, step):
        return lax.ppermute(value, "seq", [(i, i ^ (2 * step)) for i in range(self.seq_size)])

    def along_x(self, value):
        return lax.ppermute(value, "seq", [(i, i ^ 1) for i in range(self.seq_size)])

    def along_c(self, value):
        return lax.ppermute(value, "head", [(i, i ^ 1) for i in range(self.head_size)])

    def along_xy(self, value, dx, dy):
        if dy == 0:
            return self.along_x(value)
        if dx == 0:
            return lax.ppermute(
                value, "head", [(i, i ^ (2 * dy)) for i in range(self.head_size)]
            )
        return lax.ppermute(
            value,
            ("seq", "head"),
            [
                (s * self.head_size + h, (s ^ dx) * self.head_size + (h ^ (2 * dy)))
                for s in range(self.seq_size)
                for h in range(self.head_size)
            ],
        )

    def turn(self, value):
        return lax.ppermute(
            value,
            ("seq", "head"),
            [
                (s * self.head_size + h, ((s & ~1) | (h & 1)) * self.head_size + ((h & ~1) | (s & 1)))
                for s in range(self.seq_size)
                for h in range(self.head_size)
            ],
        )

    def pairs(self):
        return [(dx, dy) for dy in range(self.y_size) for dx in range(2)]

    def gather_xy(self, value):
        return [value if d == (0, 0) else self.along_xy(value, *d) for d in self.pairs()]

    def scatter_xy(self, blocks):
        return [
            block if d == (0, 0) else self.along_xy(block, *d)
            for d, block in zip(self.pairs(), blocks)
        ]

    def columns_z(self):
        return [[x + 2 * z for z in range(self.z_size)] for x in range(2)]

    def gather_z(self, value):
        return [value if d == 0 else self.along_z(value, d) for d in range(self.z_size)]

    def scatter_z(self, blocks):
        return [block if d == 0 else self.along_z(block, d) for d, block in enumerate(blocks)]

    def gather_steps(self, value, moves):
        held = value[None]
        for move in moves:
            held = jnp.concatenate([held, move(held)], axis=0)
        return held

    def scatter_steps(self, held, moves):
        for move in reversed(moves):
            cut = held.shape[0] // 2
            held = held[:cut].astype(wide) + move(held[cut:].astype(low)).astype(wide)
        return held[0]

    def xy_moves(self):
        steps = [1 << i for i in range(self.y_size.bit_length() - 1)]
        return [self.along_x] + [functools.partial(self.along_xy, dx=0, dy=step) for step in steps]

    def z_moves(self):
        steps = [1 << i for i in reversed(range(self.z_size.bit_length() - 1))]
        return [functools.partial(self.along_z, step=step) for step in steps]

    def z_order(self):
        order = [0]
        for step in [1 << i for i in reversed(range(self.z_size.bit_length() - 1))]:
            order = order + [step ^ d for d in order]
        return order


def called(name, move, *operands):
    with jax.named_scope(name):
        return move(*operands)


def tied(*values):
    return lax.optimization_barrier(values)


def pick(bit, zero, one):
    return jnp.where(bit == 0, zero, one)


def xor_list(blocks, me):
    step = 1
    while step < len(blocks):
        on = (me // step) % 2
        blocks = [pick(on, blocks[i], blocks[i ^ step]) for i in range(len(blocks))]
        step *= 2
    return blocks


def place_kernel(masks, me_ref, in_ref, out_ref):
    for i, mask in enumerate(masks):
        out_ref[jnp.bitwise_xor(me_ref[0], mask)] = in_ref[i]


def fetch_kernel(masks, me_ref, in_ref, out_ref):
    for i, mask in enumerate(masks):
        out_ref[i] = in_ref[jnp.bitwise_xor(me_ref[0], mask)]


def move_blocks(kernel, blocks, me, masks):
    return pl.pallas_call(
        functools.partial(kernel, masks),
        out_shape=jax.ShapeDtypeStruct(blocks.shape, blocks.dtype),
        in_specs=[pl.BlockSpec(memory_space=pltpu.SMEM), pl.BlockSpec(memory_space=pltpu.VMEM)],
        out_specs=pl.BlockSpec(memory_space=pltpu.VMEM),
        compiler_params=pltpu.CompilerParams(vmem_limit_bytes=32 * 2**20),
        cost_estimate=pl.CostEstimate(flops=0, bytes_accessed=4 * blocks.size, transcendentals=0),
    )(me.reshape(1).astype(jnp.int32), blocks)


def place(blocks, me, masks):
    return move_blocks(place_kernel, blocks, me, masks)


def fetch(blocks, me, masks):
    return move_blocks(fetch_kernel, blocks, me, masks)


def lane_ids(rows):
    return lax.broadcasted_iota(jnp.int32, (rows, lanes), 1)


def swap_halves(value):
    first = lane_ids(value.shape[0]) % half_lanes < half_lanes // 2
    return jnp.where(first, pltpu.roll(value, lanes - 32, 1), pltpu.roll(value, 32, 1))


def three_pieces(value):
    one = value.astype(low).astype(wide)
    rest = value - one
    two = rest.astype(low).astype(wide)
    return one, two, (rest - two).astype(low).astype(wide)


def attend_kernel(
    heads,
    bias_ref,
    near_ref,
    far_ref,
    w_ref,
    cosine_ref,
    sine_ref,
    kinds_ref,
    docs_col_ref,
    docs_row_ref,
    query_ref,
    key_ref,
    value_ref,
    out_ref,
):
    rows = near_ref.shape[0]
    length = 2 * rows
    step = min(rows, 256)
    padded = w_ref.shape[1] // 3
    for part, source in enumerate((near_ref, far_ref)):
        for start in range(0, rows, step):
            at = pl.ds(part * rows + start, step)
            packed = dot(source[start : start + step, :], w_ref[...])
            cosine, sine = cosine_ref[at, :], sine_ref[at, :]
            lane = lane_ids(step)
            kind = kinds_ref[at, :1]
            own = (lane == 64 + kind).astype(wide)
            own_two = (lane == 68 + kind).astype(wide)
            extra_query = ((lane == 72 + kind) | (lane == 76)).astype(wide)
            extra_key = own + own_two + ((lane >= 77) & (lane < 80)).astype(wide)
            extra_value = ((lane >= 64) & (lane < 67)).astype(wide)
            for head in range(heads):
                base = head // 2 * lanes
                query = packed[:, base : base + lanes]
                key = packed[:, padded + base : padded + base + lanes]
                value = packed[:, 2 * padded + base : 2 * padded + base + lanes]
                query = (query * cosine + swap_halves(query) * sine).astype(low).astype(wide) * 0.125
                key = key * cosine + swap_halves(key) * sine
                if head % 2:
                    query, key, value = (pltpu.roll(v, half_lanes, 1) for v in (query, key, value))
                body = lane < half_lanes
                extra = extra_query + own * bias_ref[0, head] + own_two * bias_ref[1, head]
                query_ref[head, at, :] = jnp.where(body, query, extra).astype(low)
                key_ref[head, at, :] = jnp.where(body, key, extra_key).astype(low)
                value_ref[head, at, :] = jnp.where(body, value, extra_value).astype(low)
    block = min(length, 256)
    lane = lane_ids(block)

    @pl.loop(0, length // block)
    def _(i):
        at = pl.ds(pl.multiple_of(i * block, block), block)
        allowed = docs_col_ref[at, :1] == docs_row_ref[...]
        done = []
        for head in range(heads):
            query = query_ref[head, at, :]
            scores = jnp.where(allowed, dot_t(query, key_ref[head]), masked_score)
            top = jnp.max(scores, axis=1, keepdims=True)
            weights = jnp.exp(scores - top).astype(low)
            summed = dot(weights, value_ref[head])
            total = summed[:, half_lanes : half_lanes + 1]
            one, two, three = three_pieces(-(top + jnp.log(total)))
            extra = jnp.where(lane == 77, one, jnp.where(lane == 78, two, jnp.where(lane == 79, three, 0.0)))
            query_ref[head, at, :] = jnp.where(lane < 77, query.astype(wide), extra).astype(low)
            done.append(summed / total)
        for base in range(0, heads, 2):
            both = done[base]
            if base + 1 < heads:
                both = jnp.where(lane < half_lanes, both, pltpu.roll(done[base + 1], half_lanes, 1))
            out_ref[at, base // 2 * lanes : (base // 2 + 1) * lanes] = both.astype(low)


def attend(bias, near, far, w, cosine, sine, ids, heads):
    length = 2 * near.shape[0]
    padded = w.shape[1] // 3
    vmem = pl.BlockSpec(memory_space=pltpu.VMEM)
    whole = jax.ShapeDtypeStruct((heads, length, lanes), low)
    return pl.pallas_call(
        functools.partial(attend_kernel, heads),
        out_shape=(whole, whole, whole, jax.ShapeDtypeStruct((length, padded), low)),
        in_specs=[pl.BlockSpec(memory_space=pltpu.SMEM)] + [vmem] * 8,
        out_specs=(vmem, vmem, vmem, vmem),
        compiler_params=pltpu.CompilerParams(vmem_limit_bytes=48 * 2**20),
        cost_estimate=pl.CostEstimate(
            flops=2**20, bytes_accessed=2**10, transcendentals=0
        ),
    )(bias, near, far, w, cosine, sine, *ids)


def attend_grad_kernel(
    heads,
    query_ref,
    key_ref,
    value_ref,
    out_ref,
    grad_out_ref,
    cosine_ref,
    sine_ref,
    kinds_ref,
    docs_col_ref,
    docs_row_ref,
    near_ref,
    far_ref,
    w_ref,
    near_up_ref,
    far_up_ref,
    grad_w_ref,
    bias_ref,
    grad_query_ref,
    grad_key_ref,
    grad_value_ref,
    packed_ref,
):
    length = query_ref.shape[1]
    padded = packed_ref.shape[1] // 3
    half = length // 2
    block = min(length, 256)
    lane = lane_ids(block)
    grad_key_ref[...] = jnp.zeros_like(grad_key_ref)
    grad_value_ref[...] = jnp.zeros_like(grad_value_ref)

    @pl.loop(0, length // block)
    def _(i):
        at = pl.ds(pl.multiple_of(i * block, block), block)
        allowed = docs_col_ref[:, :1] == docs_row_ref[:, at]
        for head in range(heads):
            columns = slice(head // 2 * lanes, (head // 2 + 1) * lanes)
            grad_out = grad_out_ref[at, columns].astype(wide)
            product = grad_out * out_ref[at, columns].astype(wide)
            mine = (lane >= half_lanes) if head % 2 else (lane < half_lanes)
            row_dot = jnp.sum(jnp.where(mine, product, 0.0), axis=1, keepdims=True)
            one, two, three = three_pieces(-row_dot)
            if head % 2:
                grad_out = pltpu.roll(grad_out, half_lanes, 1)
            extra = jnp.where(lane == 64, one, jnp.where(lane == 65, two, jnp.where(lane == 66, three, 0.0)))
            grad_out = jnp.where(lane < half_lanes, grad_out, extra).astype(low)
            query, key = query_ref[head, at, :], key_ref[head]
            weights = jnp.exp(jnp.where(allowed, dot_t(key, query), masked_score))
            grad_scores = (weights * dot_t(value_ref[head], grad_out)).astype(low)
            grad_value_ref[head] += dot(weights.astype(low), grad_out)
            grad_key_ref[head] += dot(grad_scores, query)
            grad_query_ref[head, at, :] = t_dot(grad_scores, key)

    for start in range(0, length, block):
        at = slice(start, start + block)
        cosine, sine = cosine_ref[at, :], sine_ref[at, :]
        for base in range(0, heads, 2):

            def joined(ref):
                both = ref[base, at, :]
                if base + 1 < heads:
                    both = jnp.where(lane < half_lanes, both, pltpu.roll(ref[base + 1, at, :], half_lanes, 1))
                else:
                    both = jnp.where(lane < half_lanes, both, 0.0)
                return both

            columns = base // 2 * lanes
            query = joined(grad_query_ref) * 0.125
            key = joined(grad_key_ref)
            value = joined(grad_value_ref)
            query = query * cosine - swap_halves(query) * sine
            key = key * cosine - swap_halves(key) * sine
            for part, result in enumerate((query, key, value)):
                packed_ref[at, part * padded + columns : part * padded + columns + lanes] = result.astype(low)
    for start in range(0, half, block):
        here = slice(start, start + block)
        far_up_ref[here, :] = dot_t(packed_ref[half + start : half + start + block, :], w_ref[...]).astype(low)
        near_up_ref[here, :] = dot_t(packed_ref[here, :], w_ref[...]).astype(low)
    width = near_ref.shape[1]
    for start in range(0, width, 256):
        here = slice(start, start + 256)
        grads = t_dot(near_ref[:, here], packed_ref[:half, :]) + t_dot(far_ref[:, here], packed_ref[half:, :])
        grad_w_ref[here, :] = grads.astype(low)
    every = lane_ids(length)
    kinds = kinds_ref[:, :1]
    for head in range(heads):
        grads = grad_key_ref[head]
        same = jnp.sum(jnp.where(every == 72 + kinds, grads, 0.0))
        total = jnp.sum(jnp.where(every == 76, grads, 0.0))
        bias_ref[head, 0] = same
        bias_ref[head, 1] = total - same


def attend_grad(query, key, value, out, grad_out, cosine, sine, ids, near, far, w):
    heads, length, _ = query.shape
    half, width = near.shape
    vmem = pl.BlockSpec(memory_space=pltpu.VMEM)
    scratch = pltpu.VMEM((heads, length, lanes), wide)
    return pl.pallas_call(
        functools.partial(attend_grad_kernel, heads),
        out_shape=(
            jax.ShapeDtypeStruct((half, width), low),
            jax.ShapeDtypeStruct((half, width), low),
            jax.ShapeDtypeStruct(w.shape, low),
            jax.ShapeDtypeStruct((heads, 2), wide),
        ),
        in_specs=[vmem] * 13,
        out_specs=(vmem, vmem, vmem, pl.BlockSpec(memory_space=pltpu.SMEM)),
        scratch_shapes=[scratch] * 3 + [pltpu.VMEM((length, w.shape[1]), low)],
        compiler_params=pltpu.CompilerParams(vmem_limit_bytes=48 * 2**20),
        cost_estimate=pl.CostEstimate(flops=2**20, bytes_accessed=2**10, transcendentals=0),
    )(
        query, key, value, out, grad_out, cosine, sine, *ids, near, far, w
    )


def feed_kernel(units, tokens_ref, grads_ref, w_ref, hidden_ref, grad_units_ref, up_ref, down_ref):
    gate_up = dot(tokens_ref[...], w_ref[:, : 2 * units])
    count = grads_ref.shape[0] * grads_ref.shape[1]
    grad_hidden = dot(grads_ref[...].reshape(count, -1), w_ref[:, 2 * units :])
    gate_values, up_values = gate_up[:, :units], gate_up[:, units:]
    sigmoid_gate = jax.nn.sigmoid(gate_values)
    activated = gate_values * sigmoid_gate
    hidden_ref[...] = (activated * up_values).astype(low)
    slope = sigmoid_gate + activated * (1.0 - sigmoid_gate)
    grad_units_ref[:, :units] = (grad_hidden * up_values * slope).astype(low)
    grad_units_ref[:, units:] = (grad_hidden * activated).astype(low)
    up_ref[...] = dot_t(grad_units_ref[...], w_ref[:, : 2 * units]).astype(low)
    down_ref[...] = dot_t(hidden_ref[...], w_ref[:, 2 * units :]).astype(low)


def feed(tokens, grads, w):
    count, width = tokens.shape
    rows = count // grads.shape[0]
    units = w.shape[1] // 3
    step = min(count, 256)
    return pl.pallas_call(
        functools.partial(feed_kernel, units),
        grid=(count // step,),
        out_shape=(
            jax.ShapeDtypeStruct((count, units), low),
            jax.ShapeDtypeStruct((count, 2 * units), low),
            jax.ShapeDtypeStruct((count, width), low),
            jax.ShapeDtypeStruct((count, width), low),
        ),
        in_specs=[
            pl.BlockSpec((step, width), lambda i: (i, 0)),
            pl.BlockSpec((step // rows, rows, width), lambda i: (i, 0, 0)),
            pl.BlockSpec(memory_space=pltpu.VMEM),
        ],
        out_specs=(
            pl.BlockSpec((step, units), lambda i: (i, 0)),
            pl.BlockSpec((step, 2 * units), lambda i: (i, 0)),
            pl.BlockSpec((step, width), lambda i: (i, 0)),
            pl.BlockSpec((step, width), lambda i: (i, 0)),
        ),
        compiler_params=pltpu.CompilerParams(vmem_limit_bytes=32 * 2**20),
        cost_estimate=pl.CostEstimate(
            flops=10 * count * width * units, bytes_accessed=8 * 2**20, transcendentals=count * units
        ),
    )(tokens, grads, w)


def feed_grad_kernel(units, *refs):
    *parts, out_ref = refs
    results = [0.0, 0.0]
    for tokens_ref, grads_ref, hidden_ref, grad_units_ref in (parts[:4], parts[4:]):
        grads = grads_ref[...]
        grads = grads.reshape(grads.shape[0] * grads.shape[1], -1)
        results[0] += t_dot(tokens_ref[...], grad_units_ref[...])
        results[1] += t_dot(grads, hidden_ref[...])
    out_ref[:, : 2 * units] = results[0].astype(low)
    out_ref[:, 2 * units :] = results[1].astype(low)


def feed_grad(near, far):
    tokens, grads, hidden, _ = near
    count, width = tokens.shape
    rows = count // grads.shape[0]
    units = hidden.shape[1]
    step = min(width, 256)
    whole = pl.BlockSpec(memory_space=pltpu.VMEM)
    part = [
        pl.BlockSpec((count, step), lambda i: (0, i)),
        pl.BlockSpec((grads.shape[0], rows, step), lambda i: (0, 0, i)),
        whole,
        whole,
    ]
    return pl.pallas_call(
        functools.partial(feed_grad_kernel, units),
        grid=(width // step,),
        out_shape=jax.ShapeDtypeStruct((width, 3 * units), low),
        in_specs=part + part,
        out_specs=pl.BlockSpec((step, 3 * units), lambda i: (i, 0)),
        compiler_params=pltpu.CompilerParams(vmem_limit_bytes=32 * 2**20),
        cost_estimate=pl.CostEstimate(
            flops=12 * count * width * units, bytes_accessed=12 * 2**20, transcendentals=0
        ),
    )(*near, *far)


def rope_tables(stamps, dimension):
    halfway = dimension // 2
    frequency = jnp.exp(-math.log(10000.0) * jnp.arange(halfway, dtype=wide) / halfway)
    repeated = jnp.tile(frequency, lanes // halfway)
    angles = stamps.astype(wide)[:, None] * repeated[None, :]
    sign = jnp.where(jnp.arange(lanes) % dimension < halfway, -1.0, 1.0)
    return (jnp.cos(angles), jnp.sin(angles) * sign[None, :])


def shards(
    inputs,
    gain_attn,
    w_qkv,
    head_bias,
    w_out,
    gain_ffn,
    w_gate,
    w_up,
    w_down,
    time_ids,
    variate_ids,
    seq_ids,
    cotangent,
):
    at = Place()
    z_size, y_size = at.z_size, at.y_size
    tokens = inputs[0].astype(wide)
    rows, width = tokens.shape
    head_count = head_bias.shape[0]
    head_dim = width // head_count
    groups = at.seq_size
    heads = head_count // groups
    group_width = heads * head_dim
    padded = (heads + 1) // 2 * lanes
    share = width // (at.seq_size * at.head_size)
    group = 2 * at.z + at.c
    window = 2 * at.y + at.x
    device_id = at.seq * at.head_size + at.head

    inverse_one = lax.rsqrt(jnp.mean(tokens * tokens, axis=-1, keepdims=True) + epsilon)
    unit = tokens * inverse_one
    turned = called("tokens_turn", at.turn, unit.astype(low))

    depth, units = w_gate.shape[0], w_gate.shape[1] // 2
    turned, late_gate, late_up, late_down = tied(turned, w_gate, w_up, w_down)
    down_t = with_layout_constraint(late_down.T, Layout(major_to_minor=(0, 1)))
    firsts = jnp.concatenate([v[:, :units] for v in (late_gate, late_up, down_t)], axis=1)
    seconds = jnp.concatenate([v[:, units:] for v in (late_gate, late_up, down_t)], axis=1)
    mine = pick(at.x, firsts, seconds)
    other = called("ffn_x", at.along_x, pick(at.x, seconds, firsts))
    z_block = jnp.concatenate([pick(at.x, mine, other), pick(at.x, other, mine)], axis=0)

    gain_one = gain_attn.astype(wide)[:, None]
    scaled = (w_qkv.astype(wide) * gain_one).astype(low)

    def to_parts(columns):
        parts = columns.reshape(-1, groups, heads, 3, head_dim).transpose(0, 1, 3, 2, 4)
        parts = parts.reshape(-1, groups, 3, group_width)
        parts = jnp.pad(parts, ((0, 0), (0, 0), (0, 0), (0, padded - group_width)))
        return parts.reshape(-1, groups, 3 * padded)

    parts = to_parts(scaled).reshape(share, z_size, 2, 3 * padded)
    core_own = pick(at.c, parts[:, :, 0], parts[:, :, 1])
    core_sent = pick(at.c, parts[:, :, 1], parts[:, :, 0]).reshape(-1, 3 * padded)

    def with_extra(block, *values):
        extra = jnp.stack([jnp.pad(v.astype(low), (0, 3 * padded - v.shape[0])) for v in values])
        return jnp.concatenate([block, jnp.pad(extra, ((0, 16 - len(values)), (0, 0)))], axis=0)

    core_got = called("qkv_core", at.along_c, with_extra(core_sent, gain_ffn))
    both = jnp.stack([core_own, core_got[:-16].reshape(core_own.shape)])
    both, turned, w_out_early = tied(both, turned, w_out)
    gains = jnp.concatenate([gain_ffn, core_got[-16, :share]])
    sent = []
    for d in range(z_size):
        block = lax.dynamic_index_in_dim(both, jnp.bitwise_xor(at.z, d), axis=2, keepdims=False)
        sent.append(with_extra(block.reshape(-1, 3 * padded), gains))
    by_z = jnp.stack(called("qkv_z", at.scatter_z, sent))
    gains = by_z[:, -16, : 2 * share].reshape(-1)
    by_z = by_z[:, :-16].reshape(-1, 3 * padded)
    out_z = called("out_z", at.gather_steps, w_out_early, at.z_moves()).reshape(-1, width)
    near = called("tokens_z", at.gather_steps, turned, at.z_moves()).reshape(-1, width)
    near, z_block = tied(near, z_block)
    w_ffn = lax.all_gather(z_block, "seq", axis=0, tiled=True, axis_index_groups=at.columns_z())
    by_xy = called("qkv_xy", at.gather_steps, with_extra(by_z, gains), at.xy_moves())
    gains = by_xy[:, -16, : gains.shape[0]].reshape(y_size, 2, z_size, 2, share)
    gains = gains.transpose(2, 1, 0, 3, 4).reshape(-1, share)
    by_xy = by_xy[:, :-16]
    devices = jnp.arange(at.seq_size * at.head_size)
    from_device = (devices[None, :] == jnp.bitwise_xor(devices[:, None], device_id)).astype(low)
    gain_two = dot(from_device, gains).reshape(1, width)
    masks = [
        (2 * d + dx) * at.head_size + 2 * dy + e
        for dx, dy in at.pairs()
        for d in range(z_size)
        for e in range(2)
    ]
    w_heads = place(by_xy.reshape(-1, share, 3 * padded), device_id, masks).reshape(width, 3 * padded)

    time_ids, variate_ids, seq_ids, by_z = tied(time_ids, variate_ids, seq_ids, by_z)

    def of_window(ids):
        row = lax.dynamic_index_in_dim(ids, window, axis=0, keepdims=False).reshape(z_size, 2, rows)
        order = [
            lax.dynamic_slice(
                row, (jnp.bitwise_xor(at.z, d), jnp.bitwise_xor(at.c, e), 0), (1, 1, rows)
            ).reshape(rows)
            for e in range(2)
            for d in at.z_order()
        ]
        return jnp.concatenate(order)

    docs = of_window(seq_ids)
    docs_columns = jnp.broadcast_to(docs[:, None], (docs.shape[0], lanes))
    kinds = jnp.broadcast_to(of_window(variate_ids)[:, None], docs_columns.shape)
    cosine, sine = rope_tables(of_window(time_ids), head_dim)
    local_bias = lax.dynamic_slice_in_dim(head_bias, group * heads, heads, 0)
    difference = local_bias[:, 0] - local_bias[:, 1]
    difference_high = difference.astype(low).astype(wide)
    bias = jnp.stack([difference_high, difference - difference_high])

    grad_out = cotangent[0]
    xy_rows = jnp.concatenate([grad_out, out_z], axis=0)
    xy_rows = called("cotangent_x", at.gather_steps, xy_rows, at.xy_moves()[:1])

    near, w_heads, cosine, sine, kinds, docs, docs_columns = tied(
        near, w_heads, cosine, sine, kinds, docs, docs_columns
    )
    ids = (kinds, docs_columns, docs.reshape(1, -1))
    xy_rows = called("cotangent_y", at.gather_steps, xy_rows, at.xy_moves()[1:])
    xy_rows = xy_rows.reshape(2 * y_size, -1, width)
    far = called("tokens_core", at.along_c, near)
    query, key, value, attended = attend(bias, near, far, w_heads, cosine, sine, ids, heads)

    xy_rows, query = tied(xy_rows, query)
    xy_rows_far = called("cotangent_core", at.along_c, xy_rows)
    out_blocks = jnp.stack([xy_rows[:, rows:], xy_rows_far[:, rows:]]).reshape(-1, share, width)
    out_masks = [
        (dx * z_size + d) * at.head_size + 2 * dy + e
        for e in range(2)
        for dx, dy in at.pairs()
        for d in range(z_size)
    ]
    out_rows = place(out_blocks, at.head, out_masks).reshape(width, width)

    sent = attended[:, :group_width].reshape(2, z_size, rows, group_width)
    places = {d: i for i, d in enumerate(at.z_order())}
    received = called("attended_z", at.scatter_z, [sent[:, places[d]] for d in range(z_size)])
    received = [received[d] for d in at.z_order()]
    kept = jnp.concatenate([block[0] for block in received], axis=1)
    passed = jnp.concatenate([block[1] for block in received], axis=1)
    passed = called("attended_core", at.along_c, passed)
    passed, w_ffn = tied(passed, w_ffn)
    merged = called("attended_turn", at.turn, jnp.concatenate([kept, passed], axis=1))

    middle = tokens + dot(merged, out_rows)
    inverse_two = lax.rsqrt(jnp.mean(middle * middle, axis=-1, keepdims=True) + epsilon)
    unit_two = middle * inverse_two
    normed_two = (unit_two * gain_two).astype(low)
    normed_near = jnp.concatenate(called("normed_xy", at.gather_xy, normed_two), axis=0)
    normed_far = called("normed_core", at.along_c, normed_near)

    hidden_near, units_near, up_near, down_near = feed(normed_near, xy_rows, w_ffn)
    hidden_far, units_far, up_far, down_far = feed(normed_far, xy_rows_far, w_ffn)

    units_far, up_far = tied(units_far, up_far)
    grad_w_ffn = feed_grad(
        (normed_near, xy_rows, hidden_near, units_near),
        (normed_far, xy_rows_far, hidden_far, units_far),
    )
    up_far = called("up_core", at.along_c, up_far)
    up_far, grad_w_ffn = tied(up_far, grad_w_ffn)
    kept = [
        up_near[i * rows : (i + 1) * rows].astype(wide) + up_far[i * rows : (i + 1) * rows].astype(wide)
        for i in range(2 * y_size)
    ]
    received = called("up_xy", at.scatter_xy, kept[:1] + [block.astype(low) for block in kept[1:]])
    grad_two = functools.reduce(jnp.add, [block.astype(wide) for block in received])
    gain_part = jnp.sum(grad_two * unit_two, axis=0)
    upstream = grad_two * gain_two
    grad_w_ffn = lax.psum_scatter(
        grad_w_ffn, "seq", scatter_dimension=0, tiled=True, axis_index_groups=at.columns_z()
    )

    grad_middle = (
        grad_out.astype(wide)
        + inverse_two * upstream
        - unit_two * inverse_two * jnp.mean(upstream * unit_two, axis=-1, keepdims=True)
    )
    grad_branch = grad_middle.astype(low)
    grad_merged = dot_t(grad_branch, out_rows).astype(low)

    turned_back = called("merged_turn", at.turn, grad_merged)
    cut = width // 2
    kept, passed = turned_back[:, :cut], called("merged_core", at.along_c, turned_back[:, cut:])
    sent = []
    for d in range(z_size):
        columns = slice(places[d] * group_width, (places[d] + 1) * group_width)
        sent.append(jnp.stack([part[:, columns] for part in (kept, passed)]))
    received = called("merged_z", at.scatter_z, sent)
    received = jnp.stack([received[d] for d in at.z_order()], axis=1)
    grad_attended = received.reshape(2 * z_size * rows, group_width)
    if padded > group_width:
        grad_attended = jnp.pad(grad_attended, ((0, 0), (0, padded - group_width)))

    down_far, grad_branch = tied(down_far, grad_branch)
    down = down_near.astype(wide) + called("down_core", at.along_c, down_far).astype(wide)
    down = down.reshape(y_size, 2, rows, width)
    down = called("down_y", at.scatter_steps, down, at.xy_moves()[1:])

    merged, grad_branch, turned_back = tied(merged, grad_branch, turned_back)
    grad_out_rows = t_dot(merged, grad_branch).astype(low)
    grad_out_rows = fetch(grad_out_rows.reshape(-1, share, width), at.head, out_masks)
    grad_out_rows = grad_out_rows.reshape(2, 2 * y_size, z_size * share, width)
    grad_out_far = called("w_out_core", at.along_c, grad_out_rows[1])
    grad_out_rows = (grad_out_rows[0].astype(wide) + grad_out_far.astype(wide)).astype(low)

    grad_attended, down, grad_out_rows = tied(grad_attended, down, grad_out_rows)
    output = middle + called("down_x", at.scatter_steps, down, at.xy_moves()[:1])
    upstream_near, upstream_far, grad_heads, bias_grad = attend_grad(
        query, key, value, attended, grad_attended, cosine, sine, ids, near, far, w_heads
    )

    upstream_far, grad_w_ffn = tied(upstream_far, grad_w_ffn)
    upstream_far = called("input_core", at.along_c, upstream_far)
    upstream_near = upstream_near.astype(wide) + upstream_far.astype(wide)
    z_moves = at.z_moves()
    upstream_z = upstream_near.reshape(z_size, rows, width)
    cut = z_size // 2
    upstream_z = upstream_z[:cut] + called("input_z", z_moves[-1], upstream_z[cut:].astype(low)).astype(wide)

    grad_heads = grad_heads.reshape(z_size, 2, y_size, 2, share, 3 * padded)

    def halves(values):
        high = values.astype(low)
        return high, (values - high.astype(wide)).astype(low)

    def joined(block, row, count):
        return block[row, :count].astype(wide) + block[row + 1, :count].astype(wide)

    gain_part = gain_part.reshape(z_size, 2, y_size, 2, share)
    bias_count, gain_count = 2 * heads, 2 * z_size * share

    grad_out_rows = grad_out_rows.reshape(2 * y_size, z_size, share, 2, width // 2)
    grad_out_rows = grad_out_rows.transpose(0, 1, 3, 2, 4).reshape(2 * y_size, -1, width // 2)

    def rows_of(index, dx, dy):
        x, y = jnp.bitwise_xor(at.x, dx), jnp.bitwise_xor(at.y, dy)
        picked = lax.dynamic_slice(
            grad_heads, (0, x, y, 0, 0, 0), (z_size, 1, 1, 2, share, 3 * padded)
        )
        gain = lax.dynamic_slice(gain_part, (0, x, y, 0, 0), (z_size, 1, 1, 2, share)).reshape(-1)
        block = with_extra(picked.reshape(-1, 3 * padded), *halves(bias_grad.reshape(-1)), *halves(gain))
        return jnp.concatenate([block, jnp.pad(grad_out_rows[index], ((0, 16), (0, 0)))], axis=1)

    received = called("grad_qkv_xy", at.scatter_xy, [rows_of(i, *d) for i, d in enumerate(at.pairs())])
    summed = functools.reduce(jnp.add, [block.astype(wide) for block in received])
    summed, upstream_z = tied(summed, upstream_z)
    upstream_one = called("input_z", at.scatter_steps, upstream_z, z_moves[:-1])
    bias_sum = joined(summed[-16:], 0, bias_count)
    gain_sum = joined(summed[-16:], 2, gain_count).reshape(z_size, 2 * share)
    out_sum = summed[:-16, 3 * padded :].astype(low).reshape(z_size, 2 * share, width // 2)
    summed = summed[:-16, : 3 * padded].astype(low).reshape(z_size, 2 * share, 3 * padded)
    sent = []
    for d in range(z_size):
        block, gain = (
            lax.dynamic_index_in_dim(v, jnp.bitwise_xor(at.z, d), axis=0, keepdims=False)
            for v in (summed, gain_sum)
        )
        block = with_extra(block, *halves(bias_sum), *halves(gain))
        out_block = jnp.pad(out_sum[places[d]], ((0, 16), (0, 0)))
        sent.append(jnp.concatenate([block, out_block], axis=1))
    received = called("grad_qkv_z", at.scatter_z, sent)
    grad_w_out = functools.reduce(
        jnp.add, [block[:-16, 3 * padded :].astype(wide) for block in received]
    )
    grad_w_out = grad_w_out.reshape(2, share, width // 2).transpose(1, 0, 2).reshape(share, width)
    received = [block[:, : 3 * padded] for block in received]
    bias_z = jnp.concatenate([joined(block[-16:], 0, bias_count) for block in received])
    gain_sum = functools.reduce(jnp.add, [joined(block[-16:], 2, 2 * share) for block in received])
    received = jnp.stack([block[:-16] for block in received]).reshape(z_size, 2, share, 3 * padded)
    core_own = pick(at.c, received[:, 0], received[:, 1])
    core_sent = pick(at.c, received[:, 1], received[:, 0]).reshape(-1, 3 * padded)
    gain_own = pick(at.c, gain_sum[:share], gain_sum[share:])
    gain_sent = pick(at.c, gain_sum[share:], gain_sum[:share])
    core_sent, upstream_one = tied(core_sent, upstream_one)
    mine = pick(at.x, grad_w_ffn[:depth], grad_w_ffn[depth:]).astype(wide)
    other = pick(at.x, grad_w_ffn[depth:], grad_w_ffn[:depth])
    other = called("grad_ffn_x", at.along_x, other).astype(wide)
    upstream_one, other = tied(upstream_one.astype(low), other)
    upstream_one = called("input_turn", at.turn, upstream_one).astype(wide)
    grad_input = grad_middle + inverse_one * (
        upstream_one - unit * jnp.mean(upstream_one * unit, axis=-1, keepdims=True)
    )
    core_got = called(
        "grad_qkv_core", at.along_c, with_extra(core_sent, *halves(bias_z), *halves(gain_sent))
    )
    core_other = core_got[:-16].reshape(z_size, share, 3 * padded)
    grad_gain_ffn = gain_own + joined(core_got[-16:], 2, share)
    biases = jnp.stack([bias_z, joined(core_got[-16:], 0, z_size * bias_count)])
    biases = list(biases.reshape(2, z_size, heads, 2).transpose(1, 0, 2, 3).reshape(groups, heads, 2))
    full_bias = jnp.concatenate(xor_list(biases, group), axis=0)
    by_group = jnp.stack([core_own, core_other], axis=1).reshape(groups, share, 3 * padded)
    by_group = place(by_group, group, list(range(groups))).astype(wide).reshape(groups, share, 3, padded)
    by_group = by_group[..., :group_width].reshape(groups, share, 3, heads, head_dim)
    raw = by_group.transpose(1, 0, 3, 2, 4).reshape(share, 3 * width)
    grad_w_qkv = raw * gain_one
    grad_gain_attn = jnp.sum(raw * w_qkv.astype(wide), axis=1)
    first, second = pick(at.x, mine, other), pick(at.x, other, mine)
    grad_w_gate, grad_w_up, grad_w_down_t = (
        jnp.concatenate([first[:, i * units : (i + 1) * units], second[:, i * units : (i + 1) * units]], axis=1)
        for i in range(3)
    )
    return (
        output.astype(low).reshape(1, rows, width),
        grad_input.astype(low).reshape(1, rows, width),
        grad_gain_attn,
        grad_w_qkv,
        full_bias,
        grad_w_out,
        grad_gain_ffn,
        grad_w_gate,
        grad_w_up,
        grad_w_down_t.T,
    )


def solution(mesh):
    placed = (
        P("head", "seq", None),
        P(("seq", "head")),
        P(("seq", "head"), None),
        P(),
        P(("seq", "head"), None),
        P(("seq", "head")),
        P("seq", "head"),
        P("seq", "head"),
        P("head", "seq"),
        P(),
        P(),
        P(),
        P("head", "seq", None),
    )
    return jax.shard_map(
        shards,
        mesh=mesh,
        in_specs=placed,
        out_specs=(
            P("head", "seq", None),
            P("head", "seq", None),
            P(("seq", "head")),
            P(("seq", "head"), None),
            P(),
            P(("seq", "head"), None),
            P(("seq", "head")),
            P("seq", "head"),
            P("seq", "head"),
            P("head", "seq"),
        ),
        check_vma=False,
    )
```

```python
import functools
import math

import jax
import jax.numpy as jnp
from jax import lax
from jax.experimental import pallas as pl
from jax.experimental.layout import Layout, with_layout_constraint
from jax.experimental.pallas import tpu as pltpu
from jax.sharding import PartitionSpec as P


epsilon = 1e-05
masked_score = -1e30
low = jnp.bfloat16
wide = jnp.float32
lanes = 128
half_lanes = 64
attend_flops = 2**20
attend_grad_flops = 4 * 10**9
final_flops = 3 * 10**9


def dot(a, b):
    return jnp.dot(a, b, preferred_element_type=wide)


def dot_t(a, b):
    return lax.dot_general(a, b, (((1,), (1,)), ((), ())), preferred_element_type=wide)


def t_dot(a, b):
    return lax.dot_general(a, b, (((0,), (0,)), ((), ())), preferred_element_type=wide)


class Place:
    def __init__(self):
        self.seq_size = lax.axis_size("seq")
        self.head_size = lax.axis_size("head")
        self.z_size = self.seq_size // 2
        self.y_size = self.head_size // 2
        self.seq = lax.axis_index("seq")
        self.head = lax.axis_index("head")
        self.z, self.x = self.seq // 2, self.seq % 2
        self.y, self.c = self.head // 2, self.head % 2

    def along_z(self, value, step):
        return lax.ppermute(value, "seq", [(i, i ^ (2 * step)) for i in range(self.seq_size)])

    def along_x(self, value):
        return lax.ppermute(value, "seq", [(i, i ^ 1) for i in range(self.seq_size)])

    def along_c(self, value):
        return lax.ppermute(value, "head", [(i, i ^ 1) for i in range(self.head_size)])

    def along_xy(self, value, dx, dy):
        if dy == 0:
            return self.along_x(value)
        if dx == 0:
            return lax.ppermute(
                value, "head", [(i, i ^ (2 * dy)) for i in range(self.head_size)]
            )
        return lax.ppermute(
            value,
            ("seq", "head"),
            [
                (s * self.head_size + h, (s ^ dx) * self.head_size + (h ^ (2 * dy)))
                for s in range(self.seq_size)
                for h in range(self.head_size)
            ],
        )

    def turn(self, value):
        return lax.ppermute(
            value,
            ("seq", "head"),
            [
                (s * self.head_size + h, ((s & ~1) | (h & 1)) * self.head_size + ((h & ~1) | (s & 1)))
                for s in range(self.seq_size)
                for h in range(self.head_size)
            ],
        )

    def pairs(self):
        return [(dx, dy) for dy in range(self.y_size) for dx in range(2)]

    def gather_xy(self, value):
        return [value if d == (0, 0) else self.along_xy(value, *d) for d in self.pairs()]

    def scatter_xy(self, blocks):
        return [
            block if d == (0, 0) else self.along_xy(block, *d)
            for d, block in zip(self.pairs(), blocks)
        ]

    def columns_z(self):
        return [[x + 2 * z for z in range(self.z_size)] for x in range(2)]

    def gather_z(self, value):
        return [value if d == 0 else self.along_z(value, d) for d in range(self.z_size)]

    def scatter_z(self, blocks):
        return [block if d == 0 else self.along_z(block, d) for d, block in enumerate(blocks)]

    def gather_steps(self, value, moves):
        held = value[None]
        for move in moves:
            held = jnp.concatenate([held, move(held)], axis=0)
        return held

    def scatter_steps(self, addends, moves):
        for move in reversed(moves):
            cut = addends[0].shape[0] // 2
            received = move(total([value[cut:] for value in addends]).astype(low))
            addends = [value[:cut] for value in addends] + [received]
        return addends

    def xy_moves(self):
        steps = [1 << i for i in range(self.y_size.bit_length() - 1)]
        return [self.along_x] + [functools.partial(self.along_xy, dx=0, dy=step) for step in steps]

    def z_moves(self):
        steps = [1 << i for i in reversed(range(self.z_size.bit_length() - 1))]
        return [functools.partial(self.along_z, step=step) for step in steps]

    def z_order(self):
        order = [0]
        for step in [1 << i for i in reversed(range(self.z_size.bit_length() - 1))]:
            order = order + [step ^ d for d in order]
        return order


def called(name, move, *operands):
    with jax.named_scope(name):
        return move(*operands)


def total(addends):
    return functools.reduce(jnp.add, [value.astype(wide) for value in addends])


def tied(*values):
    return lax.optimization_barrier(values)


def pick(bit, zero, one):
    return jnp.where(bit == 0, zero, one)


def xor_list(blocks, me):
    step = 1
    while step < len(blocks):
        on = (me // step) % 2
        blocks = [pick(on, blocks[i], blocks[i ^ step]) for i in range(len(blocks))]
        step *= 2
    return blocks


def place_kernel(masks, me_ref, in_ref, out_ref):
    for i, mask in enumerate(masks):
        out_ref[jnp.bitwise_xor(me_ref[0], mask)] = in_ref[i]


def fetch_kernel(masks, me_ref, in_ref, out_ref):
    for i, mask in enumerate(masks):
        out_ref[i] = in_ref[jnp.bitwise_xor(me_ref[0], mask)]


def move_blocks(kernel, blocks, me, masks):
    return pl.pallas_call(
        functools.partial(kernel, masks),
        out_shape=jax.ShapeDtypeStruct(blocks.shape, blocks.dtype),
        in_specs=[pl.BlockSpec(memory_space=pltpu.SMEM), pl.BlockSpec(memory_space=pltpu.VMEM)],
        out_specs=pl.BlockSpec(memory_space=pltpu.VMEM),
        compiler_params=pltpu.CompilerParams(vmem_limit_bytes=32 * 2**20),
        cost_estimate=pl.CostEstimate(flops=0, bytes_accessed=4 * blocks.size, transcendentals=0),
    )(me.reshape(1).astype(jnp.int32), blocks)


def place(blocks, me, masks):
    return move_blocks(place_kernel, blocks, me, masks)


def fetch(blocks, me, masks):
    return move_blocks(fetch_kernel, blocks, me, masks)


def lane_ids(rows):
    return lax.broadcasted_iota(jnp.int32, (rows, lanes), 1)


def swap_halves(value):
    first = lane_ids(value.shape[0]) % half_lanes < half_lanes // 2
    return jnp.where(first, pltpu.roll(value, lanes - 32, 1), pltpu.roll(value, 32, 1))


def column_of(row):
    wide_row = jnp.broadcast_to(row.astype(wide), (8, row.shape[1]))
    return jnp.transpose(wide_row)[:, :1].astype(jnp.int32)


def three_pieces(value):
    one = value.astype(low).astype(wide)
    rest = value - one
    two = rest.astype(low).astype(wide)
    return one, two, (rest - two).astype(low).astype(wide)


def attend_kernel(
    heads,
    bias_ref,
    near_ref,
    far_ref,
    w_ref,
    cosine_ref,
    sine_ref,
    kinds_ref,
    docs_ref,
    query_ref,
    key_ref,
    value_ref,
    out_ref,
    docs_column_ref,
):
    rows = near_ref.shape[0]
    docs_column_ref[...] = column_of(docs_ref[...])
    length = 2 * rows
    step = min(rows, 256)
    padded = w_ref.shape[1] // 3
    for part, source in enumerate((near_ref, far_ref)):
        for start in range(0, rows, step):
            at = pl.ds(part * rows + start, step)
            packed = dot(source[start : start + step, :], w_ref[...])
            cosine, sine = cosine_ref[at, :], sine_ref[at, :]
            lane = lane_ids(step)
            kind = column_of(kinds_ref[:, at])
            own = (lane == 64 + kind).astype(wide)
            own_two = (lane == 68 + kind).astype(wide)
            extra_query = ((lane == 72 + kind) | (lane == 76)).astype(wide)
            extra_key = own + own_two + ((lane >= 77) & (lane < 80)).astype(wide)
            extra_value = ((lane >= 64) & (lane < 67)).astype(wide)
            for head in range(heads):
                base = head // 2 * lanes
                query = packed[:, base : base + lanes]
                key = packed[:, padded + base : padded + base + lanes]
                value = packed[:, 2 * padded + base : 2 * padded + base + lanes]
                query = (query * cosine + swap_halves(query) * sine).astype(low).astype(wide) * 0.125
                key = key * cosine + swap_halves(key) * sine
                if head % 2:
                    query, key, value = (pltpu.roll(v, half_lanes, 1) for v in (query, key, value))
                body = lane < half_lanes
                extra = extra_query + own * bias_ref[0, head] + own_two * bias_ref[1, head]
                query_ref[head, at, :] = jnp.where(body, query, extra).astype(low)
                key_ref[head, at, :] = jnp.where(body, key, extra_key).astype(low)
                value_ref[head, at, :] = jnp.where(body, value, extra_value).astype(low)
    block = min(length, 256)
    lane = lane_ids(block)

    @pl.loop(0, length // block)
    def _(i):
        at = pl.ds(pl.multiple_of(i * block, block), block)
        allowed = docs_column_ref[at, :] == docs_ref[...]
        done = []
        for head in range(heads):
            query = query_ref[head, at, :]
            scores = jnp.where(allowed, dot_t(query, key_ref[head]), masked_score)
            top = jnp.max(scores, axis=1, keepdims=True)
            weights = jnp.exp(scores - top).astype(low)
            summed = dot(weights, value_ref[head])
            total = summed[:, half_lanes : half_lanes + 1]
            one, two, three = three_pieces(-(top + jnp.log(total)))
            extra = jnp.where(lane == 77, one, jnp.where(lane == 78, two, jnp.where(lane == 79, three, 0.0)))
            query_ref[head, at, :] = jnp.where(lane < 77, query.astype(wide), extra).astype(low)
            done.append(summed / total)
        for base in range(0, heads, 2):
            both = done[base]
            if base + 1 < heads:
                both = jnp.where(lane < half_lanes, both, pltpu.roll(done[base + 1], half_lanes, 1))
            out_ref[at, base // 2 * lanes : (base // 2 + 1) * lanes] = both.astype(low)


def attend(bias, near, far, w, cosine, sine, ids, heads):
    length = 2 * near.shape[0]
    padded = w.shape[1] // 3
    vmem = pl.BlockSpec(memory_space=pltpu.VMEM)
    whole = jax.ShapeDtypeStruct((heads, length, lanes), low)
    return pl.pallas_call(
        functools.partial(attend_kernel, heads),
        out_shape=(whole, whole, whole, jax.ShapeDtypeStruct((length, padded), low)),
        in_specs=[pl.BlockSpec(memory_space=pltpu.SMEM)] + [vmem] * 7,
        out_specs=(vmem, vmem, vmem, vmem),
        scratch_shapes=[pltpu.VMEM((length, 1), jnp.int32)],
        compiler_params=pltpu.CompilerParams(vmem_limit_bytes=48 * 2**20),
        cost_estimate=pl.CostEstimate(
            flops=attend_flops, bytes_accessed=2**20, transcendentals=0
        ),
    )(bias, near, far, w, cosine, sine, *ids)


def attend_grad_kernel(
    heads,
    masks,
    *refs,
):
    if masks:
        place_ref, near_ref, far_ref, extra_ref, *refs = refs
        *refs, messages_ref, total_ref = refs
    attend_grad_body(heads, *refs)
    if not masks:
        return
    packed_ref, bias_ref = refs[12:14]
    half, width = near_ref.shape
    share = (messages_ref.shape[1] - 16) // len(masks[0])
    for start in range(0, width, 256):
        here = slice(start, start + 256)
        grads = t_dot(near_ref[:, here], packed_ref[:half, :]) + t_dot(far_ref[:, here], packed_ref[half:, :])
        total_ref[here, :] = grads.astype(low)
    columns = packed_ref.shape[1]
    row = lax.broadcasted_iota(jnp.int32, (16, columns), 0)
    lane = lax.broadcasted_iota(jnp.int32, (16, columns), 1)
    biases = jnp.zeros((16, columns), wide)
    for head in range(heads):
        for i in range(2):
            biases = jnp.where(lane == 2 * head + i, bias_ref[head, i], biases)
    high = biases.astype(low).astype(wide)
    biases = jnp.where(row == 0, high, jnp.where(row == 1, biases - high, 0.0))
    for i, part in enumerate(masks):
        for j, mask in enumerate(part):
            start = pl.multiple_of(jnp.bitwise_xor(place_ref[0], mask) * share, share)
            messages_ref[i, j * share : (j + 1) * share, :] = total_ref[pl.ds(start, share), :]
        messages_ref[i, len(part) * share :, :] = (extra_ref[i].astype(wide) + biases).astype(low)


def attend_grad_body(
    heads,
    query_ref,
    key_ref,
    value_ref,
    out_ref,
    grad_out_ref,
    cosine_ref,
    sine_ref,
    kinds_ref,
    docs_ref,
    w_ref,
    near_up_ref,
    far_up_ref,
    packed_ref,
    bias_ref,
    grad_query_ref,
    grad_key_ref,
    grad_value_ref,
    docs_column_ref,
):
    length = query_ref.shape[1]
    docs_column_ref[...] = column_of(docs_ref[...])
    padded = packed_ref.shape[1] // 3
    half = length // 2
    block = min(length, 256)
    lane = lane_ids(block)
    grad_key_ref[...] = jnp.zeros_like(grad_key_ref)
    grad_value_ref[...] = jnp.zeros_like(grad_value_ref)

    @pl.loop(0, length // block)
    def _(i):
        at = pl.ds(pl.multiple_of(i * block, block), block)
        allowed = docs_column_ref[...] == docs_ref[:, at]
        for head in range(heads):
            columns = slice(head // 2 * lanes, (head // 2 + 1) * lanes)
            grad_out = grad_out_ref[at, columns].astype(wide)
            product = grad_out * out_ref[at, columns].astype(wide)
            mine = (lane >= half_lanes) if head % 2 else (lane < half_lanes)
            row_dot = jnp.sum(jnp.where(mine, product, 0.0), axis=1, keepdims=True)
            one, two, three = three_pieces(-row_dot)
            if head % 2:
                grad_out = pltpu.roll(grad_out, half_lanes, 1)
            extra = jnp.where(lane == 64, one, jnp.where(lane == 65, two, jnp.where(lane == 66, three, 0.0)))
            grad_out = jnp.where(lane < half_lanes, grad_out, extra).astype(low)
            query, key = query_ref[head, at, :], key_ref[head]
            weights = jnp.exp(jnp.where(allowed, dot_t(key, query), masked_score))
            grad_scores = (weights * dot_t(value_ref[head], grad_out)).astype(low)
            grad_value_ref[head] += dot(weights.astype(low), grad_out)
            grad_key_ref[head] += dot(grad_scores, query)
            grad_query_ref[head, at, :] = t_dot(grad_scores, key)

    for start in range(0, length, block):
        at = slice(start, start + block)
        cosine, sine = cosine_ref[at, :], sine_ref[at, :]
        for base in range(0, heads, 2):

            def joined(ref):
                both = ref[base, at, :]
                if base + 1 < heads:
                    both = jnp.where(lane < half_lanes, both, pltpu.roll(ref[base + 1, at, :], half_lanes, 1))
                else:
                    both = jnp.where(lane < half_lanes, both, 0.0)
                return both

            columns = base // 2 * lanes
            query = joined(grad_query_ref) * 0.125
            key = joined(grad_key_ref)
            value = joined(grad_value_ref)
            query = query * cosine - swap_halves(query) * sine
            key = key * cosine - swap_halves(key) * sine
            for part, result in enumerate((query, key, value)):
                packed_ref[at, part * padded + columns : part * padded + columns + lanes] = result.astype(low)
    for start in range(0, half, block):
        here = slice(start, start + block)
        far_up_ref[here, :] = dot_t(packed_ref[half + start : half + start + block, :], w_ref[...]).astype(low)
        near_up_ref[here, :] = dot_t(packed_ref[here, :], w_ref[...]).astype(low)
    every = lane_ids(length)
    kinds = column_of(kinds_ref[...])
    for head in range(heads):
        grads = grad_key_ref[head]
        same = jnp.sum(jnp.where(every == 72 + kinds, grads, 0.0))
        total = jnp.sum(jnp.where(every == 76, grads, 0.0))
        bias_ref[head, 0] = same
        bias_ref[head, 1] = total - same


def attend_grad(query, key, value, out, grad_out, cosine, sine, ids, w, near, far, extra, place, masks):
    heads, length, _ = query.shape
    half, width = length // 2, w.shape[0]
    vmem, smem = pl.BlockSpec(memory_space=pltpu.VMEM), pl.BlockSpec(memory_space=pltpu.SMEM)
    columns = w.shape[1]
    out_shape = [
        jax.ShapeDtypeStruct((half, width), low),
        jax.ShapeDtypeStruct((half, width), low),
        jax.ShapeDtypeStruct((length, columns), low),
        jax.ShapeDtypeStruct((heads, 2), wide),
    ]
    scratch = [pltpu.VMEM((heads, length, lanes), wide)] * 3 + [pltpu.VMEM((length, 1), jnp.int32)]
    in_specs, out_specs = [vmem] * 10, [vmem] * 3 + [smem]
    operands = [query, key, value, out, grad_out, cosine, sine, *ids, w]
    kernel = functools.partial(attend_grad_kernel, heads, masks)
    if masks:
        share = width // sum(map(len, masks))
        in_specs = [smem, vmem, vmem, vmem] + in_specs
        operands = [place.reshape(1).astype(jnp.int32), near, far, extra] + operands
        out_shape.append(jax.ShapeDtypeStruct((len(masks), len(masks[0]) * share + 16, columns), low))
        out_specs = out_specs + [vmem]
        scratch = scratch + [pltpu.VMEM((width, columns), low)]

        def kernel(*refs):
            before, messages, after = refs[: len(in_specs) + 4], refs[len(in_specs) + 4], refs[len(in_specs) + 5 :]
            attend_grad_kernel(heads, masks, *before, *after[:-1], messages, after[-1])

    return pl.pallas_call(
        kernel,
        out_shape=out_shape,
        in_specs=in_specs,
        out_specs=out_specs,
        scratch_shapes=scratch,
        compiler_params=pltpu.CompilerParams(vmem_limit_bytes=48 * 2**20),
        cost_estimate=pl.CostEstimate(flops=attend_grad_flops, bytes_accessed=2**10, transcendentals=0),
    )(*operands)


def feed_kernel(units, tokens_ref, grads_ref, w_ref, hidden_ref, grad_units_ref, up_ref, down_ref):
    gate_up = dot(tokens_ref[...], w_ref[:, : 2 * units])
    count = grads_ref.shape[0] * grads_ref.shape[1]
    grad_hidden = dot(grads_ref[...].reshape(count, -1), w_ref[:, 2 * units :])
    gate_values, up_values = gate_up[:, :units], gate_up[:, units:]
    sigmoid_gate = jax.nn.sigmoid(gate_values)
    activated = gate_values * sigmoid_gate
    hidden_ref[...] = (activated * up_values).astype(low)
    slope = sigmoid_gate + activated * (1.0 - sigmoid_gate)
    grad_units_ref[:, :units] = (grad_hidden * up_values * slope).astype(low)
    grad_units_ref[:, units:] = (grad_hidden * activated).astype(low)
    up_ref[...] = dot_t(grad_units_ref[...], w_ref[:, : 2 * units]).astype(low)
    down_ref[...] = dot_t(hidden_ref[...], w_ref[:, 2 * units :]).astype(low)


def feed(tokens, grads, w):
    count, width = tokens.shape
    rows = count // grads.shape[0]
    units = w.shape[1] // 3
    step = min(count, 256)
    return pl.pallas_call(
        functools.partial(feed_kernel, units),
        grid=(count // step,),
        out_shape=(
            jax.ShapeDtypeStruct((count, units), low),
            jax.ShapeDtypeStruct((count, 2 * units), low),
            jax.ShapeDtypeStruct((count, width), low),
            jax.ShapeDtypeStruct((count, width), low),
        ),
        in_specs=[
            pl.BlockSpec((step, width), lambda i: (i, 0)),
            pl.BlockSpec((step // rows, rows, width), lambda i: (i, 0, 0)),
            pl.BlockSpec(memory_space=pltpu.VMEM),
        ],
        out_specs=(
            pl.BlockSpec((step, units), lambda i: (i, 0)),
            pl.BlockSpec((step, 2 * units), lambda i: (i, 0)),
            pl.BlockSpec((step, width), lambda i: (i, 0)),
            pl.BlockSpec((step, width), lambda i: (i, 0)),
        ),
        compiler_params=pltpu.CompilerParams(vmem_limit_bytes=58 * 2**20),
        cost_estimate=pl.CostEstimate(
            flops=10 * count * width * units, bytes_accessed=8 * 2**20, transcendentals=count * units
        ),
    )(tokens, grads, w)


def feed_grad_kernel(units, *refs):
    *parts, out_ref = refs
    results = [0.0, 0.0]
    for tokens_ref, grads_ref, hidden_ref, grad_units_ref in (parts[:4], parts[4:]):
        grads = grads_ref[...]
        grads = grads.reshape(grads.shape[0] * grads.shape[1], -1)
        results[0] += t_dot(tokens_ref[...], grad_units_ref[...])
        results[1] += t_dot(grads, hidden_ref[...])
    out_ref[:, : 2 * units] = results[0].astype(low)
    out_ref[:, 2 * units :] = results[1].astype(low)


def feed_grad(near, far):
    tokens, grads, hidden, _ = near
    count, width = tokens.shape
    rows = count // grads.shape[0]
    units = hidden.shape[1]
    step = min(width, 256)
    whole = pl.BlockSpec(memory_space=pltpu.VMEM)
    part = [
        pl.BlockSpec((count, step), lambda i: (0, i)),
        pl.BlockSpec((grads.shape[0], rows, step), lambda i: (0, 0, i)),
        whole,
        whole,
    ]
    return pl.pallas_call(
        functools.partial(feed_grad_kernel, units),
        grid=(width // step,),
        out_shape=jax.ShapeDtypeStruct((width, 3 * units), low),
        in_specs=part + part,
        out_specs=pl.BlockSpec((step, 3 * units), lambda i: (i, 0)),
        compiler_params=pltpu.CompilerParams(vmem_limit_bytes=58 * 2**20),
        cost_estimate=pl.CostEstimate(
            flops=12 * count * width * units, bytes_accessed=12 * 2**20, transcendentals=0
        ),
    )(*near, *far)


def finish_input_kernel(tokens_ref, upstream_ref, grads_ref, out_ref):
    tokens = tokens_ref[...].astype(wide)
    upstream = upstream_ref[...].astype(wide)
    inverse = lax.rsqrt(jnp.mean(tokens * tokens, axis=-1, keepdims=True) + epsilon)
    unit = tokens * inverse
    mean = jnp.mean(upstream * unit, axis=-1, keepdims=True)
    out_ref[...] = (grads_ref[...] + inverse * (upstream - unit * mean)).astype(low)


def finish_input(tokens, upstream, grads):
    return pl.pallas_call(
        finish_input_kernel,
        out_shape=jax.ShapeDtypeStruct(tokens.shape, low),
        cost_estimate=pl.CostEstimate(flops=final_flops, bytes_accessed=2**20, transcendentals=0),
    )(tokens, upstream, grads)


def finish_qkv_kernel(group_ref, grads_ref, w_ref, gain_ref, out_ref, gain_out_ref):
    share = w_ref.shape[0]
    low_half = lane_ids(share) < half_lanes
    gain = gain_ref[...].astype(wide)
    total = jnp.zeros((share, lanes), wide)
    for i in range(grads_ref.shape[0]):
        query, key, value = (grads_ref[i, :, j * lanes : (j + 1) * lanes].astype(wide) for j in range(3))
        key = pltpu.roll(key, half_lanes, 1)
        start = jnp.bitwise_xor(group_ref[0], i) * (3 * lanes)
        parts = (
            jnp.where(low_half, query, key),
            jnp.where(low_half, value, query),
            jnp.where(low_half, key, value),
        )
        for j, part in enumerate(parts):
            at = pl.ds(pl.multiple_of(start + j * lanes, lanes), lanes)
            total += part * w_ref[:, at].astype(wide)
            out_ref[:, at] = part * gain
    column = jnp.broadcast_to(jnp.sum(total, axis=1, keepdims=True), (share, lanes))
    gain_out_ref[...] = jnp.transpose(column)[:1, :]


def finish_qkv(group, grads, w, gain):
    vmem = pl.BlockSpec(memory_space=pltpu.VMEM)
    return pl.pallas_call(
        finish_qkv_kernel,
        out_shape=(
            jax.ShapeDtypeStruct(w.shape, wide),
            jax.ShapeDtypeStruct((1, w.shape[0]), wide),
        ),
        in_specs=[pl.BlockSpec(memory_space=pltpu.SMEM)] + [vmem] * 3,
        out_specs=(vmem, vmem),
        cost_estimate=pl.CostEstimate(flops=final_flops, bytes_accessed=2**20, transcendentals=0),
    )(group.reshape(1).astype(jnp.int32), grads, w, gain)


def finish_feed_kernel(x_ref, mine_ref, other_ref, gate_ref, up_ref, down_ref):
    units = mine_ref.shape[1] // 3
    for ref, x in ((mine_ref, x_ref[0]), (other_ref, 1 - x_ref[0])):
        at = pl.ds(pl.multiple_of(x * units, units), units)
        parts = [ref[:, j * units : (j + 1) * units].astype(wide) for j in range(3)]
        gate_ref[:, at], up_ref[:, at] = parts[:2]
        if down_ref.shape[0] == 2 * units:
            down_ref[at, :] = jnp.transpose(parts[2])
        else:
            down_ref[:, at] = parts[2]


def finish_feed(x, mine, other):
    vmem = pl.BlockSpec(memory_space=pltpu.VMEM)
    depth, units = mine.shape[0], mine.shape[1] // 3
    return pl.pallas_call(
        finish_feed_kernel,
        out_shape=(
            jax.ShapeDtypeStruct((depth, 2 * units), wide),
            jax.ShapeDtypeStruct((depth, 2 * units), wide),
            jax.ShapeDtypeStruct((2 * units, depth) if depth % lanes == 0 else (depth, 2 * units), wide),
        ),
        in_specs=[pl.BlockSpec(memory_space=pltpu.SMEM), vmem, vmem],
        out_specs=(vmem,) * 3,
        cost_estimate=pl.CostEstimate(flops=final_flops, bytes_accessed=2**20, transcendentals=0),
    )(x.reshape(1).astype(jnp.int32), mine, other)


def rope_tables(stamps, dimension):
    halfway = dimension // 2
    frequency = jnp.exp(-math.log(10000.0) * jnp.arange(halfway, dtype=wide) / halfway)
    repeated = jnp.tile(frequency, lanes // halfway)
    angles = stamps.astype(wide)[:, None] * repeated[None, :]
    sign = jnp.where(jnp.arange(lanes) % dimension < halfway, -1.0, 1.0)
    return (jnp.cos(angles), jnp.sin(angles) * sign[None, :])


def shards(
    inputs,
    gain_attn,
    w_qkv,
    head_bias,
    w_out,
    gain_ffn,
    w_gate,
    w_up,
    w_down,
    time_ids,
    variate_ids,
    seq_ids,
    cotangent,
):
    at = Place()
    z_size, y_size = at.z_size, at.y_size
    tokens = inputs[0].astype(wide)
    rows, width = tokens.shape
    head_count = head_bias.shape[0]
    head_dim = width // head_count
    groups = at.seq_size
    heads = head_count // groups
    group_width = heads * head_dim
    padded = (heads + 1) // 2 * lanes
    share = width // (at.seq_size * at.head_size)
    group = 2 * at.z + at.c
    window = 2 * at.y + at.x
    device_id = at.seq * at.head_size + at.head

    inverse_one = lax.rsqrt(jnp.mean(tokens * tokens, axis=-1, keepdims=True) + epsilon)
    unit = tokens * inverse_one
    turned = called("tokens_turn", at.turn, unit.astype(low))

    depth, units = w_gate.shape[0], w_gate.shape[1] // 2
    gain_one = gain_attn.astype(wide)[:, None]
    scaled = (w_qkv.astype(wide) * gain_one).astype(low)

    def to_parts(columns):
        parts = columns.reshape(-1, groups, heads, 3, head_dim).transpose(0, 1, 3, 2, 4)
        parts = parts.reshape(-1, groups, 3, group_width)
        parts = jnp.pad(parts, ((0, 0), (0, 0), (0, 0), (0, padded - group_width)))
        return parts.reshape(-1, groups, 3 * padded)

    parts = to_parts(scaled).reshape(share, z_size, 2, 3 * padded)
    core_own = pick(at.c, parts[:, :, 0], parts[:, :, 1])
    core_sent = pick(at.c, parts[:, :, 1], parts[:, :, 0]).reshape(-1, 3 * padded)

    def with_extra(block, *values):
        extra = jnp.stack([jnp.pad(v.astype(low), (0, 3 * padded - v.shape[0])) for v in values])
        return jnp.concatenate([block, jnp.pad(extra, ((0, 16 - len(values)), (0, 0)))], axis=0)

    core_got = called("qkv_core", at.along_c, with_extra(core_sent, gain_ffn))
    both = jnp.stack([core_own, core_got[:-16].reshape(core_own.shape)])
    out_z = called("out_z", at.gather_steps, w_out, at.z_moves()).reshape(-1, width)
    gains = jnp.concatenate([gain_ffn, core_got[-16, :share]])
    sent = []
    for d in range(z_size):
        block = lax.dynamic_index_in_dim(both, jnp.bitwise_xor(at.z, d), axis=2, keepdims=False)
        sent.append(with_extra(block.reshape(-1, 3 * padded), gains))
    by_z = jnp.stack(called("qkv_z", at.scatter_z, sent))
    gains = by_z[:, -16, : 2 * share].reshape(-1)
    by_z = by_z[:, :-16].reshape(-1, 3 * padded)
    turned, by_z, out_z = tied(turned, by_z, out_z)
    near = called("tokens_z", at.gather_steps, turned, at.z_moves()).reshape(-1, width)
    by_xy = jnp.stack(called("qkv_xy", at.gather_xy, with_extra(by_z, gains)))
    gains = by_xy[:, -16, : gains.shape[0]].reshape(y_size, 2, z_size, 2, share)
    gains = gains.transpose(2, 1, 0, 3, 4).reshape(-1, share)
    by_xy = by_xy[:, :-16]
    devices = jnp.arange(at.seq_size * at.head_size)
    from_device = (devices[None, :] == jnp.bitwise_xor(devices[:, None], device_id)).astype(low)
    gain_two = dot(from_device, gains).reshape(1, width)
    masks = [
        (2 * d + dx) * at.head_size + 2 * dy + e
        for dx, dy in at.pairs()
        for d in range(z_size)
        for e in range(2)
    ]
    w_heads = place(by_xy.reshape(-1, share, 3 * padded), device_id, masks).reshape(width, 3 * padded)

    w_heads, late_gate, late_up, late_down = tied(w_heads, w_gate, w_up, w_down)
    units = w_gate.shape[1] // 2
    down_t = with_layout_constraint(late_down.T, Layout(major_to_minor=(0, 1)))
    firsts = jnp.concatenate([v[:, :units] for v in (late_gate, late_up, down_t)], axis=1)
    seconds = jnp.concatenate([v[:, units:] for v in (late_gate, late_up, down_t)], axis=1)
    mine = pick(at.x, firsts, seconds)
    other = called("ffn_x", at.along_x, pick(at.x, seconds, firsts))
    z_block = jnp.concatenate([pick(at.x, mine, other), pick(at.x, other, mine)], axis=0)

    grad_out = cotangent[0]
    xy_rows = jnp.concatenate([grad_out, out_z], axis=0)
    xy_rows = called("cotangent_x", at.gather_steps, xy_rows, at.xy_moves()[:1])

    near, z_block, w_heads, xy_rows = tied(near, z_block, w_heads, xy_rows)
    w_ffn = lax.all_gather(z_block, "seq", axis=0, tiled=True, axis_index_groups=at.columns_z())

    time_ids, variate_ids, seq_ids, by_z = tied(time_ids, variate_ids, seq_ids, by_z)

    def of_window(ids):
        row = lax.dynamic_index_in_dim(ids, window, axis=0, keepdims=False).reshape(z_size, 2, rows)
        order = [
            lax.dynamic_slice(
                row, (jnp.bitwise_xor(at.z, d), jnp.bitwise_xor(at.c, e), 0), (1, 1, rows)
            ).reshape(rows)
            for e in range(2)
            for d in at.z_order()
        ]
        return jnp.concatenate(order)

    ids = (of_window(variate_ids).reshape(1, -1), of_window(seq_ids).reshape(1, -1))
    cosine, sine = rope_tables(of_window(time_ids), head_dim)
    local_bias = lax.dynamic_slice_in_dim(head_bias, group * heads, heads, 0)
    difference = local_bias[:, 0] - local_bias[:, 1]
    difference_high = difference.astype(low).astype(wide)
    bias = jnp.stack([difference_high, difference - difference_high])

    near, w_heads, cosine, sine, ids = tied(near, w_heads, cosine, sine, ids)
    far = called("tokens_core", at.along_c, near)
    query, key, value, attended = attend(bias, near, far, w_heads, cosine, sine, ids, heads)

    held = xy_rows[None]
    for move in at.xy_moves()[1:]:
        received = called("cotangent_y", move, held)
        received, query = tied(received, query)
        held = jnp.concatenate([held, received], axis=0)
    xy_rows = held.reshape(2 * y_size, -1, width)
    xy_rows_far = called("cotangent_core", at.along_c, xy_rows)
    out_blocks = jnp.stack([xy_rows[:, rows:], xy_rows_far[:, rows:]]).reshape(-1, share, width)
    out_masks = [
        (dx * z_size + d) * at.head_size + 2 * dy + e
        for e in range(2)
        for dx, dy in at.pairs()
        for d in range(z_size)
    ]
    out_rows = place(out_blocks, at.head, out_masks).reshape(width, width)

    sent = attended[:, :group_width].reshape(2, z_size, rows, group_width)
    places = {d: i for i, d in enumerate(at.z_order())}
    received = called("attended_z", at.scatter_z, [sent[:, places[d]] for d in range(z_size)])
    received = [received[d] for d in at.z_order()]
    kept = jnp.concatenate([block[0] for block in received], axis=1)
    passed = jnp.concatenate([block[1] for block in received], axis=1)
    passed = called("attended_core", at.along_c, passed)
    merged = called("attended_turn", at.turn, jnp.concatenate([kept, passed], axis=1))

    middle = tokens + dot(merged, out_rows)
    inverse_two = lax.rsqrt(jnp.mean(middle * middle, axis=-1, keepdims=True) + epsilon)
    unit_two = middle * inverse_two
    normed_two = (unit_two * gain_two).astype(low)
    normed_near = jnp.concatenate(called("normed_xy", at.gather_xy, normed_two), axis=0)
    normed_far = called("normed_core", at.along_c, normed_near)

    hidden_far, units_far, up_far, down_far = feed(normed_far, xy_rows_far, w_ffn)
    hidden_near, units_near, up_near, down_near = feed(normed_near, xy_rows, w_ffn)

    grad_w_ffn = feed_grad(
        (normed_near, xy_rows, hidden_near, units_near),
        (normed_far, xy_rows_far, hidden_far, units_far),
    )
    blocks = (2 * y_size, rows, width)
    up = up_near.reshape(blocks), called("up_core", at.along_c, up_far).reshape(blocks)
    received = called(
        "up_xy", at.scatter_xy, [total([part[i] for part in up]).astype(low) for i in range(2 * y_size)]
    )
    down = [down_near.reshape(blocks), called("down_core", at.along_c, down_far).reshape(blocks)]
    received[0], down[1] = tied(received[0], down[1])
    grad_two = total(received)
    gain_part = jnp.sum(grad_two * unit_two, axis=0)
    upstream = grad_two * gain_two
    grad_w_ffn = lax.psum_scatter(
        grad_w_ffn, "seq", scatter_dimension=0, tiled=True, axis_index_groups=at.columns_z()
    )

    grad_middle = (
        grad_out.astype(wide)
        + inverse_two * upstream
        - unit_two * inverse_two * jnp.mean(upstream * unit_two, axis=-1, keepdims=True)
    )
    grad_branch = grad_middle.astype(low)
    grad_merged = dot_t(grad_branch, out_rows).astype(low)

    turned_back = called("merged_turn", at.turn, grad_merged)
    cut = width // 2
    kept, passed = turned_back[:, :cut], called("merged_core", at.along_c, turned_back[:, cut:])
    sent = []
    for d in range(z_size):
        columns = slice(places[d] * group_width, (places[d] + 1) * group_width)
        sent.append(jnp.stack([part[:, columns] for part in (kept, passed)]))
    received = called("merged_z", at.scatter_z, sent)
    received = jnp.stack([received[d] for d in at.z_order()], axis=1)
    grad_attended = received.reshape(2 * z_size * rows, group_width)
    if padded > group_width:
        grad_attended = jnp.pad(grad_attended, ((0, 0), (0, padded - group_width)))

    moves = at.xy_moves()
    down[1], grad_branch = tied(down[1], grad_branch)
    down = called("down_y", at.scatter_steps, [part.reshape(y_size, 2, rows, width) for part in down], moves[1:])

    merged, grad_branch, turned_back = tied(merged, grad_branch, turned_back)
    grad_out_rows = t_dot(merged, grad_branch).astype(low)
    grad_out_rows = fetch(grad_out_rows.reshape(-1, share, width), at.head, out_masks)
    grad_out_rows = grad_out_rows.reshape(2, y_size, 2, z_size * share, width)
    out_parts = [grad_out_rows[0], called("w_out_core", at.along_c, grad_out_rows[1])]
    y_cut = y_size // 2
    out_sent = total([part[y_cut:] for part in out_parts]).astype(low)
    grad_attended, out_sent, down[-1] = tied(grad_attended, out_sent, down[-1])
    out_parts = [part[:y_cut] for part in out_parts] + [called("w_out_y", moves[-1], out_sent)]
    out_parts = called("w_out_y", at.scatter_steps, out_parts, moves[1:-1])

    def halves(values):
        high = values.astype(low)
        return high, (values - high.astype(wide)).astype(low)

    gain_part = gain_part.reshape(z_size, 2, y_size, 2, share)
    bias_count, gain_count = 2 * heads, 2 * z_size * share
    extra, device_masks = [], []
    for dx, dy in at.pairs():
        x, y = jnp.bitwise_xor(at.x, dx), jnp.bitwise_xor(at.y, dy)
        gain = lax.dynamic_slice(gain_part, (0, x, y, 0, 0), (z_size, 1, 1, 2, share)).reshape(-1)
        none = jnp.zeros((0, 3 * padded), low)
        extra.append(with_extra(none, *(jnp.zeros_like(v) for v in halves(gain)), *halves(gain)))
        device_masks.append([
            (2 * d + dx) * at.head_size + 2 * dy + e for d in range(z_size) for e in range(2)
        ])
    extra = jnp.stack(extra)
    place_xy = at.x * at.head_size + 2 * at.y
    in_kernel = share % 16 == 0
    upstream_near, upstream_far, grad_packed, bias_grad, *messages = attend_grad(
        query, key, value, attended, grad_attended, cosine, sine, ids, w_heads,
        near, far, extra, place_xy, device_masks if in_kernel else None,
    )
    half = near.shape[0]
    if in_kernel:
        messages = [messages[0][i] for i in range(2 * y_size)]
    else:
        grad_heads = t_dot(near, grad_packed[:half]) + t_dot(far, grad_packed[half:])
        grad_heads = grad_heads.astype(low).reshape(-1, share, 3 * padded)
        none = jnp.zeros((0, 3 * padded), low)
        biases = with_extra(none, *halves(bias_grad.reshape(-1)))
        messages = [
            jnp.concatenate([
                lax.dynamic_index_in_dim(grad_heads, jnp.bitwise_xor(place_xy, mask), 0, False)
                for mask in masks
            ] + [extra[i] + biases])
            for i, masks in enumerate(device_masks)
        ]

    upstream_far = called("input_core", at.along_c, upstream_far)
    z_moves = at.z_moves()
    blocks = (z_size, rows, width)
    upstream_z = [upstream_near.reshape(blocks), upstream_far.reshape(blocks)]
    upstream_z = called("input_z", at.scatter_steps, upstream_z, z_moves[-1:])

    def joined(block, row, count):
        return block[row, :count].astype(wide) + block[row + 1, :count].astype(wide)

    received = called("grad_qkv_xy", at.scatter_xy, messages)
    summed = functools.reduce(jnp.add, [block.astype(wide) for block in received])
    depth = grad_w_ffn.shape[0] // 2
    mine = pick(at.x, grad_w_ffn[:depth], grad_w_ffn[depth:])
    other = called("grad_ffn_x", at.along_x, pick(at.x, grad_w_ffn[depth:], grad_w_ffn[:depth]))
    summed, upstream_z[-1], other, down[-1], out_parts[-1] = tied(
        summed, upstream_z[-1], other, down[-1], out_parts[-1]
    )
    upstream_one = total(called("input_z", at.scatter_steps, upstream_z, z_moves[:-1]))[0]
    down = [part.reshape(2, rows, width) for part in down]
    output = middle + total(called("down_x", at.scatter_steps, down, moves[:1]))[0]
    out_parts = called("w_out_x", at.scatter_steps, [part.reshape(2, -1, width) for part in out_parts], moves[:1])
    out_parts = [part.reshape(z_size, share, width) for part in out_parts]
    grad_w_out = total(called("w_out_z", at.scatter_steps, out_parts, z_moves))[0]
    bias_sum = joined(summed[-16:], 0, bias_count)
    gain_sum = joined(summed[-16:], 2, gain_count).reshape(z_size, 2 * share)
    summed = summed[:-16].astype(low).reshape(z_size, 2 * share, 3 * padded)
    sent = []
    for d in range(z_size):
        block, gain = (
            lax.dynamic_index_in_dim(v, jnp.bitwise_xor(at.z, d), axis=0, keepdims=False)
            for v in (summed, gain_sum)
        )
        sent.append(with_extra(block, *halves(bias_sum), *halves(gain)))
    received = called("grad_qkv_z", at.scatter_z, sent)
    bias_z = jnp.concatenate([joined(block[-16:], 0, bias_count) for block in received])
    gain_sum = functools.reduce(jnp.add, [joined(block[-16:], 2, 2 * share) for block in received])
    received = jnp.stack([block[:-16] for block in received]).reshape(z_size, 2, share, 3 * padded)
    core_own = pick(at.c, received[:, 0], received[:, 1])
    core_sent = pick(at.c, received[:, 1], received[:, 0]).reshape(-1, 3 * padded)
    gain_own = pick(at.c, gain_sum[:share], gain_sum[share:])
    gain_sent = pick(at.c, gain_sum[share:], gain_sum[:share])
    core_sent, upstream_one = tied(core_sent, upstream_one)
    grad_w_gate, grad_w_up, grad_w_down = finish_feed(at.x, mine, other)
    if grad_w_down.shape != w_down.shape:
        grad_w_down = grad_w_down.T
    upstream_one = called("input_turn", at.turn, upstream_one.astype(low))
    grad_input = finish_input(inputs[0], upstream_one, grad_middle)
    core_got = called(
        "grad_qkv_core", at.along_c, with_extra(core_sent, *halves(bias_z), *halves(gain_sent))
    )
    core_other = core_got[:-16].reshape(z_size, share, 3 * padded)
    grad_gain_ffn = gain_own + joined(core_got[-16:], 2, share)
    biases = jnp.stack([bias_z, joined(core_got[-16:], 0, z_size * bias_count)])
    biases = list(biases.reshape(2, z_size, heads, 2).transpose(1, 0, 2, 3).reshape(groups, heads, 2))
    full_bias = jnp.concatenate(xor_list(biases, group), axis=0)
    by_group = jnp.stack([core_own, core_other], axis=1).reshape(groups, share, 3 * padded)
    if heads == 2 and head_dim == half_lanes:
        grad_w_qkv, grad_gain_attn = finish_qkv(group, by_group, w_qkv, gain_attn[:, None])
        grad_gain_attn = grad_gain_attn[0]
    else:
        by_group = place(by_group, group, list(range(groups))).astype(wide).reshape(groups, share, 3, padded)
        by_group = by_group[..., :group_width].reshape(groups, share, 3, heads, head_dim)
        raw = by_group.transpose(1, 0, 3, 2, 4).reshape(share, 3 * width)
        grad_w_qkv = raw * gain_one
        grad_gain_attn = jnp.sum(raw * w_qkv.astype(wide), axis=1)

    return (
        output.astype(low).reshape(1, rows, width),
        grad_input.reshape(1, rows, width),
        grad_gain_attn,
        grad_w_qkv,
        full_bias,
        grad_w_out,
        grad_gain_ffn,
        grad_w_gate,
        grad_w_up,
        grad_w_down,
    )


def solution(mesh):
    placed = (
        P("head", "seq", None),
        P(("seq", "head")),
        P(("seq", "head"), None),
        P(),
        P(("seq", "head"), None),
        P(("seq", "head")),
        P("seq", "head"),
        P("seq", "head"),
        P("head", "seq"),
        P(),
        P(),
        P(),
        P("head", "seq", None),
    )
    return jax.shard_map(
        shards,
        mesh=mesh,
        in_specs=placed,
        out_specs=(
            P("head", "seq", None),
            P("head", "seq", None),
            P(("seq", "head")),
            P(("seq", "head"), None),
            P(),
            P(("seq", "head"), None),
            P(("seq", "head")),
            P("seq", "head"),
            P("seq", "head"),
            P("head", "seq"),
        ),
        check_vma=False,
    )
```

```python
import functools
import math

import jax
import jax.numpy as jnp
from jax import lax
from jax.experimental import pallas as pl
from jax.experimental.layout import Layout, with_layout_constraint
from jax.experimental.pallas import tpu as pltpu
from jax.sharding import PartitionSpec as P


epsilon = 1e-05
masked_score = -1e30
low = jnp.bfloat16
wide = jnp.float32
lanes = 128
half_lanes = 64


def dot(a, b):
    return jnp.dot(a, b, preferred_element_type=wide)


def dot_t(a, b):
    return lax.dot_general(a, b, (((1,), (1,)), ((), ())), preferred_element_type=wide)


def t_dot(a, b):
    return lax.dot_general(a, b, (((0,), (0,)), ((), ())), preferred_element_type=wide)


class Place:
    def __init__(self):
        self.seq_size = lax.axis_size("seq")
        self.head_size = lax.axis_size("head")
        self.z_size = self.seq_size // 2
        self.y_size = self.head_size // 2
        self.seq = lax.axis_index("seq")
        self.head = lax.axis_index("head")
        self.z, self.x = self.seq // 2, self.seq % 2
        self.y, self.c = self.head // 2, self.head % 2

    def along_z(self, value, step):
        return lax.ppermute(value, "seq", [(i, i ^ (2 * step)) for i in range(self.seq_size)])

    def along_x(self, value):
        return lax.ppermute(value, "seq", [(i, i ^ 1) for i in range(self.seq_size)])

    def along_c(self, value):
        return lax.ppermute(value, "head", [(i, i ^ 1) for i in range(self.head_size)])

    def along_xy(self, value, dx, dy):
        if dy == 0:
            return self.along_x(value)
        if dx == 0:
            return lax.ppermute(
                value, "head", [(i, i ^ (2 * dy)) for i in range(self.head_size)]
            )
        return lax.ppermute(
            value,
            ("seq", "head"),
            [
                (s * self.head_size + h, (s ^ dx) * self.head_size + (h ^ (2 * dy)))
                for s in range(self.seq_size)
                for h in range(self.head_size)
            ],
        )

    def turn(self, value):
        return lax.ppermute(
            value,
            ("seq", "head"),
            [
                (s * self.head_size + h, ((s & ~1) | (h & 1)) * self.head_size + ((h & ~1) | (s & 1)))
                for s in range(self.seq_size)
                for h in range(self.head_size)
            ],
        )

    def pairs(self):
        return [(dx, dy) for dy in range(self.y_size) for dx in range(2)]

    def gather_xy(self, value):
        return [value if d == (0, 0) else self.along_xy(value, *d) for d in self.pairs()]

    def scatter_xy(self, blocks):
        return [
            block if d == (0, 0) else self.along_xy(block, *d)
            for d, block in zip(self.pairs(), blocks)
        ]

    def columns_z(self):
        return [[x + 2 * z for z in range(self.z_size)] for x in range(2)]

    def gather_z(self, value):
        return [value if d == 0 else self.along_z(value, d) for d in range(self.z_size)]

    def scatter_z(self, blocks):
        return [block if d == 0 else self.along_z(block, d) for d, block in enumerate(blocks)]

    def gather_steps(self, value, moves):
        held = value[None]
        for move in moves:
            held = jnp.concatenate([held, move(held)], axis=0)
        return held

    def scatter_steps(self, addends, moves):
        for move in reversed(moves):
            cut = addends[0].shape[0] // 2
            received = move(total([value[cut:] for value in addends]).astype(low))
            if len(addends) > 2:
                addends = [total([value[:cut] for value in addends])]
            else:
                addends = [value[:cut] for value in addends]
            addends = addends + [received]
        return addends

    def xy_moves(self):
        steps = [1 << i for i in range(self.y_size.bit_length() - 1)]
        return [self.along_x] + [functools.partial(self.along_xy, dx=0, dy=step) for step in steps]

    def z_moves(self):
        steps = [1 << i for i in reversed(range(self.z_size.bit_length() - 1))]
        return [functools.partial(self.along_z, step=step) for step in steps]

    def z_order(self):
        order = [0]
        for step in [1 << i for i in reversed(range(self.z_size.bit_length() - 1))]:
            order = order + [step ^ d for d in order]
        return order


def called(name, move, *operands):
    with jax.named_scope(name):
        return move(*operands)


def total(addends):
    return functools.reduce(jnp.add, [value.astype(wide) for value in addends])


def after(value, *others):
    return lax.optimization_barrier((value, others))[0]


def tied(*values):
    return lax.optimization_barrier(values)


def pick(bit, zero, one):
    return jnp.where(bit == 0, zero, one)


def xor_list(blocks, me):
    step = 1
    while step < len(blocks):
        on = (me // step) % 2
        blocks = [pick(on, blocks[i], blocks[i ^ step]) for i in range(len(blocks))]
        step *= 2
    return blocks


def place_kernel(masks, me_ref, in_ref, out_ref):
    for i, mask in enumerate(masks):
        out_ref[jnp.bitwise_xor(me_ref[0], mask)] = in_ref[i]


def fetch_kernel(masks, me_ref, in_ref, out_ref):
    for i, mask in enumerate(masks):
        out_ref[i] = in_ref[jnp.bitwise_xor(me_ref[0], mask)]


def move_blocks(kernel, blocks, me, masks):
    return pl.pallas_call(
        functools.partial(kernel, masks),
        out_shape=jax.ShapeDtypeStruct(blocks.shape, blocks.dtype),
        in_specs=[pl.BlockSpec(memory_space=pltpu.SMEM), pl.BlockSpec(memory_space=pltpu.VMEM)],
        out_specs=pl.BlockSpec(memory_space=pltpu.VMEM),
        compiler_params=pltpu.CompilerParams(vmem_limit_bytes=32 * 2**20),
        cost_estimate=pl.CostEstimate(flops=0, bytes_accessed=4 * blocks.size, transcendentals=0),
    )(me.reshape(1).astype(jnp.int32), blocks)


def place(blocks, me, masks):
    return move_blocks(place_kernel, blocks, me, masks)


def fetch(blocks, me, masks):
    return move_blocks(fetch_kernel, blocks, me, masks)


def join_kernel(first_ref, second_ref, out_ref):
    count = first_ref.shape[0]
    out_ref[:count] = first_ref[...]
    out_ref[count:] = second_ref[...]


def join(first, second):
    return pl.pallas_call(
        join_kernel,
        out_shape=jax.ShapeDtypeStruct((2 * first.shape[0],) + first.shape[1:], first.dtype),
        cost_estimate=pl.CostEstimate(flops=1 << 20, bytes_accessed=2**10, transcendentals=0),
    )(first, second)


def lane_ids(rows):
    return lax.broadcasted_iota(jnp.int32, (rows, lanes), 1)


def swap_halves(value):
    first = lane_ids(value.shape[0]) % half_lanes < half_lanes // 2
    return jnp.where(first, pltpu.roll(value, lanes - 32, 1), pltpu.roll(value, 32, 1))


def column_of(row):
    wide_row = jnp.broadcast_to(row.astype(wide), (8, row.shape[1]))
    return jnp.transpose(wide_row)[:, :1].astype(jnp.int32)


def three_pieces(value):
    one = value.astype(low).astype(wide)
    rest = value - one
    two = rest.astype(low).astype(wide)
    return one, two, (rest - two).astype(low).astype(wide)


def attend_kernel(
    heads,
    bias_ref,
    near_ref,
    far_ref,
    w_ref,
    cosine_ref,
    sine_ref,
    kinds_ref,
    docs_ref,
    query_ref,
    key_ref,
    value_ref,
    out_ref,
    docs_column_ref,
):
    rows = near_ref.shape[0]
    docs_column_ref[...] = column_of(docs_ref[...])
    length = 2 * rows
    step = min(rows, 256)
    padded = w_ref.shape[1] // 3
    for part, source in enumerate((near_ref, far_ref)):
        for start in range(0, rows, step):
            at = pl.ds(part * rows + start, step)
            packed = dot(source[start : start + step, :], w_ref[...])
            cosine, sine = cosine_ref[at, :], sine_ref[at, :]
            lane = lane_ids(step)
            kind = column_of(kinds_ref[:, at])
            own = (lane == 64 + kind).astype(wide)
            own_two = (lane == 68 + kind).astype(wide)
            extra_query = ((lane == 72 + kind) | (lane == 76)).astype(wide)
            extra_key = own + own_two + ((lane >= 77) & (lane < 80)).astype(wide)
            extra_value = ((lane >= 64) & (lane < 67)).astype(wide)
            for head in range(heads):
                base = head // 2 * lanes
                query = packed[:, base : base + lanes]
                key = packed[:, padded + base : padded + base + lanes]
                value = packed[:, 2 * padded + base : 2 * padded + base + lanes]
                query = (query * cosine + swap_halves(query) * sine).astype(low).astype(wide) * 0.125
                key = key * cosine + swap_halves(key) * sine
                if head % 2:
                    query, key, value = (pltpu.roll(v, half_lanes, 1) for v in (query, key, value))
                body = lane < half_lanes
                extra = extra_query + own * bias_ref[0, head] + own_two * bias_ref[1, head]
                query_ref[head, at, :] = jnp.where(body, query, extra).astype(low)
                key_ref[head, at, :] = jnp.where(body, key, extra_key).astype(low)
                value_ref[head, at, :] = jnp.where(body, value, extra_value).astype(low)
    block = min(length, 256)
    lane = lane_ids(block)

    @pl.loop(0, length // block)
    def _(i):
        at = pl.ds(pl.multiple_of(i * block, block), block)
        allowed = docs_column_ref[at, :] == docs_ref[...]
        done = []
        for head in range(heads):
            query = query_ref[head, at, :]
            scores = jnp.where(allowed, dot_t(query, key_ref[head]), masked_score)
            top = jnp.max(scores, axis=1, keepdims=True)
            weights = jnp.exp(scores - top).astype(low)
            summed = dot(weights, value_ref[head])
            total = summed[:, half_lanes : half_lanes + 1]
            one, two, three = three_pieces(-(top + jnp.log(total)))
            extra = jnp.where(lane == 77, one, jnp.where(lane == 78, two, jnp.where(lane == 79, three, 0.0)))
            query_ref[head, at, :] = jnp.where(lane < 77, query.astype(wide), extra).astype(low)
            done.append(summed / total)
        for base in range(0, heads, 2):
            both = done[base]
            if base + 1 < heads:
                both = jnp.where(lane < half_lanes, both, pltpu.roll(done[base + 1], half_lanes, 1))
            out_ref[at, base // 2 * lanes : (base // 2 + 1) * lanes] = both.astype(low)


def attend(bias, near, far, w, cosine, sine, ids, heads):
    length = 2 * near.shape[0]
    padded = w.shape[1] // 3
    vmem = pl.BlockSpec(memory_space=pltpu.VMEM)
    whole = jax.ShapeDtypeStruct((heads, length, lanes), low)
    return pl.pallas_call(
        functools.partial(attend_kernel, heads),
        out_shape=(whole, whole, whole, jax.ShapeDtypeStruct((length, padded), low)),
        in_specs=[pl.BlockSpec(memory_space=pltpu.SMEM)] + [vmem] * 7,
        out_specs=(vmem, vmem, vmem, vmem),
        scratch_shapes=[pltpu.VMEM((length, 1), jnp.int32)],
        compiler_params=pltpu.CompilerParams(vmem_limit_bytes=48 * 2**20),
        cost_estimate=pl.CostEstimate(
            flops=1 << 20, bytes_accessed=2**20, transcendentals=0
        ),
    )(bias, near, far, w, cosine, sine, *ids)


def attend_grad_kernel(
    heads,
    masks,
    *refs,
):
    if masks:
        place_ref, near_ref, far_ref, extra_ref, *refs = refs
        *refs, messages_ref, total_ref = refs
    attend_grad_body(heads, *refs)
    if not masks:
        return
    packed_ref, bias_ref = refs[12:14]
    half, width = near_ref.shape
    share = (messages_ref.shape[1] - 16) // len(masks[0])
    for start in range(0, width, 256):
        here = slice(start, start + 256)
        grads = t_dot(near_ref[:, here], packed_ref[:half, :]) + t_dot(far_ref[:, here], packed_ref[half:, :])
        total_ref[here, :] = grads.astype(low)
    columns = packed_ref.shape[1]
    row = lax.broadcasted_iota(jnp.int32, (16, columns), 0)
    lane = lax.broadcasted_iota(jnp.int32, (16, columns), 1)
    biases = jnp.zeros((16, columns), wide)
    for head in range(heads):
        for i in range(2):
            biases = jnp.where(lane == 2 * head + i, bias_ref[head, i], biases)
    high = biases.astype(low).astype(wide)
    biases = jnp.where(row == 0, high, jnp.where(row == 1, biases - high, 0.0))
    for i, part in enumerate(masks):
        for j, mask in enumerate(part):
            start = pl.multiple_of(jnp.bitwise_xor(place_ref[0], mask) * share, share)
            messages_ref[i, j * share : (j + 1) * share, :] = total_ref[pl.ds(start, share), :]
        messages_ref[i, len(part) * share :, :] = (extra_ref[i].astype(wide) + biases).astype(low)


def attend_grad_body(
    heads,
    query_ref,
    key_ref,
    value_ref,
    out_ref,
    grad_out_ref,
    cosine_ref,
    sine_ref,
    kinds_ref,
    docs_ref,
    w_ref,
    near_up_ref,
    far_up_ref,
    packed_ref,
    bias_ref,
    grad_query_ref,
    grad_key_ref,
    grad_value_ref,
    docs_column_ref,
):
    length = query_ref.shape[1]
    docs_column_ref[...] = column_of(docs_ref[...])
    padded = packed_ref.shape[1] // 3
    half = length // 2
    block = min(length, 256)
    lane = lane_ids(block)
    grad_key_ref[...] = jnp.zeros_like(grad_key_ref)
    grad_value_ref[...] = jnp.zeros_like(grad_value_ref)

    @pl.loop(0, length // block)
    def _(i):
        at = pl.ds(pl.multiple_of(i * block, block), block)
        allowed = docs_column_ref[...] == docs_ref[:, at]
        for head in range(heads):
            columns = slice(head // 2 * lanes, (head // 2 + 1) * lanes)
            grad_out = grad_out_ref[at, columns].astype(wide)
            product = grad_out * out_ref[at, columns].astype(wide)
            mine = (lane >= half_lanes) if head % 2 else (lane < half_lanes)
            row_dot = jnp.sum(jnp.where(mine, product, 0.0), axis=1, keepdims=True)
            one, two, three = three_pieces(-row_dot)
            if head % 2:
                grad_out = pltpu.roll(grad_out, half_lanes, 1)
            extra = jnp.where(lane == 64, one, jnp.where(lane == 65, two, jnp.where(lane == 66, three, 0.0)))
            grad_out = jnp.where(lane < half_lanes, grad_out, extra).astype(low)
            query, key = query_ref[head, at, :], key_ref[head]
            weights = jnp.exp(jnp.where(allowed, dot_t(key, query), masked_score))
            grad_scores = (weights * dot_t(value_ref[head], grad_out)).astype(low)
            grad_value_ref[head] += dot(weights.astype(low), grad_out)
            grad_key_ref[head] += dot(grad_scores, query)
            grad_query_ref[head, at, :] = t_dot(grad_scores, key)

    for start in range(0, length, block):
        at = slice(start, start + block)
        cosine, sine = cosine_ref[at, :], sine_ref[at, :]
        for base in range(0, heads, 2):

            def joined(ref):
                both = ref[base, at, :]
                if base + 1 < heads:
                    both = jnp.where(lane < half_lanes, both, pltpu.roll(ref[base + 1, at, :], half_lanes, 1))
                else:
                    both = jnp.where(lane < half_lanes, both, 0.0)
                return both

            columns = base // 2 * lanes
            query = joined(grad_query_ref) * 0.125
            key = joined(grad_key_ref)
            value = joined(grad_value_ref)
            query = query * cosine - swap_halves(query) * sine
            key = key * cosine - swap_halves(key) * sine
            for part, result in enumerate((query, key, value)):
                packed_ref[at, part * padded + columns : part * padded + columns + lanes] = result.astype(low)
    for start in range(0, half, block):
        here = slice(start, start + block)
        far_up_ref[here, :] = dot_t(packed_ref[half + start : half + start + block, :], w_ref[...]).astype(low)
        near_up_ref[here, :] = dot_t(packed_ref[here, :], w_ref[...]).astype(low)
    every = lane_ids(length)
    kinds = column_of(kinds_ref[...])
    for head in range(heads):
        grads = grad_key_ref[head]
        same = jnp.sum(jnp.where(every == 72 + kinds, grads, 0.0))
        total = jnp.sum(jnp.where(every == 76, grads, 0.0))
        bias_ref[head, 0] = same
        bias_ref[head, 1] = total - same


def attend_grad(query, key, value, out, grad_out, cosine, sine, ids, w, near, far, extra, place, masks):
    heads, length, _ = query.shape
    half, width = length // 2, w.shape[0]
    vmem, smem = pl.BlockSpec(memory_space=pltpu.VMEM), pl.BlockSpec(memory_space=pltpu.SMEM)
    columns = w.shape[1]
    out_shape = [
        jax.ShapeDtypeStruct((half, width), low),
        jax.ShapeDtypeStruct((half, width), low),
        jax.ShapeDtypeStruct((length, columns), low),
        jax.ShapeDtypeStruct((heads, 2), wide),
    ]
    scratch = [pltpu.VMEM((heads, length, lanes), wide)] * 3 + [pltpu.VMEM((length, 1), jnp.int32)]
    in_specs, out_specs = [vmem] * 10, [vmem] * 3 + [smem]
    operands = [query, key, value, out, grad_out, cosine, sine, *ids, w]
    kernel = functools.partial(attend_grad_kernel, heads, masks)
    if masks:
        share = width // sum(map(len, masks))
        in_specs = [smem, vmem, vmem, vmem] + in_specs
        operands = [place.reshape(1).astype(jnp.int32), near, far, extra] + operands
        out_shape.append(jax.ShapeDtypeStruct((len(masks), len(masks[0]) * share + 16, columns), low))
        out_specs = out_specs + [vmem]
        scratch = scratch + [pltpu.VMEM((width, columns), low)]

        def kernel(*refs):
            before, messages, after = refs[: len(in_specs) + 4], refs[len(in_specs) + 4], refs[len(in_specs) + 5 :]
            attend_grad_kernel(heads, masks, *before, *after[:-1], messages, after[-1])

    return pl.pallas_call(
        kernel,
        out_shape=out_shape,
        in_specs=in_specs,
        out_specs=out_specs,
        scratch_shapes=scratch,
        compiler_params=pltpu.CompilerParams(vmem_limit_bytes=48 * 2**20),
        cost_estimate=pl.CostEstimate(flops=4000 << 20, bytes_accessed=2**10, transcendentals=0),
    )(*operands)


def middle_grad_kernel(middle_ref, grad_out_ref, gain_ref, w_ref, *refs):
    *parts, grads_ref, branch_ref, merged_ref, gain_out_ref = refs
    middle = middle_ref[...]
    inverse = lax.rsqrt(jnp.mean(middle * middle, axis=-1, keepdims=True) + epsilon)
    unit = middle * inverse
    grads = total([part[...] for part in parts])
    gain_out_ref[...] = jnp.sum(grads * unit, axis=0, keepdims=True)
    grads = grads * gain_ref[...]
    mean = jnp.mean(grads * unit, axis=-1, keepdims=True)
    grads = grad_out_ref[...].astype(wide) + inverse * (grads - unit * mean)
    grads_ref[...] = grads
    branch = grads.astype(low)
    branch_ref[...] = branch
    merged_ref[...] = dot_t(branch, w_ref[...]).astype(low)


def middle_grad(middle, grad_out, gain, w, parts):
    return pl.pallas_call(
        middle_grad_kernel,
        out_shape=(
            jax.ShapeDtypeStruct(middle.shape, wide),
            jax.ShapeDtypeStruct(middle.shape, low),
            jax.ShapeDtypeStruct((middle.shape[0], w.shape[0]), low),
            jax.ShapeDtypeStruct((1, middle.shape[1]), wide),
        ),
        cost_estimate=pl.CostEstimate(flops=1 << 20, bytes_accessed=2**10, transcendentals=0),
    )(middle, grad_out, gain, w, *parts)


def feed_kernel(units, tokens_ref, grads_ref, w_ref, hidden_ref, grad_units_ref, up_ref, down_ref):
    gate_up = dot(tokens_ref[...], w_ref[:, : 2 * units])
    count = grads_ref.shape[0] * grads_ref.shape[1]
    grad_hidden = dot(grads_ref[...].reshape(count, -1), w_ref[:, 2 * units :])
    gate_values, up_values = gate_up[:, :units], gate_up[:, units:]
    sigmoid_gate = jax.nn.sigmoid(gate_values)
    activated = gate_values * sigmoid_gate
    hidden_ref[...] = (activated * up_values).astype(low)
    slope = sigmoid_gate + activated * (1.0 - sigmoid_gate)
    grad_units_ref[:, :units] = (grad_hidden * up_values * slope).astype(low)
    grad_units_ref[:, units:] = (grad_hidden * activated).astype(low)
    up_ref[...] = dot_t(grad_units_ref[...], w_ref[:, : 2 * units]).astype(low)
    down_ref[...] = dot_t(hidden_ref[...], w_ref[:, 2 * units :]).astype(low)


def feed(tokens, grads, w):
    count, width = tokens.shape
    rows = count // grads.shape[0]
    units = w.shape[1] // 3
    step = min(count, 256)
    return pl.pallas_call(
        functools.partial(feed_kernel, units),
        grid=(count // step,),
        out_shape=(
            jax.ShapeDtypeStruct((count, units), low),
            jax.ShapeDtypeStruct((count, 2 * units), low),
            jax.ShapeDtypeStruct((count, width), low),
            jax.ShapeDtypeStruct((count, width), low),
        ),
        in_specs=[
            pl.BlockSpec((step, width), lambda i: (i, 0)),
            pl.BlockSpec((step // rows, rows, width), lambda i: (i, 0, 0)),
            pl.BlockSpec(memory_space=pltpu.VMEM),
        ],
        out_specs=(
            pl.BlockSpec((step, units), lambda i: (i, 0)),
            pl.BlockSpec((step, 2 * units), lambda i: (i, 0)),
            pl.BlockSpec((step, width), lambda i: (i, 0)),
            pl.BlockSpec((step, width), lambda i: (i, 0)),
        ),
        compiler_params=pltpu.CompilerParams(vmem_limit_bytes=58 * 2**20),
        cost_estimate=pl.CostEstimate(
            flops=5000 << 20, bytes_accessed=2**10, transcendentals=0
        ),
    )(tokens, grads, w)


def feed_grad_kernel(units, *refs):
    *parts, out_ref = refs
    results = [0.0, 0.0]
    for tokens_ref, grads_ref, hidden_ref, grad_units_ref in (parts[:4], parts[4:]):
        grads = grads_ref[...]
        grads = grads.reshape(grads.shape[0] * grads.shape[1], -1)
        results[0] += t_dot(tokens_ref[...], grad_units_ref[...])
        results[1] += t_dot(grads, hidden_ref[...])
    out_ref[:, : 2 * units] = results[0].astype(low)
    out_ref[:, 2 * units :] = results[1].astype(low)


def feed_grad(near, far):
    tokens, grads, hidden, _ = near
    count, width = tokens.shape
    rows = count // grads.shape[0]
    units = hidden.shape[1]
    step = min(width, 256)
    whole = pl.BlockSpec(memory_space=pltpu.VMEM)
    part = [
        pl.BlockSpec((count, step), lambda i: (0, i)),
        pl.BlockSpec((grads.shape[0], rows, step), lambda i: (0, 0, i)),
        whole,
        whole,
    ]
    return pl.pallas_call(
        functools.partial(feed_grad_kernel, units),
        grid=(width // step,),
        out_shape=jax.ShapeDtypeStruct((width, 3 * units), low),
        in_specs=part + part,
        out_specs=pl.BlockSpec((step, 3 * units), lambda i: (i, 0)),
        compiler_params=pltpu.CompilerParams(vmem_limit_bytes=58 * 2**20),
        cost_estimate=pl.CostEstimate(
            flops=5000 << 20, bytes_accessed=2**10, transcendentals=0
        ),
    )(*near, *far)


def finish_input_kernel(tokens_ref, upstream_ref, grads_ref, out_ref):
    tokens = tokens_ref[...].astype(wide)
    upstream = upstream_ref[...].astype(wide)
    inverse = lax.rsqrt(jnp.mean(tokens * tokens, axis=-1, keepdims=True) + epsilon)
    unit = tokens * inverse
    mean = jnp.mean(upstream * unit, axis=-1, keepdims=True)
    out_ref[...] = (grads_ref[...] + inverse * (upstream - unit * mean)).astype(low)


def finish_input(tokens, upstream, grads):
    return pl.pallas_call(
        finish_input_kernel,
        out_shape=jax.ShapeDtypeStruct(tokens.shape, low),
        cost_estimate=pl.CostEstimate(flops=3000 << 20, bytes_accessed=2**20, transcendentals=0),
    )(tokens, upstream, grads)


def extra_rows(first, second):
    shape = (16, first.shape[1])
    row = lax.broadcasted_iota(jnp.int32, shape, 0)
    result = jnp.zeros(shape, wide)
    for i, value in enumerate((first, second)):
        high = value.astype(low).astype(wide)
        result = jnp.where(row == 2 * i, high, jnp.where(row == 2 * i + 1, value - high, result))
    return result.astype(low)


def moved(row, shift):
    rows = jnp.broadcast_to(row, (8, row.shape[1]))
    return pltpu.roll(rows, lax.rem(shift + row.shape[1], row.shape[1]), 1)[:1]


def first_lanes(row, count):
    return jnp.where(lax.broadcasted_iota(jnp.int32, row.shape, 1) < count, row, 0.0)


def qkv_sum_kernel(z_size, z_ref, *refs):
    *parts, out_ref, sum_ref = refs
    sum_ref[...] = total([part[...] for part in parts])
    count = (sum_ref.shape[0] - 16) // z_size
    extra = sum_ref[sum_ref.shape[0] - 16 :, :]
    bias, gain = extra[0:1] + extra[1:2], extra[2:3] + extra[3:4]
    for d in range(z_size):
        z = jnp.bitwise_xor(z_ref[0], d)
        out_ref[d, :count, :] = sum_ref[pl.ds(pl.multiple_of(z * count, count), count), :].astype(low)
        out_ref[d, count:, :] = extra_rows(bias, first_lanes(moved(gain, -z * count), count))


def qkv_sum(z, z_size, parts):
    rows, columns = parts[0].shape
    vmem = pl.BlockSpec(memory_space=pltpu.VMEM)
    return pl.pallas_call(
        functools.partial(qkv_sum_kernel, z_size),
        out_shape=jax.ShapeDtypeStruct((z_size, (rows - 16) // z_size + 16, columns), low),
        in_specs=[pl.BlockSpec(memory_space=pltpu.SMEM)] + [vmem] * len(parts),
        out_specs=vmem,
        scratch_shapes=[pltpu.VMEM((rows, columns), wide)],
        cost_estimate=pl.CostEstimate(flops=2**20, bytes_accessed=2**10, transcendentals=0),
    )(z.reshape(1).astype(jnp.int32), *parts)


def qkv_pack_kernel(biases, c_ref, *refs):
    *parts, own_ref, sent_ref, extra_ref = refs
    share = own_ref.shape[1]
    c = c_ref[0]
    bias, gain = 0.0, 0.0
    for d, part in enumerate(parts):
        own_ref[d] = part[pl.ds(pl.multiple_of(c * share, share), share), :]
        sent_ref[d * share : (d + 1) * share, :] = part[pl.ds(pl.multiple_of((1 - c) * share, share), share), :]
        extra = part[2 * share :, :].astype(wide)
        bias += moved(first_lanes(extra[0:1] + extra[1:2], biases), d * biases)
        gain += first_lanes(extra[2:3] + extra[3:4], 2 * share)
    gain_sent = first_lanes(moved(gain, -(1 - c) * share), share)
    sent_ref[len(parts) * share :, :] = extra_rows(bias, gain_sent)
    row = lax.broadcasted_iota(jnp.int32, extra_ref.shape, 0)
    gain_own = first_lanes(moved(gain, -c * share), share)
    extra_ref[...] = jnp.where(row == 0, bias, jnp.where(row == 1, gain_own, 0.0))


def qkv_pack(c, share, biases, parts):
    columns = parts[0].shape[1]
    vmem = pl.BlockSpec(memory_space=pltpu.VMEM)
    return pl.pallas_call(
        functools.partial(qkv_pack_kernel, biases),
        out_shape=(
            jax.ShapeDtypeStruct((len(parts), share, columns), low),
            jax.ShapeDtypeStruct((len(parts) * share + 16, columns), low),
            jax.ShapeDtypeStruct((8, columns), wide),
        ),
        in_specs=[pl.BlockSpec(memory_space=pltpu.SMEM)] + [vmem] * len(parts),
        out_specs=(vmem, vmem, vmem),
        cost_estimate=pl.CostEstimate(flops=2**20, bytes_accessed=2**10, transcendentals=0),
    )(c.reshape(1).astype(jnp.int32), *parts)


def finish_qkv_kernel(
    biases, group_ref, own_ref, got_ref, extra_ref, w_ref, gain_ref, out_ref, gain_out_ref, gain_two_ref, bias_ref
):
    count, share, _ = own_ref.shape
    low_half = lane_ids(share) < half_lanes
    gain = gain_ref[...].astype(wide)
    summed = jnp.zeros((share, lanes), wide)
    extra = got_ref[count * share :, :].astype(wide)
    bias_rows = extra_ref[0:1, :], extra[0:1] + extra[1:2]
    bias = jnp.zeros((1, bias_rows[0].shape[1]), wide)
    lane = lax.broadcasted_iota(jnp.int32, bias.shape, 1)
    for i in range(2 * count):
        d, e = i // 2, i % 2
        place = jnp.bitwise_xor(group_ref[0], i)
        parts = []
        for j in range(3):
            columns = slice(j * lanes, (j + 1) * lanes)
            part = got_ref[d * share : (d + 1) * share, columns] if e else own_ref[d, :, columns]
            parts.append(part.astype(wide))
        query, key, value = parts
        key = pltpu.roll(key, half_lanes, 1)
        parts = (
            jnp.where(low_half, query, key),
            jnp.where(low_half, value, query),
            jnp.where(low_half, key, value),
        )
        for j, part in enumerate(parts):
            at = pl.ds(pl.multiple_of(place * (3 * lanes) + j * lanes, lanes), lanes)
            summed += part * w_ref[:, at].astype(wide)
            out_ref[:, at] = part * gain
        here = (lane >= place * biases) & (lane < (place + 1) * biases)
        bias = jnp.where(here, moved(bias_rows[e], place * biases - d * biases), bias)
    column = jnp.broadcast_to(jnp.sum(summed, axis=1, keepdims=True), (share, lanes))
    gain_out_ref[...] = jnp.transpose(column)[:1, :]
    gain_two_ref[...] = (extra_ref[1:2, :] + extra[2:3] + extra[3:4])[:, :lanes]
    bias_ref[...] = bias[:, :lanes]


def finish_qkv(biases, group, own, got, extra, w, gain):
    vmem = pl.BlockSpec(memory_space=pltpu.VMEM)
    share = w.shape[0]
    return pl.pallas_call(
        functools.partial(finish_qkv_kernel, biases),
        out_shape=(
            jax.ShapeDtypeStruct(w.shape, wide),
            jax.ShapeDtypeStruct((1, share), wide),
            jax.ShapeDtypeStruct((1, lanes), wide),
            jax.ShapeDtypeStruct((1, lanes), wide),
        ),
        in_specs=[pl.BlockSpec(memory_space=pltpu.SMEM)] + [vmem] * 5,
        out_specs=(vmem,) * 4,
        cost_estimate=pl.CostEstimate(flops=3000 << 20, bytes_accessed=2**20, transcendentals=0),
    )(group.reshape(1).astype(jnp.int32), own, got, extra, w, gain)


def finish_feed_kernel(x_ref, both_ref, other_ref, gate_ref, up_ref, down_ref):
    depth, units = other_ref.shape[0], other_ref.shape[1] // 3
    mine = pl.ds(pl.multiple_of(x_ref[0] * depth, depth), depth)
    for value, x in ((both_ref[mine, :], x_ref[0]), (other_ref[...], 1 - x_ref[0])):
        at = pl.ds(pl.multiple_of(x * units, units), units)
        parts = [value[:, j * units : (j + 1) * units].astype(wide) for j in range(3)]
        gate_ref[:, at], up_ref[:, at] = parts[:2]
        if down_ref.shape[0] == 2 * units:
            down_ref[at, :] = jnp.transpose(parts[2])
        else:
            down_ref[:, at] = parts[2]


def finish_feed(x, both, other):
    vmem = pl.BlockSpec(memory_space=pltpu.VMEM)
    depth, units = other.shape[0], other.shape[1] // 3
    return pl.pallas_call(
        finish_feed_kernel,
        out_shape=(
            jax.ShapeDtypeStruct((depth, 2 * units), wide),
            jax.ShapeDtypeStruct((depth, 2 * units), wide),
            jax.ShapeDtypeStruct((2 * units, depth) if depth % lanes == 0 else (depth, 2 * units), wide),
        ),
        in_specs=[pl.BlockSpec(memory_space=pltpu.SMEM), vmem, vmem],
        out_specs=(vmem,) * 3,
        cost_estimate=pl.CostEstimate(flops=3000 << 20, bytes_accessed=2**20, transcendentals=0),
    )(x.reshape(1).astype(jnp.int32), both, other)


def rope_tables(stamps, dimension):
    halfway = dimension // 2
    frequency = jnp.exp(-math.log(10000.0) * jnp.arange(halfway, dtype=wide) / halfway)
    repeated = jnp.tile(frequency, lanes // halfway)
    angles = stamps.astype(wide)[:, None] * repeated[None, :]
    sign = jnp.where(jnp.arange(lanes) % dimension < halfway, -1.0, 1.0)
    return (jnp.cos(angles), jnp.sin(angles) * sign[None, :])


def shards(
    inputs,
    gain_attn,
    w_qkv,
    head_bias,
    w_out,
    gain_ffn,
    w_gate,
    w_up,
    w_down,
    time_ids,
    variate_ids,
    seq_ids,
    cotangent,
):
    at = Place()
    z_size, y_size = at.z_size, at.y_size
    tokens = inputs[0].astype(wide)
    rows, width = tokens.shape
    head_count = head_bias.shape[0]
    head_dim = width // head_count
    groups = at.seq_size
    heads = head_count // groups
    group_width = heads * head_dim
    padded = (heads + 1) // 2 * lanes
    share = width // (at.seq_size * at.head_size)
    group = 2 * at.z + at.c
    window = 2 * at.y + at.x
    device_id = at.seq * at.head_size + at.head

    inverse_one = lax.rsqrt(jnp.mean(tokens * tokens, axis=-1, keepdims=True) + epsilon)
    unit = tokens * inverse_one
    turned = called("tokens_turn", at.turn, unit.astype(low))

    depth, units = w_gate.shape[0], w_gate.shape[1] // 2
    gain_one = gain_attn.astype(wide)[:, None]
    scaled = (w_qkv.astype(wide) * gain_one).astype(low)

    def to_parts(columns):
        parts = columns.reshape(-1, groups, heads, 3, head_dim).transpose(0, 1, 3, 2, 4)
        parts = parts.reshape(-1, groups, 3, group_width)
        parts = jnp.pad(parts, ((0, 0), (0, 0), (0, 0), (0, padded - group_width)))
        return parts.reshape(-1, groups, 3 * padded)

    parts = to_parts(scaled).reshape(share, z_size, 2, 3 * padded)
    core_own = pick(at.c, parts[:, :, 0], parts[:, :, 1])
    core_sent = pick(at.c, parts[:, :, 1], parts[:, :, 0]).reshape(-1, 3 * padded)

    def with_extra(block, *values):
        extra = jnp.stack([jnp.pad(v.astype(low), (0, 3 * padded - v.shape[0])) for v in values])
        return jnp.concatenate([block, jnp.pad(extra, ((0, 16 - len(values)), (0, 0)))], axis=0)

    core_got = called("qkv_core", at.along_c, with_extra(core_sent, gain_ffn))
    both = jnp.stack([core_own, core_got[:-16].reshape(core_own.shape)])
    out_z = called("out_z", at.gather_steps, w_out, at.z_moves()).reshape(-1, width)
    gains = jnp.concatenate([gain_ffn, core_got[-16, :share]])
    sent = []
    for d in range(z_size):
        block = lax.dynamic_index_in_dim(both, jnp.bitwise_xor(at.z, d), axis=2, keepdims=False)
        sent.append(with_extra(block.reshape(-1, 3 * padded), gains))
    by_z = jnp.stack(called("qkv_z", at.scatter_z, sent))
    gains = by_z[:, -16, : 2 * share].reshape(-1)
    by_z = by_z[:, :-16].reshape(-1, 3 * padded)
    late_gate, late_up, late_down = w_gate, w_up, w_down
    by_z, late_gate, late_up, late_down = tied(by_z, w_gate, w_up, w_down)
    units = w_gate.shape[1] // 2
    down_t = with_layout_constraint(late_down.T, Layout(major_to_minor=(0, 1)))
    firsts = jnp.concatenate([v[:, :units] for v in (late_gate, late_up, down_t)], axis=1)
    seconds = jnp.concatenate([v[:, units:] for v in (late_gate, late_up, down_t)], axis=1)
    mine = pick(at.x, firsts, seconds)
    other = called("ffn_x", at.along_x, pick(at.x, seconds, firsts))
    z_block = jnp.concatenate([pick(at.x, mine, other), pick(at.x, other, mine)], axis=0)

    z_early = z_block
    near = called("tokens_z", at.gather_steps, turned, at.z_moves()[:-1])
    near = near
    near = join(near, called("tokens_z", at.z_moves()[-1], near)).reshape(-1, width)
    by_xy = jnp.stack(called("qkv_xy", at.gather_xy, with_extra(by_z, gains)))
    gains = by_xy[:, -16, : gains.shape[0]].reshape(y_size, 2, z_size, 2, share)
    gains = gains.transpose(2, 1, 0, 3, 4).reshape(-1, share)
    by_xy = by_xy[:, :-16]
    devices = jnp.arange(at.seq_size * at.head_size)
    from_device = (devices[None, :] == jnp.bitwise_xor(devices[:, None], device_id)).astype(low)
    gain_two = dot(from_device, gains).reshape(1, width)
    masks = [
        (2 * d + dx) * at.head_size + 2 * dy + e
        for dx, dy in at.pairs()
        for d in range(z_size)
        for e in range(2)
    ]
    w_heads = place(by_xy.reshape(-1, share, 3 * padded), device_id, masks).reshape(width, 3 * padded)

    out_xy = called("out_xy", at.gather_steps, out_z, at.xy_moves())

    grad_out = cotangent[0]
    grad_out_near = called("cotangent_x", at.gather_steps, grad_out, at.xy_moves()[:1])

    near, w_heads = tied(near, w_heads)
    near, out_xy = tied(near, out_xy)
    near, grad_out_near = tied(near, grad_out_near)
    w_ffn = lax.all_gather(z_block, "seq", axis=0, tiled=True, axis_index_groups=at.columns_z())

    time_ids, variate_ids, seq_ids, by_z = tied(time_ids, variate_ids, seq_ids, by_z)

    def of_window(ids):
        row = lax.dynamic_index_in_dim(ids, window, axis=0, keepdims=False).reshape(z_size, 2, rows)
        order = [
            lax.dynamic_slice(
                row, (jnp.bitwise_xor(at.z, d), jnp.bitwise_xor(at.c, e), 0), (1, 1, rows)
            ).reshape(rows)
            for e in range(2)
            for d in at.z_order()
        ]
        return jnp.concatenate(order)

    ids = (of_window(variate_ids).reshape(1, -1), of_window(seq_ids).reshape(1, -1))
    cosine, sine = rope_tables(of_window(time_ids), head_dim)
    local_bias = lax.dynamic_slice_in_dim(head_bias, group * heads, heads, 0)
    difference = local_bias[:, 0] - local_bias[:, 1]
    difference_high = difference.astype(low).astype(wide)
    bias = jnp.stack([difference_high, difference - difference_high])

    near, w_heads, cosine, sine, ids = tied(near, w_heads, cosine, sine, ids)
    far = called("tokens_core", at.along_c, near)
    query, key, value, attended = attend(bias, near, far, w_heads, cosine, sine, ids, heads)

    out_far = called("out_core", at.along_c, out_xy)
    out_blocks = jnp.stack([out_xy, out_far]).reshape(-1, share, width)
    out_masks = [
        (dx * z_size + d) * at.head_size + 2 * dy + e
        for e in range(2)
        for dx, dy in at.pairs()
        for d in range(z_size)
    ]
    out_rows = place(out_blocks, at.head, out_masks).reshape(width, width)

    sent = attended[:, :group_width].reshape(2, z_size, rows, group_width)
    places = {d: i for i, d in enumerate(at.z_order())}
    received = called("attended_z", at.scatter_z, [sent[:, places[d]] for d in range(z_size)])
    received = [received[d] for d in at.z_order()]
    kept = jnp.concatenate([block[0] for block in received], axis=1)
    passed = jnp.concatenate([block[1] for block in received], axis=1)
    held = grad_out_near[None]
    for move in at.xy_moves()[1:]:
        got = called("cotangent_y", move, held)
        got, passed = tied(got, passed)
        held = jnp.concatenate([held, got], axis=0)
    grad_out_near = held.reshape(2 * y_size, rows, width)
    grad_out_far = called("cotangent_core", at.along_c, grad_out_near)

    passed = called("attended_core", at.along_c, passed)

    merged = called("attended_turn", at.turn, jnp.concatenate([kept, passed], axis=1))

    middle = tokens + dot(merged, out_rows)
    inverse_two = lax.rsqrt(jnp.mean(middle * middle, axis=-1, keepdims=True) + epsilon)
    unit_two = middle * inverse_two
    normed_two = (unit_two * gain_two).astype(low)
    normed_near = jnp.concatenate(called("normed_xy", at.gather_xy, normed_two), axis=0)
    normed_far = called("normed_core", at.along_c, normed_near)

    hidden_far, units_far, up_far, down_far = feed(normed_far, grad_out_far, w_ffn)
    hidden_near, units_near, up_near, down_near = feed(normed_near, grad_out_near, w_ffn)

    blocks = (2 * y_size, rows, width)
    up = up_near.reshape(blocks), called("up_core", at.along_c, up_far).reshape(blocks)
    kept = [total([part[i] for part in up]).astype(low) for i in range(2 * y_size)]
    grad_w_ffn = feed_grad(
        (normed_near, grad_out_near, hidden_near, units_near),
        (normed_far, grad_out_far, hidden_far, units_far),
    )
    received = called("up_xy", at.scatter_xy, kept)
    down = [down_near.reshape(blocks), called("down_core", at.along_c, down_far).reshape(blocks)]
    moves = at.xy_moves()
    y_cut = y_size // 2
    down = [part.reshape(y_size, 2, rows, width) for part in down]
    down_sent = total([part[y_cut:] for part in down]).astype(low)
    received[0], down_sent = tied(received[0], down_sent)
    down = [part[:y_cut] for part in down] + [called("down_y", moves[-1], down_sent)]
    *received[1:], grad_w_ffn = tied(*received[1:], grad_w_ffn)
    grad_middle, grad_branch, grad_merged, gain_part = middle_grad(middle, grad_out, gain_two, out_rows, received)

    turned_back = called("merged_turn", at.turn, grad_merged)
    grad_w_ffn = lax.psum_scatter(
        grad_w_ffn, "seq", scatter_dimension=0, tiled=True, axis_index_groups=at.columns_z()
    )
    cut = width // 2
    kept, passed = turned_back[:, :cut], called("merged_core", at.along_c, turned_back[:, cut:])
    merged, grad_branch, passed = tied(merged, grad_branch, passed)
    sent = []
    for d in range(z_size):
        columns = slice(places[d] * group_width, (places[d] + 1) * group_width)
        sent.append(jnp.stack([part[:, columns] for part in (kept, passed)]))
    received_z = called("merged_z", at.scatter_z, sent)
    received_one = received_z[1]

    grad_out_rows = t_dot(merged, grad_branch).astype(low)
    grad_out_rows = fetch(grad_out_rows.reshape(-1, share, width), at.head, out_masks)
    grad_out_rows = grad_out_rows.reshape(2, y_size, 2, z_size * share, width)
    out_parts = [grad_out_rows[0], called("w_out_core", at.along_c, grad_out_rows[1])]
    out_sent = total([part[y_cut:] for part in out_parts]).astype(low)
    received_one, out_sent = tied(received_one, out_sent)
    received_z[1] = received_one
    received = jnp.stack([received_z[d] for d in at.z_order()], axis=1)
    grad_attended = received.reshape(2 * z_size * rows, group_width)
    if padded > group_width:
        grad_attended = jnp.pad(grad_attended, ((0, 0), (0, padded - group_width)))
    down = called("down_y", at.scatter_steps, down, moves[1:-1])
    down = [part.reshape(2, rows, width) for part in down]
    down_sent = total([part[1] for part in down]).astype(low)
    down = [part[0] for part in down] + [called("down_x", moves[0], down_sent)]
    grad_attended, out_sent = tied(grad_attended, out_sent)
    grad_attended, down[-1] = tied(grad_attended, down[-1])
    out_got = called("w_out_y", moves[-1], out_sent)
    out_parts = [part[:y_cut] for part in out_parts] + [out_got]

    def halves(values):
        high = values.astype(low)
        return high, (values - high.astype(wide)).astype(low)

    gain_part = gain_part.reshape(z_size, 2, y_size, 2, share)
    bias_count, gain_count = 2 * heads, 2 * z_size * share
    extra, device_masks = [], []
    for dx, dy in at.pairs():
        x, y = jnp.bitwise_xor(at.x, dx), jnp.bitwise_xor(at.y, dy)
        gain = lax.dynamic_slice(gain_part, (0, x, y, 0, 0), (z_size, 1, 1, 2, share)).reshape(-1)
        none = jnp.zeros((0, 3 * padded), low)
        extra.append(with_extra(none, *(jnp.zeros_like(v) for v in halves(gain)), *halves(gain)))
        device_masks.append([
            (2 * d + dx) * at.head_size + 2 * dy + e for d in range(z_size) for e in range(2)
        ])
    extra = jnp.stack(extra)
    place_xy = at.x * at.head_size + 2 * at.y
    in_kernel = share % 16 == 0
    upstream_near, upstream_far, grad_packed, bias_grad, *messages = attend_grad(
        query, key, value, attended, grad_attended, cosine, sine, ids, w_heads,
        near, far, extra, place_xy, device_masks if in_kernel else None,
    )
    half = near.shape[0]
    if in_kernel:
        messages = [messages[0][i] for i in range(2 * y_size)]
    else:
        grad_heads = t_dot(near, grad_packed[:half]) + t_dot(far, grad_packed[half:])
        grad_heads = grad_heads.astype(low).reshape(-1, share, 3 * padded)
        none = jnp.zeros((0, 3 * padded), low)
        biases = with_extra(none, *halves(bias_grad.reshape(-1)))
        messages = [
            jnp.concatenate([
                lax.dynamic_index_in_dim(grad_heads, jnp.bitwise_xor(place_xy, mask), 0, False)
                for mask in masks
            ] + [extra[i] + biases])
            for i, masks in enumerate(device_masks)
        ]

    upstream_far, out_parts[-1] = tied(upstream_far, out_parts[-1])
    upstream_far = called("input_core", at.along_c, upstream_far)
    z_moves = at.z_moves()
    blocks = (z_size, rows, width)
    upstream_z = [upstream_near.reshape(blocks), upstream_far.reshape(blocks)]
    z_cut = z_size // 2
    upstream_sent = total([part[z_cut:] for part in upstream_z]).astype(low)
    upstream_z = [part[:z_cut] for part in upstream_z] + [called("input_z", z_moves[-1], upstream_sent)]

    out_parts = called("w_out_y", at.scatter_steps, out_parts, moves[1:-1])
    out_parts = [part.reshape(2, -1, width) for part in out_parts]
    out_parts = called("w_out_x", at.scatter_steps, out_parts, moves[:1])
    out_parts[-1] = out_parts[-1]

    def joined(block, row, count):
        return block[row, :count].astype(wide) + block[row + 1, :count].astype(wide)

    received = called("grad_qkv_xy", at.scatter_xy, messages)
    fast = in_kernel and heads == 2 and head_dim == half_lanes
    if fast:
        sent = qkv_sum(at.z, z_size, received)
    else:
        summed = total(received)
        bias_sum = joined(summed[-16:], 0, bias_count)
        gain_sum = joined(summed[-16:], 2, gain_count).reshape(z_size, 2 * share)
        summed = summed[:-16].astype(low).reshape(z_size, 2 * share, 3 * padded)
        sent = []
        for d in range(z_size):
            block, gain = (
                lax.dynamic_index_in_dim(v, jnp.bitwise_xor(at.z, d), axis=0, keepdims=False)
                for v in (summed, gain_sum)
            )
            sent.append(with_extra(block, *halves(bias_sum), *halves(gain)))
    depth = grad_w_ffn.shape[0] // 2
    other = called("grad_ffn_x", at.along_x, pick(at.x, grad_w_ffn[depth:], grad_w_ffn[:depth]))
    upstream_z[-1], other = tied(upstream_z[-1], other)
    upstream_z[-1], sent = tied(upstream_z[-1], sent)
    z_cut = z_cut // 2
    upstream_sent = total([part[z_cut:] for part in upstream_z]).astype(low)
    upstream_sent, sent = tied(upstream_sent, sent)
    upstream_z = [part[:z_cut] for part in upstream_z] + [called("input_z", z_moves[-2], upstream_sent)]
    grad_w_gate, grad_w_up, grad_w_down = finish_feed(at.x, grad_w_ffn, other)
    if grad_w_down.shape != w_down.shape:
        grad_w_down = grad_w_down.T
    upstream_z[-1] = after(upstream_z[-1], grad_w_gate)
    upstream_one = total(called("input_z", at.scatter_steps, upstream_z, z_moves[:-2]))[0]
    out_parts[-1] = out_parts[-1]
    output = middle + total(down)
    out_parts = [part.reshape(z_size, share, width) for part in out_parts]
    grad_w_out = total(called("w_out_z", at.scatter_steps, out_parts, z_moves))[0]
    received = called("grad_qkv_z", at.scatter_z, [sent[d] for d in range(z_size)])
    upstream_one, received[0] = tied(upstream_one, received[0])
    if fast:
        core_own, core_sent, extra_own = qkv_pack(at.c, share, bias_count, received)
    else:
        bias_z = jnp.concatenate([joined(block[-16:], 0, bias_count) for block in received])
        gain_sum = functools.reduce(jnp.add, [joined(block[-16:], 2, 2 * share) for block in received])
        received = jnp.stack([block[:-16] for block in received]).reshape(z_size, 2, share, 3 * padded)
        core_own = pick(at.c, received[:, 0], received[:, 1])
        core_sent = pick(at.c, received[:, 1], received[:, 0]).reshape(-1, 3 * padded)
        gain_own = pick(at.c, gain_sum[:share], gain_sum[share:])
        gain_sent = pick(at.c, gain_sum[share:], gain_sum[:share])
        core_sent = with_extra(core_sent, *halves(bias_z), *halves(gain_sent))
    upstream_one = upstream_one.astype(low)
    core_sent = core_sent
    upstream_one = called("input_turn", at.turn, upstream_one)
    grad_input = finish_input(inputs[0], upstream_one, grad_middle)
    core_got = called("grad_qkv_core", at.along_c, core_sent)
    if fast:
        grad_w_qkv, grad_gain_attn, grad_gain_ffn, full_bias = finish_qkv(
            bias_count, group, core_own, core_got, extra_own, w_qkv, gain_attn[:, None]
        )
        grad_gain_attn, grad_gain_ffn = grad_gain_attn[0], grad_gain_ffn[0, :share]
        full_bias = full_bias[0, : 2 * head_count].reshape(head_count, 2)
    else:
        core_other = core_got[:-16].reshape(z_size, share, 3 * padded)
        grad_gain_ffn = gain_own + joined(core_got[-16:], 2, share)
        biases = jnp.stack([bias_z, joined(core_got[-16:], 0, z_size * bias_count)])
        biases = list(biases.reshape(2, z_size, heads, 2).transpose(1, 0, 2, 3).reshape(groups, heads, 2))
        full_bias = jnp.concatenate(xor_list(biases, group), axis=0)
        by_group = jnp.stack([core_own, core_other], axis=1).reshape(groups, share, 3 * padded)
        by_group = place(by_group, group, list(range(groups))).astype(wide).reshape(groups, share, 3, padded)
        by_group = by_group[..., :group_width].reshape(groups, share, 3, heads, head_dim)
        raw = by_group.transpose(1, 0, 3, 2, 4).reshape(share, 3 * width)
        grad_w_qkv = raw * gain_one
        grad_gain_attn = jnp.sum(raw * w_qkv.astype(wide), axis=1)

    return (
        output.astype(low).reshape(1, rows, width),
        grad_input.reshape(1, rows, width),
        grad_gain_attn,
        grad_w_qkv,
        full_bias,
        grad_w_out,
        grad_gain_ffn,
        grad_w_gate,
        grad_w_up,
        grad_w_down,
    )


def solution(mesh):
    placed = (
        P("head", "seq", None),
        P(("seq", "head")),
        P(("seq", "head"), None),
        P(),
        P(("seq", "head"), None),
        P(("seq", "head")),
        P("seq", "head"),
        P("seq", "head"),
        P("head", "seq"),
        P(),
        P(),
        P(),
        P("head", "seq", None),
    )
    return jax.shard_map(
        shards,
        mesh=mesh,
        in_specs=placed,
        out_specs=(
            P("head", "seq", None),
            P("head", "seq", None),
            P(("seq", "head")),
            P(("seq", "head"), None),
            P(),
            P(("seq", "head"), None),
            P(("seq", "head")),
            P("seq", "head"),
            P("seq", "head"),
            P("head", "seq"),
        ),
        check_vma=False,
    )
```

```python
import functools
import math

import jax
import jax.numpy as jnp
from jax import lax
from jax.experimental import pallas as pl
from jax.experimental.layout import Layout, with_layout_constraint
from jax.experimental.pallas import tpu as pltpu
from jax.sharding import PartitionSpec as P


epsilon = 1e-05
masked_score = -1e30
low = jnp.bfloat16
wide = jnp.float32
lanes = 128
half_lanes = 64


def dot(a, b):
    return jnp.dot(a, b, preferred_element_type=wide)


def dot_t(a, b):
    return lax.dot_general(a, b, (((1,), (1,)), ((), ())), preferred_element_type=wide)


def t_dot(a, b):
    return lax.dot_general(a, b, (((0,), (0,)), ((), ())), preferred_element_type=wide)


class Place:
    def __init__(self):
        self.seq_size = lax.axis_size("seq")
        self.head_size = lax.axis_size("head")
        self.z_size = self.seq_size // 2
        self.y_size = self.head_size // 2
        self.seq = lax.axis_index("seq")
        self.head = lax.axis_index("head")
        self.z, self.x = self.seq // 2, self.seq % 2
        self.y, self.c = self.head // 2, self.head % 2

    def along_z(self, value, step):
        return lax.ppermute(value, "seq", [(i, i ^ (2 * step)) for i in range(self.seq_size)])

    def along_x(self, value):
        return lax.ppermute(value, "seq", [(i, i ^ 1) for i in range(self.seq_size)])

    def along_c(self, value):
        return lax.ppermute(value, "head", [(i, i ^ 1) for i in range(self.head_size)])

    def along_xy(self, value, dx, dy):
        if dy == 0:
            return self.along_x(value)
        if dx == 0:
            return lax.ppermute(
                value, "head", [(i, i ^ (2 * dy)) for i in range(self.head_size)]
            )
        return lax.ppermute(
            value,
            ("seq", "head"),
            [
                (s * self.head_size + h, (s ^ dx) * self.head_size + (h ^ (2 * dy)))
                for s in range(self.seq_size)
                for h in range(self.head_size)
            ],
        )

    def turn(self, value):
        return lax.ppermute(
            value,
            ("seq", "head"),
            [
                (s * self.head_size + h, ((s & ~1) | (h & 1)) * self.head_size + ((h & ~1) | (s & 1)))
                for s in range(self.seq_size)
                for h in range(self.head_size)
            ],
        )

    def pairs(self):
        return [(dx, dy) for dy in range(self.y_size) for dx in range(2)]

    def gather_xy(self, value):
        return [value if d == (0, 0) else self.along_xy(value, *d) for d in self.pairs()]

    def scatter_xy(self, blocks):
        return [
            block if d == (0, 0) else self.along_xy(block, *d)
            for d, block in zip(self.pairs(), blocks)
        ]

    def columns_z(self):
        return [[x + 2 * z for z in range(self.z_size)] for x in range(2)]

    def gather_z(self, value):
        return [value if d == 0 else self.along_z(value, d) for d in range(self.z_size)]

    def scatter_z(self, blocks):
        return [block if d == 0 else self.along_z(block, d) for d, block in enumerate(blocks)]

    def gather_steps(self, value, moves):
        held = value[None]
        for move in moves:
            held = jnp.concatenate([held, move(held)], axis=0)
        return held

    def scatter_steps(self, addends, moves):
        for move in reversed(moves):
            cut = addends[0].shape[0] // 2
            received = move(total([value[cut:] for value in addends]).astype(low))
            if len(addends) > 2:
                addends = [total([value[:cut] for value in addends])]
            else:
                addends = [value[:cut] for value in addends]
            addends = addends + [received]
        return addends

    def xy_moves(self):
        steps = [1 << i for i in range(self.y_size.bit_length() - 1)]
        return [self.along_x] + [functools.partial(self.along_xy, dx=0, dy=step) for step in steps]

    def z_moves(self):
        steps = [1 << i for i in reversed(range(self.z_size.bit_length() - 1))]
        return [functools.partial(self.along_z, step=step) for step in steps]

    def z_order(self):
        order = [0]
        for step in [1 << i for i in reversed(range(self.z_size.bit_length() - 1))]:
            order = order + [step ^ d for d in order]
        return order


def called(name, move, *operands):
    with jax.named_scope(name):
        return move(*operands)


def total(addends):
    return functools.reduce(jnp.add, [value.astype(wide) for value in addends])


def after(value, *others):
    return lax.optimization_barrier((value, others))[0]


def tied(*values):
    return lax.optimization_barrier(values)


def pick(bit, zero, one):
    return jnp.where(bit == 0, zero, one)


def xor_list(blocks, me):
    step = 1
    while step < len(blocks):
        on = (me // step) % 2
        blocks = [pick(on, blocks[i], blocks[i ^ step]) for i in range(len(blocks))]
        step *= 2
    return blocks


def place_kernel(masks, me_ref, in_ref, out_ref):
    for i, mask in enumerate(masks):
        out_ref[jnp.bitwise_xor(me_ref[0], mask)] = in_ref[i]


def fetch_kernel(masks, me_ref, in_ref, out_ref):
    for i, mask in enumerate(masks):
        out_ref[i] = in_ref[jnp.bitwise_xor(me_ref[0], mask)]


def move_blocks(kernel, blocks, me, masks):
    return pl.pallas_call(
        functools.partial(kernel, masks),
        out_shape=jax.ShapeDtypeStruct(blocks.shape, blocks.dtype),
        in_specs=[pl.BlockSpec(memory_space=pltpu.SMEM), pl.BlockSpec(memory_space=pltpu.VMEM)],
        out_specs=pl.BlockSpec(memory_space=pltpu.VMEM),
        compiler_params=pltpu.CompilerParams(vmem_limit_bytes=32 * 2**20),
        cost_estimate=pl.CostEstimate(flops=0, bytes_accessed=4 * blocks.size, transcendentals=0),
    )(me.reshape(1).astype(jnp.int32), blocks)


def place(blocks, me, masks):
    return move_blocks(place_kernel, blocks, me, masks)


def fetch(blocks, me, masks):
    return move_blocks(fetch_kernel, blocks, me, masks)


def join_kernel(first_ref, second_ref, out_ref):
    count = first_ref.shape[0]
    out_ref[:count] = first_ref[...]
    out_ref[count:] = second_ref[...]


def join(first, second):
    return pl.pallas_call(
        join_kernel,
        out_shape=jax.ShapeDtypeStruct((2 * first.shape[0],) + first.shape[1:], first.dtype),
        cost_estimate=pl.CostEstimate(flops=1 << 20, bytes_accessed=2**10, transcendentals=0),
    )(first, second)


def lane_ids(rows):
    return lax.broadcasted_iota(jnp.int32, (rows, lanes), 1)


def swap_halves(value):
    first = lane_ids(value.shape[0]) % half_lanes < half_lanes // 2
    return jnp.where(first, pltpu.roll(value, lanes - 32, 1), pltpu.roll(value, 32, 1))


def column_of(row):
    wide_row = jnp.broadcast_to(row.astype(wide), (8, row.shape[1]))
    return jnp.transpose(wide_row)[:, :1].astype(jnp.int32)


def three_pieces(value):
    one = value.astype(low).astype(wide)
    rest = value - one
    two = rest.astype(low).astype(wide)
    return one, two, (rest - two).astype(low).astype(wide)


def attend_kernel(
    heads,
    bias_ref,
    near_ref,
    far_ref,
    w_ref,
    cosine_ref,
    sine_ref,
    kinds_ref,
    docs_ref,
    query_ref,
    key_ref,
    value_ref,
    out_ref,
    docs_column_ref,
):
    rows = near_ref.shape[0]
    docs_column_ref[...] = column_of(docs_ref[...])
    length = 2 * rows
    step = min(rows, 256)
    padded = w_ref.shape[1] // 3
    for part, source in enumerate((near_ref, far_ref)):
        for start in range(0, rows, step):
            at = pl.ds(part * rows + start, step)
            packed = dot(source[start : start + step, :], w_ref[...])
            cosine, sine = cosine_ref[at, :], sine_ref[at, :]
            lane = lane_ids(step)
            kind = column_of(kinds_ref[:, at])
            own = (lane == 64 + kind).astype(wide)
            own_two = (lane == 68 + kind).astype(wide)
            extra_query = ((lane == 72 + kind) | (lane == 76)).astype(wide)
            extra_key = own + own_two + ((lane >= 77) & (lane < 80)).astype(wide)
            extra_value = ((lane >= 64) & (lane < 67)).astype(wide)
            for head in range(heads):
                base = head // 2 * lanes
                query = packed[:, base : base + lanes]
                key = packed[:, padded + base : padded + base + lanes]
                value = packed[:, 2 * padded + base : 2 * padded + base + lanes]
                query = (query * cosine + swap_halves(query) * sine).astype(low).astype(wide) * 0.125
                key = key * cosine + swap_halves(key) * sine
                if head % 2:
                    query, key, value = (pltpu.roll(v, half_lanes, 1) for v in (query, key, value))
                body = lane < half_lanes
                extra = extra_query + own * bias_ref[0, head] + own_two * bias_ref[1, head]
                query_ref[head, at, :] = jnp.where(body, query, extra).astype(low)
                key_ref[head, at, :] = jnp.where(body, key, extra_key).astype(low)
                value_ref[head, at, :] = jnp.where(body, value, extra_value).astype(low)
    block = min(length, 256)
    lane = lane_ids(block)

    @pl.loop(0, length // block)
    def _(i):
        at = pl.ds(pl.multiple_of(i * block, block), block)
        allowed = docs_column_ref[at, :] == docs_ref[...]
        done = []
        for head in range(heads):
            query = query_ref[head, at, :]
            scores = jnp.where(allowed, dot_t(query, key_ref[head]), masked_score)
            top = jnp.max(scores, axis=1, keepdims=True)
            weights = jnp.exp(scores - top).astype(low)
            summed = dot(weights, value_ref[head])
            total = summed[:, half_lanes : half_lanes + 1]
            one, two, three = three_pieces(-(top + jnp.log(total)))
            extra = jnp.where(lane == 77, one, jnp.where(lane == 78, two, jnp.where(lane == 79, three, 0.0)))
            query_ref[head, at, :] = jnp.where(lane < 77, query.astype(wide), extra).astype(low)
            done.append(summed / total)
        for base in range(0, heads, 2):
            both = done[base]
            if base + 1 < heads:
                both = jnp.where(lane < half_lanes, both, pltpu.roll(done[base + 1], half_lanes, 1))
            out_ref[at, base // 2 * lanes : (base // 2 + 1) * lanes] = both.astype(low)


def attend(bias, near, far, w, cosine, sine, ids, heads):
    length = 2 * near.shape[0]
    padded = w.shape[1] // 3
    vmem = pl.BlockSpec(memory_space=pltpu.VMEM)
    whole = jax.ShapeDtypeStruct((heads, length, lanes), low)
    return pl.pallas_call(
        functools.partial(attend_kernel, heads),
        out_shape=(whole, whole, whole, jax.ShapeDtypeStruct((length, padded), low)),
        in_specs=[pl.BlockSpec(memory_space=pltpu.SMEM)] + [vmem] * 7,
        out_specs=(vmem, vmem, vmem, vmem),
        scratch_shapes=[pltpu.VMEM((length, 1), jnp.int32)],
        compiler_params=pltpu.CompilerParams(vmem_limit_bytes=48 * 2**20),
        cost_estimate=pl.CostEstimate(
            flops=1 << 20, bytes_accessed=2**20, transcendentals=0
        ),
    )(bias, near, far, w, cosine, sine, *ids)


def attend_grad_kernel(
    heads,
    masks,
    *refs,
):
    if masks:
        place_ref, near_ref, far_ref, extra_ref, *refs = refs
        *refs, messages_ref, total_ref = refs
    attend_grad_body(heads, *refs)
    if not masks:
        return
    packed_ref, bias_ref = refs[12:14]
    half, width = near_ref.shape
    share = (messages_ref.shape[1] - 16) // len(masks[0])
    for start in range(0, width, 256):
        here = slice(start, start + 256)
        grads = t_dot(near_ref[:, here], packed_ref[:half, :]) + t_dot(far_ref[:, here], packed_ref[half:, :])
        total_ref[here, :] = grads.astype(low)
    columns = packed_ref.shape[1]
    row = lax.broadcasted_iota(jnp.int32, (16, columns), 0)
    lane = lax.broadcasted_iota(jnp.int32, (16, columns), 1)
    biases = jnp.zeros((16, columns), wide)
    for head in range(heads):
        for i in range(2):
            biases = jnp.where(lane == 2 * head + i, bias_ref[head, i], biases)
    high = biases.astype(low).astype(wide)
    biases = jnp.where(row == 0, high, jnp.where(row == 1, biases - high, 0.0))
    for i, part in enumerate(masks):
        for j, mask in enumerate(part):
            start = pl.multiple_of(jnp.bitwise_xor(place_ref[0], mask) * share, share)
            messages_ref[i, j * share : (j + 1) * share, :] = total_ref[pl.ds(start, share), :]
        messages_ref[i, len(part) * share :, :] = (extra_ref[i].astype(wide) + biases).astype(low)


def attend_grad_body(
    heads,
    query_ref,
    key_ref,
    value_ref,
    out_ref,
    grad_out_ref,
    cosine_ref,
    sine_ref,
    kinds_ref,
    docs_ref,
    w_ref,
    near_up_ref,
    far_up_ref,
    packed_ref,
    bias_ref,
    grad_query_ref,
    grad_key_ref,
    grad_value_ref,
    docs_column_ref,
):
    length = query_ref.shape[1]
    docs_column_ref[...] = column_of(docs_ref[...])
    padded = packed_ref.shape[1] // 3
    half = length // 2
    block = min(length, 256)
    lane = lane_ids(block)
    grad_key_ref[...] = jnp.zeros_like(grad_key_ref)
    grad_value_ref[...] = jnp.zeros_like(grad_value_ref)

    @pl.loop(0, length // block)
    def _(i):
        at = pl.ds(pl.multiple_of(i * block, block), block)
        allowed = docs_column_ref[...] == docs_ref[:, at]
        for head in range(heads):
            columns = slice(head // 2 * lanes, (head // 2 + 1) * lanes)
            grad_out = grad_out_ref[at, columns].astype(wide)
            product = grad_out * out_ref[at, columns].astype(wide)
            mine = (lane >= half_lanes) if head % 2 else (lane < half_lanes)
            row_dot = jnp.sum(jnp.where(mine, product, 0.0), axis=1, keepdims=True)
            one, two, three = three_pieces(-row_dot)
            if head % 2:
                grad_out = pltpu.roll(grad_out, half_lanes, 1)
            extra = jnp.where(lane == 64, one, jnp.where(lane == 65, two, jnp.where(lane == 66, three, 0.0)))
            grad_out = jnp.where(lane < half_lanes, grad_out, extra).astype(low)
            query, key = query_ref[head, at, :], key_ref[head]
            weights = jnp.exp(jnp.where(allowed, dot_t(key, query), masked_score))
            grad_scores = (weights * dot_t(value_ref[head], grad_out)).astype(low)
            grad_value_ref[head] += dot(weights.astype(low), grad_out)
            grad_key_ref[head] += dot(grad_scores, query)
            grad_query_ref[head, at, :] = t_dot(grad_scores, key)

    for start in range(0, length, block):
        at = slice(start, start + block)
        cosine, sine = cosine_ref[at, :], sine_ref[at, :]
        for base in range(0, heads, 2):

            def joined(ref):
                both = ref[base, at, :]
                if base + 1 < heads:
                    both = jnp.where(lane < half_lanes, both, pltpu.roll(ref[base + 1, at, :], half_lanes, 1))
                else:
                    both = jnp.where(lane < half_lanes, both, 0.0)
                return both

            columns = base // 2 * lanes
            query = joined(grad_query_ref) * 0.125
            key = joined(grad_key_ref)
            value = joined(grad_value_ref)
            query = query * cosine - swap_halves(query) * sine
            key = key * cosine - swap_halves(key) * sine
            for part, result in enumerate((query, key, value)):
                packed_ref[at, part * padded + columns : part * padded + columns + lanes] = result.astype(low)
    for start in range(0, half, block):
        here = slice(start, start + block)
        far_up_ref[here, :] = dot_t(packed_ref[half + start : half + start + block, :], w_ref[...]).astype(low)
        near_up_ref[here, :] = dot_t(packed_ref[here, :], w_ref[...]).astype(low)
    every = lane_ids(length)
    kinds = column_of(kinds_ref[...])
    for head in range(heads):
        grads = grad_key_ref[head]
        same = jnp.sum(jnp.where(every == 72 + kinds, grads, 0.0))
        total = jnp.sum(jnp.where(every == 76, grads, 0.0))
        bias_ref[head, 0] = same
        bias_ref[head, 1] = total - same


def attend_grad(query, key, value, out, grad_out, cosine, sine, ids, w, near, far, extra, place, masks):
    heads, length, _ = query.shape
    half, width = length // 2, w.shape[0]
    vmem, smem = pl.BlockSpec(memory_space=pltpu.VMEM), pl.BlockSpec(memory_space=pltpu.SMEM)
    columns = w.shape[1]
    out_shape = [
        jax.ShapeDtypeStruct((half, width), low),
        jax.ShapeDtypeStruct((half, width), low),
        jax.ShapeDtypeStruct((length, columns), low),
        jax.ShapeDtypeStruct((heads, 2), wide),
    ]
    scratch = [pltpu.VMEM((heads, length, lanes), wide)] * 3 + [pltpu.VMEM((length, 1), jnp.int32)]
    in_specs, out_specs = [vmem] * 10, [vmem] * 3 + [smem]
    operands = [query, key, value, out, grad_out, cosine, sine, *ids, w]
    kernel = functools.partial(attend_grad_kernel, heads, masks)
    if masks:
        share = width // sum(map(len, masks))
        in_specs = [smem, vmem, vmem, vmem] + in_specs
        operands = [place.reshape(1).astype(jnp.int32), near, far, extra] + operands
        out_shape.append(jax.ShapeDtypeStruct((len(masks), len(masks[0]) * share + 16, columns), low))
        out_specs = out_specs + [vmem]
        scratch = scratch + [pltpu.VMEM((width, columns), low)]

        def kernel(*refs):
            before, messages, after = refs[: len(in_specs) + 4], refs[len(in_specs) + 4], refs[len(in_specs) + 5 :]
            attend_grad_kernel(heads, masks, *before, *after[:-1], messages, after[-1])

    return pl.pallas_call(
        kernel,
        out_shape=out_shape,
        in_specs=in_specs,
        out_specs=out_specs,
        scratch_shapes=scratch,
        compiler_params=pltpu.CompilerParams(vmem_limit_bytes=48 * 2**20),
        cost_estimate=pl.CostEstimate(flops=4000 << 20, bytes_accessed=2**10, transcendentals=0),
    )(*operands)


def middle_grad_kernel(middle_ref, grad_out_ref, gain_ref, w_ref, *refs):
    *parts, grads_ref, branch_ref, merged_ref, gain_out_ref = refs
    middle = middle_ref[...]
    inverse = lax.rsqrt(jnp.mean(middle * middle, axis=-1, keepdims=True) + epsilon)
    unit = middle * inverse
    grads = total([part[...] for part in parts])
    gain_out_ref[...] = jnp.sum(grads * unit, axis=0, keepdims=True)
    grads = grads * gain_ref[...]
    mean = jnp.mean(grads * unit, axis=-1, keepdims=True)
    grads = grad_out_ref[...].astype(wide) + inverse * (grads - unit * mean)
    grads_ref[...] = grads
    branch = grads.astype(low)
    branch_ref[...] = branch
    merged_ref[...] = dot_t(branch, w_ref[...]).astype(low)


def middle_grad(middle, grad_out, gain, w, parts):
    return pl.pallas_call(
        middle_grad_kernel,
        out_shape=(
            jax.ShapeDtypeStruct(middle.shape, wide),
            jax.ShapeDtypeStruct(middle.shape, low),
            jax.ShapeDtypeStruct((middle.shape[0], w.shape[0]), low),
            jax.ShapeDtypeStruct((1, middle.shape[1]), wide),
        ),
        cost_estimate=pl.CostEstimate(flops=1 << 20, bytes_accessed=2**10, transcendentals=0),
    )(middle, grad_out, gain, w, *parts)


def feed_kernel(units, tokens_ref, grads_ref, w_ref, hidden_ref, grad_units_ref, up_ref, down_ref):
    gate_up = dot(tokens_ref[...], w_ref[:, : 2 * units])
    count = grads_ref.shape[0] * grads_ref.shape[1]
    grad_hidden = dot(grads_ref[...].reshape(count, -1), w_ref[:, 2 * units :])
    gate_values, up_values = gate_up[:, :units], gate_up[:, units:]
    sigmoid_gate = jax.nn.sigmoid(gate_values)
    activated = gate_values * sigmoid_gate
    hidden_ref[...] = (activated * up_values).astype(low)
    slope = sigmoid_gate + activated * (1.0 - sigmoid_gate)
    grad_units_ref[:, :units] = (grad_hidden * up_values * slope).astype(low)
    grad_units_ref[:, units:] = (grad_hidden * activated).astype(low)
    up_ref[...] = dot_t(grad_units_ref[...], w_ref[:, : 2 * units]).astype(low)
    down_ref[...] = dot_t(hidden_ref[...], w_ref[:, 2 * units :]).astype(low)


def feed(tokens, grads, w):
    count, width = tokens.shape
    rows = count // grads.shape[0]
    units = w.shape[1] // 3
    step = min(count, 256)
    return pl.pallas_call(
        functools.partial(feed_kernel, units),
        grid=(count // step,),
        out_shape=(
            jax.ShapeDtypeStruct((count, units), low),
            jax.ShapeDtypeStruct((count, 2 * units), low),
            jax.ShapeDtypeStruct((count, width), low),
            jax.ShapeDtypeStruct((count, width), low),
        ),
        in_specs=[
            pl.BlockSpec((step, width), lambda i: (i, 0)),
            pl.BlockSpec((step // rows, rows, width), lambda i: (i, 0, 0)),
            pl.BlockSpec(memory_space=pltpu.VMEM),
        ],
        out_specs=(
            pl.BlockSpec((step, units), lambda i: (i, 0)),
            pl.BlockSpec((step, 2 * units), lambda i: (i, 0)),
            pl.BlockSpec((step, width), lambda i: (i, 0)),
            pl.BlockSpec((step, width), lambda i: (i, 0)),
        ),
        compiler_params=pltpu.CompilerParams(vmem_limit_bytes=40 * 2**20),
        cost_estimate=pl.CostEstimate(
            flops=5000 << 20, bytes_accessed=2**10, transcendentals=0
        ),
    )(tokens, grads, w)


def feed_grad_kernel(units, *refs):
    *parts, out_ref = refs
    results = [0.0, 0.0]
    for tokens_ref, grads_ref, hidden_ref, grad_units_ref in (parts[:4], parts[4:]):
        grads = grads_ref[...]
        grads = grads.reshape(grads.shape[0] * grads.shape[1], -1)
        results[0] += t_dot(tokens_ref[...], grad_units_ref[...])
        results[1] += t_dot(grads, hidden_ref[...])
    out_ref[:, : 2 * units] = results[0].astype(low)
    out_ref[:, 2 * units :] = results[1].astype(low)


def feed_grad(near, far):
    tokens, grads, hidden, _ = near
    count, width = tokens.shape
    rows = count // grads.shape[0]
    units = hidden.shape[1]
    step = min(width, 256)
    whole = pl.BlockSpec(memory_space=pltpu.VMEM)
    part = [
        pl.BlockSpec((count, step), lambda i: (0, i)),
        pl.BlockSpec((grads.shape[0], rows, step), lambda i: (0, 0, i)),
        whole,
        whole,
    ]
    return pl.pallas_call(
        functools.partial(feed_grad_kernel, units),
        grid=(width // step,),
        out_shape=jax.ShapeDtypeStruct((width, 3 * units), low),
        in_specs=part + part,
        out_specs=pl.BlockSpec((step, 3 * units), lambda i: (i, 0)),
        compiler_params=pltpu.CompilerParams(vmem_limit_bytes=40 * 2**20),
        cost_estimate=pl.CostEstimate(
            flops=5000 << 20, bytes_accessed=2**10, transcendentals=0
        ),
    )(*near, *far)


def finish_input_kernel(tokens_ref, upstream_ref, grads_ref, out_ref):
    tokens = tokens_ref[...].astype(wide)
    upstream = upstream_ref[...].astype(wide)
    inverse = lax.rsqrt(jnp.mean(tokens * tokens, axis=-1, keepdims=True) + epsilon)
    unit = tokens * inverse
    mean = jnp.mean(upstream * unit, axis=-1, keepdims=True)
    out_ref[...] = (grads_ref[...] + inverse * (upstream - unit * mean)).astype(low)


def finish_input(tokens, upstream, grads):
    return pl.pallas_call(
        finish_input_kernel,
        out_shape=jax.ShapeDtypeStruct(tokens.shape, low),
        cost_estimate=pl.CostEstimate(flops=3000 << 20, bytes_accessed=2**20, transcendentals=0),
    )(tokens, upstream, grads)


def extra_rows(first, second):
    shape = (16, first.shape[1])
    row = lax.broadcasted_iota(jnp.int32, shape, 0)
    result = jnp.zeros(shape, wide)
    for i, value in enumerate((first, second)):
        high = value.astype(low).astype(wide)
        result = jnp.where(row == 2 * i, high, jnp.where(row == 2 * i + 1, value - high, result))
    return result.astype(low)


def moved(row, shift):
    rows = jnp.broadcast_to(row, (8, row.shape[1]))
    return pltpu.roll(rows, lax.rem(shift + row.shape[1], row.shape[1]), 1)[:1]


def first_lanes(row, count):
    return jnp.where(lax.broadcasted_iota(jnp.int32, row.shape, 1) < count, row, 0.0)


def qkv_sum_kernel(z_size, z_ref, *refs):
    *parts, out_ref, sum_ref = refs
    sum_ref[...] = total([part[...] for part in parts])
    count = (sum_ref.shape[0] - 16) // z_size
    extra = sum_ref[sum_ref.shape[0] - 16 :, :]
    bias, gain = extra[0:1] + extra[1:2], extra[2:3] + extra[3:4]
    for d in range(z_size):
        z = jnp.bitwise_xor(z_ref[0], d)
        out_ref[d, :count, :] = sum_ref[pl.ds(pl.multiple_of(z * count, count), count), :].astype(low)
        out_ref[d, count:, :] = extra_rows(bias, first_lanes(moved(gain, -z * count), count))


def qkv_sum(z, z_size, parts):
    rows, columns = parts[0].shape
    vmem = pl.BlockSpec(memory_space=pltpu.VMEM)
    return pl.pallas_call(
        functools.partial(qkv_sum_kernel, z_size),
        out_shape=jax.ShapeDtypeStruct((z_size, (rows - 16) // z_size + 16, columns), low),
        in_specs=[pl.BlockSpec(memory_space=pltpu.SMEM)] + [vmem] * len(parts),
        out_specs=vmem,
        scratch_shapes=[pltpu.VMEM((rows, columns), wide)],
        cost_estimate=pl.CostEstimate(flops=2**20, bytes_accessed=2**10, transcendentals=0),
    )(z.reshape(1).astype(jnp.int32), *parts)


def qkv_pack_kernel(biases, c_ref, *refs):
    *parts, own_ref, sent_ref, extra_ref = refs
    share = own_ref.shape[1]
    c = c_ref[0]
    bias, gain = 0.0, 0.0
    for d, part in enumerate(parts):
        own_ref[d] = part[pl.ds(pl.multiple_of(c * share, share), share), :]
        sent_ref[d * share : (d + 1) * share, :] = part[pl.ds(pl.multiple_of((1 - c) * share, share), share), :]
        extra = part[2 * share :, :].astype(wide)
        bias += moved(first_lanes(extra[0:1] + extra[1:2], biases), d * biases)
        gain += first_lanes(extra[2:3] + extra[3:4], 2 * share)
    gain_sent = first_lanes(moved(gain, -(1 - c) * share), share)
    sent_ref[len(parts) * share :, :] = extra_rows(bias, gain_sent)
    row = lax.broadcasted_iota(jnp.int32, extra_ref.shape, 0)
    gain_own = first_lanes(moved(gain, -c * share), share)
    extra_ref[...] = jnp.where(row == 0, bias, jnp.where(row == 1, gain_own, 0.0))


def qkv_pack(c, share, biases, parts):
    columns = parts[0].shape[1]
    vmem = pl.BlockSpec(memory_space=pltpu.VMEM)
    return pl.pallas_call(
        functools.partial(qkv_pack_kernel, biases),
        out_shape=(
            jax.ShapeDtypeStruct((len(parts), share, columns), low),
            jax.ShapeDtypeStruct((len(parts) * share + 16, columns), low),
            jax.ShapeDtypeStruct((8, columns), wide),
        ),
        in_specs=[pl.BlockSpec(memory_space=pltpu.SMEM)] + [vmem] * len(parts),
        out_specs=(vmem, vmem, vmem),
        cost_estimate=pl.CostEstimate(flops=2**20, bytes_accessed=2**10, transcendentals=0),
    )(c.reshape(1).astype(jnp.int32), *parts)


def finish_qkv_kernel(
    biases, group_ref, own_ref, got_ref, extra_ref, w_ref, gain_ref, out_ref, gain_out_ref, gain_two_ref, bias_ref
):
    count, share, _ = own_ref.shape
    low_half = lane_ids(share) < half_lanes
    gain = gain_ref[...].astype(wide)
    summed = jnp.zeros((share, lanes), wide)
    extra = got_ref[count * share :, :].astype(wide)
    bias_rows = extra_ref[0:1, :], extra[0:1] + extra[1:2]
    bias = jnp.zeros((1, bias_rows[0].shape[1]), wide)
    lane = lax.broadcasted_iota(jnp.int32, bias.shape, 1)
    for i in range(2 * count):
        d, e = i // 2, i % 2
        place = jnp.bitwise_xor(group_ref[0], i)
        parts = []
        for j in range(3):
            columns = slice(j * lanes, (j + 1) * lanes)
            part = got_ref[d * share : (d + 1) * share, columns] if e else own_ref[d, :, columns]
            parts.append(part.astype(wide))
        query, key, value = parts
        key = pltpu.roll(key, half_lanes, 1)
        parts = (
            jnp.where(low_half, query, key),
            jnp.where(low_half, value, query),
            jnp.where(low_half, key, value),
        )
        for j, part in enumerate(parts):
            at = pl.ds(pl.multiple_of(place * (3 * lanes) + j * lanes, lanes), lanes)
            summed += part * w_ref[:, at].astype(wide)
            out_ref[:, at] = part * gain
        here = (lane >= place * biases) & (lane < (place + 1) * biases)
        bias = jnp.where(here, moved(bias_rows[e], place * biases - d * biases), bias)
    column = jnp.broadcast_to(jnp.sum(summed, axis=1, keepdims=True), (share, lanes))
    gain_out_ref[...] = jnp.transpose(column)[:1, :]
    gain_two_ref[...] = (extra_ref[1:2, :] + extra[2:3] + extra[3:4])[:, :lanes]
    bias_ref[...] = bias[:, :lanes]


def finish_qkv(biases, group, own, got, extra, w, gain):
    vmem = pl.BlockSpec(memory_space=pltpu.VMEM)
    share = w.shape[0]
    return pl.pallas_call(
        functools.partial(finish_qkv_kernel, biases),
        out_shape=(
            jax.ShapeDtypeStruct(w.shape, wide),
            jax.ShapeDtypeStruct((1, share), wide),
            jax.ShapeDtypeStruct((1, lanes), wide),
            jax.ShapeDtypeStruct((1, lanes), wide),
        ),
        in_specs=[pl.BlockSpec(memory_space=pltpu.SMEM)] + [vmem] * 5,
        out_specs=(vmem,) * 4,
        cost_estimate=pl.CostEstimate(flops=3000 << 20, bytes_accessed=2**20, transcendentals=0),
    )(group.reshape(1).astype(jnp.int32), own, got, extra, w, gain)


def finish_feed_kernel(x_ref, both_ref, other_ref, gate_ref, up_ref, down_ref):
    depth, units = other_ref.shape[0], other_ref.shape[1] // 3
    mine = pl.ds(pl.multiple_of(x_ref[0] * depth, depth), depth)
    for value, x in ((both_ref[mine, :], x_ref[0]), (other_ref[...], 1 - x_ref[0])):
        at = pl.ds(pl.multiple_of(x * units, units), units)
        parts = [value[:, j * units : (j + 1) * units].astype(wide) for j in range(3)]
        gate_ref[:, at], up_ref[:, at] = parts[:2]
        if down_ref.shape[0] == 2 * units:
            down_ref[at, :] = jnp.transpose(parts[2])
        else:
            down_ref[:, at] = parts[2]


def finish_feed(x, both, other):
    vmem = pl.BlockSpec(memory_space=pltpu.VMEM)
    depth, units = other.shape[0], other.shape[1] // 3
    return pl.pallas_call(
        finish_feed_kernel,
        out_shape=(
            jax.ShapeDtypeStruct((depth, 2 * units), wide),
            jax.ShapeDtypeStruct((depth, 2 * units), wide),
            jax.ShapeDtypeStruct((2 * units, depth) if depth % lanes == 0 else (depth, 2 * units), wide),
        ),
        in_specs=[pl.BlockSpec(memory_space=pltpu.SMEM), vmem, vmem],
        out_specs=(vmem,) * 3,
        cost_estimate=pl.CostEstimate(flops=3000 << 20, bytes_accessed=2**20, transcendentals=0),
    )(x.reshape(1).astype(jnp.int32), both, other)


def rope_tables(stamps, dimension):
    halfway = dimension // 2
    frequency = jnp.exp(-math.log(10000.0) * jnp.arange(halfway, dtype=wide) / halfway)
    repeated = jnp.tile(frequency, lanes // halfway)
    angles = stamps.astype(wide)[:, None] * repeated[None, :]
    sign = jnp.where(jnp.arange(lanes) % dimension < halfway, -1.0, 1.0)
    return (jnp.cos(angles), jnp.sin(angles) * sign[None, :])


def shards(
    inputs,
    gain_attn,
    w_qkv,
    head_bias,
    w_out,
    gain_ffn,
    w_gate,
    w_up,
    w_down,
    time_ids,
    variate_ids,
    seq_ids,
    cotangent,
):
    at = Place()
    z_size, y_size = at.z_size, at.y_size
    tokens = inputs[0].astype(wide)
    rows, width = tokens.shape
    head_count = head_bias.shape[0]
    head_dim = width // head_count
    groups = at.seq_size
    heads = head_count // groups
    group_width = heads * head_dim
    padded = (heads + 1) // 2 * lanes
    share = width // (at.seq_size * at.head_size)
    group = 2 * at.z + at.c
    window = 2 * at.y + at.x
    device_id = at.seq * at.head_size + at.head

    inverse_one = lax.rsqrt(jnp.mean(tokens * tokens, axis=-1, keepdims=True) + epsilon)
    unit = tokens * inverse_one
    turned = called("tokens_turn", at.turn, unit.astype(low))

    depth, units = w_gate.shape[0], w_gate.shape[1] // 2
    gain_one = gain_attn.astype(wide)[:, None]
    scaled = (w_qkv.astype(wide) * gain_one).astype(low)

    def to_parts(columns):
        parts = columns.reshape(-1, groups, heads, 3, head_dim).transpose(0, 1, 3, 2, 4)
        parts = parts.reshape(-1, groups, 3, group_width)
        parts = jnp.pad(parts, ((0, 0), (0, 0), (0, 0), (0, padded - group_width)))
        return parts.reshape(-1, groups, 3 * padded)

    parts = to_parts(scaled).reshape(share, z_size, 2, 3 * padded)
    core_own = pick(at.c, parts[:, :, 0], parts[:, :, 1])
    core_sent = pick(at.c, parts[:, :, 1], parts[:, :, 0]).reshape(-1, 3 * padded)

    def with_extra(block, *values):
        extra = jnp.stack([jnp.pad(v.astype(low), (0, 3 * padded - v.shape[0])) for v in values])
        return jnp.concatenate([block, jnp.pad(extra, ((0, 16 - len(values)), (0, 0)))], axis=0)

    core_got = called("qkv_core", at.along_c, with_extra(core_sent, gain_ffn))
    both = jnp.stack([core_own, core_got[:-16].reshape(core_own.shape)])
    out_z = called("out_z", at.gather_steps, w_out, at.z_moves()).reshape(-1, width)
    gains = jnp.concatenate([gain_ffn, core_got[-16, :share]])
    sent = []
    for d in range(z_size):
        block = lax.dynamic_index_in_dim(both, jnp.bitwise_xor(at.z, d), axis=2, keepdims=False)
        sent.append(with_extra(block.reshape(-1, 3 * padded), gains))
    by_z = jnp.stack(called("qkv_z", at.scatter_z, sent))
    gains = by_z[:, -16, : 2 * share].reshape(-1)
    by_z = by_z[:, :-16].reshape(-1, 3 * padded)
    late_gate, late_up, late_down = w_gate, w_up, w_down
    by_z, late_gate, late_up, late_down = tied(by_z, w_gate, w_up, w_down)
    units = w_gate.shape[1] // 2
    down_t = with_layout_constraint(late_down.T, Layout(major_to_minor=(0, 1)))
    firsts = jnp.concatenate([v[:, :units] for v in (late_gate, late_up, down_t)], axis=1)
    seconds = jnp.concatenate([v[:, units:] for v in (late_gate, late_up, down_t)], axis=1)
    mine = pick(at.x, firsts, seconds)
    other = called("ffn_x", at.along_x, pick(at.x, seconds, firsts))
    z_block = jnp.concatenate([pick(at.x, mine, other), pick(at.x, other, mine)], axis=0)

    z_early = z_block
    near = called("tokens_z", at.gather_steps, turned, at.z_moves()[:-1])
    near = near
    near = join(near, called("tokens_z", at.z_moves()[-1], near)).reshape(-1, width)
    by_xy = jnp.stack(called("qkv_xy", at.gather_xy, with_extra(by_z, gains)))
    gains = by_xy[:, -16, : gains.shape[0]].reshape(y_size, 2, z_size, 2, share)
    gains = gains.transpose(2, 1, 0, 3, 4).reshape(-1, share)
    by_xy = by_xy[:, :-16]
    devices = jnp.arange(at.seq_size * at.head_size)
    from_device = (devices[None, :] == jnp.bitwise_xor(devices[:, None], device_id)).astype(low)
    gain_two = dot(from_device, gains).reshape(1, width)
    masks = [
        (2 * d + dx) * at.head_size + 2 * dy + e
        for dx, dy in at.pairs()
        for d in range(z_size)
        for e in range(2)
    ]
    w_heads = place(by_xy.reshape(-1, share, 3 * padded), device_id, masks).reshape(width, 3 * padded)

    out_xy = called("out_xy", at.gather_steps, out_z, at.xy_moves())

    grad_out = cotangent[0]
    grad_out_near = called("cotangent_x", at.gather_steps, grad_out, at.xy_moves()[:1])

    near, w_heads = tied(near, w_heads)
    near, out_xy = tied(near, out_xy)
    near, grad_out_near = tied(near, grad_out_near)
    w_ffn = lax.all_gather(z_block, "seq", axis=0, tiled=True, axis_index_groups=at.columns_z())

    time_ids, variate_ids, seq_ids, by_z = tied(time_ids, variate_ids, seq_ids, by_z)

    def of_window(ids):
        row = lax.dynamic_index_in_dim(ids, window, axis=0, keepdims=False).reshape(z_size, 2, rows)
        order = [
            lax.dynamic_slice(
                row, (jnp.bitwise_xor(at.z, d), jnp.bitwise_xor(at.c, e), 0), (1, 1, rows)
            ).reshape(rows)
            for e in range(2)
            for d in at.z_order()
        ]
        return jnp.concatenate(order)

    ids = (of_window(variate_ids).reshape(1, -1), of_window(seq_ids).reshape(1, -1))
    cosine, sine = rope_tables(of_window(time_ids), head_dim)
    local_bias = lax.dynamic_slice_in_dim(head_bias, group * heads, heads, 0)
    difference = local_bias[:, 0] - local_bias[:, 1]
    difference_high = difference.astype(low).astype(wide)
    bias = jnp.stack([difference_high, difference - difference_high])

    near, w_heads, cosine, sine, ids = tied(near, w_heads, cosine, sine, ids)
    far = called("tokens_core", at.along_c, near)
    query, key, value, attended = attend(bias, near, far, w_heads, cosine, sine, ids, heads)

    out_far = called("out_core", at.along_c, out_xy)
    out_blocks = jnp.stack([out_xy, out_far]).reshape(-1, share, width)
    out_masks = [
        (dx * z_size + d) * at.head_size + 2 * dy + e
        for e in range(2)
        for dx, dy in at.pairs()
        for d in range(z_size)
    ]
    out_rows = place(out_blocks, at.head, out_masks).reshape(width, width)

    sent = attended[:, :group_width].reshape(2, z_size, rows, group_width)
    places = {d: i for i, d in enumerate(at.z_order())}
    received = called("attended_z", at.scatter_z, [sent[:, places[d]] for d in range(z_size)])
    received = [received[d] for d in at.z_order()]
    kept = jnp.concatenate([block[0] for block in received], axis=1)
    passed = jnp.concatenate([block[1] for block in received], axis=1)
    held = grad_out_near[None]
    for move in at.xy_moves()[1:]:
        got = called("cotangent_y", move, held)
        got, passed = tied(got, passed)
        held = jnp.concatenate([held, got], axis=0)
    grad_out_near = held.reshape(2 * y_size, rows, width)
    grad_out_far = called("cotangent_core", at.along_c, grad_out_near)

    passed = called("attended_core", at.along_c, passed)

    merged = called("attended_turn", at.turn, jnp.concatenate([kept, passed], axis=1))

    middle = tokens + dot(merged, out_rows)
    inverse_two = lax.rsqrt(jnp.mean(middle * middle, axis=-1, keepdims=True) + epsilon)
    unit_two = middle * inverse_two
    normed_two = (unit_two * gain_two).astype(low)
    normed_near = jnp.concatenate(called("normed_xy", at.gather_xy, normed_two), axis=0)
    normed_far = called("normed_core", at.along_c, normed_near)

    hidden_far, units_far, up_far, down_far = feed(normed_far, grad_out_far, w_ffn)
    hidden_near, units_near, up_near, down_near = feed(normed_near, grad_out_near, w_ffn)

    blocks = (2 * y_size, rows, width)
    up = up_near.reshape(blocks), called("up_core", at.along_c, up_far).reshape(blocks)
    kept = [total([part[i] for part in up]).astype(low) for i in range(2 * y_size)]
    grad_w_ffn = feed_grad(
        (normed_near, grad_out_near, hidden_near, units_near),
        (normed_far, grad_out_far, hidden_far, units_far),
    )
    received = called("up_xy", at.scatter_xy, kept)
    down = [down_near.reshape(blocks), called("down_core", at.along_c, down_far).reshape(blocks)]
    moves = at.xy_moves()
    y_cut = y_size // 2
    down = [part.reshape(y_size, 2, rows, width) for part in down]
    down_sent = total([part[y_cut:] for part in down]).astype(low)
    received[0], down_sent = tied(received[0], down_sent)
    down = [part[:y_cut] for part in down] + [called("down_y", moves[-1], down_sent)]
    *received[1:], grad_w_ffn = tied(*received[1:], grad_w_ffn)
    grad_middle, grad_branch, grad_merged, gain_part = middle_grad(middle, grad_out, gain_two, out_rows, received)

    turned_back = called("merged_turn", at.turn, grad_merged)
    grad_w_ffn = lax.psum_scatter(
        grad_w_ffn, "seq", scatter_dimension=0, tiled=True, axis_index_groups=at.columns_z()
    )
    cut = width // 2
    kept, passed = turned_back[:, :cut], called("merged_core", at.along_c, turned_back[:, cut:])
    merged, grad_branch, passed = tied(merged, grad_branch, passed)
    sent = []
    for d in range(z_size):
        columns = slice(places[d] * group_width, (places[d] + 1) * group_width)
        sent.append(jnp.stack([part[:, columns] for part in (kept, passed)]))
    received_z = called("merged_z", at.scatter_z, sent)
    received_one = received_z[1]

    grad_out_rows = t_dot(merged, grad_branch).astype(low)
    grad_out_rows = fetch(grad_out_rows.reshape(-1, share, width), at.head, out_masks)
    grad_out_rows = grad_out_rows.reshape(2, y_size, 2, z_size * share, width)
    out_parts = [grad_out_rows[0], called("w_out_core", at.along_c, grad_out_rows[1])]
    out_sent = total([part[y_cut:] for part in out_parts]).astype(low)
    received_one, out_sent = tied(received_one, out_sent)
    received_z[1] = received_one
    received = jnp.stack([received_z[d] for d in at.z_order()], axis=1)
    grad_attended = received.reshape(2 * z_size * rows, group_width)
    if padded > group_width:
        grad_attended = jnp.pad(grad_attended, ((0, 0), (0, padded - group_width)))
    down = called("down_y", at.scatter_steps, down, moves[1:-1])
    down = [part.reshape(2, rows, width) for part in down]
    down_sent = total([part[1] for part in down]).astype(low)
    down = [part[0] for part in down] + [called("down_x", moves[0], down_sent)]
    grad_attended, out_sent = tied(grad_attended, out_sent)
    grad_attended, down[-1] = tied(grad_attended, down[-1])
    out_got = called("w_out_y", moves[-1], out_sent)
    out_parts = [part[:y_cut] for part in out_parts] + [out_got]

    def halves(values):
        high = values.astype(low)
        return high, (values - high.astype(wide)).astype(low)

    gain_part = gain_part.reshape(z_size, 2, y_size, 2, share)
    bias_count, gain_count = 2 * heads, 2 * z_size * share
    extra, device_masks = [], []
    for dx, dy in at.pairs():
        x, y = jnp.bitwise_xor(at.x, dx), jnp.bitwise_xor(at.y, dy)
        gain = lax.dynamic_slice(gain_part, (0, x, y, 0, 0), (z_size, 1, 1, 2, share)).reshape(-1)
        none = jnp.zeros((0, 3 * padded), low)
        extra.append(with_extra(none, *(jnp.zeros_like(v) for v in halves(gain)), *halves(gain)))
        device_masks.append([
            (2 * d + dx) * at.head_size + 2 * dy + e for d in range(z_size) for e in range(2)
        ])
    extra = jnp.stack(extra)
    place_xy = at.x * at.head_size + 2 * at.y
    in_kernel = share % 16 == 0
    upstream_near, upstream_far, grad_packed, bias_grad, *messages = attend_grad(
        query, key, value, attended, grad_attended, cosine, sine, ids, w_heads,
        near, far, extra, place_xy, device_masks if in_kernel else None,
    )
    half = near.shape[0]
    if in_kernel:
        messages = [messages[0][i] for i in range(2 * y_size)]
    else:
        grad_heads = t_dot(near, grad_packed[:half]) + t_dot(far, grad_packed[half:])
        grad_heads = grad_heads.astype(low).reshape(-1, share, 3 * padded)
        none = jnp.zeros((0, 3 * padded), low)
        biases = with_extra(none, *halves(bias_grad.reshape(-1)))
        messages = [
            jnp.concatenate([
                lax.dynamic_index_in_dim(grad_heads, jnp.bitwise_xor(place_xy, mask), 0, False)
                for mask in masks
            ] + [extra[i] + biases])
            for i, masks in enumerate(device_masks)
        ]

    upstream_far, out_parts[-1] = tied(upstream_far, out_parts[-1])
    upstream_far = called("input_core", at.along_c, upstream_far)
    z_moves = at.z_moves()
    blocks = (z_size, rows, width)
    upstream_z = [upstream_near.reshape(blocks), upstream_far.reshape(blocks)]
    z_cut = z_size // 2
    upstream_sent = total([part[z_cut:] for part in upstream_z]).astype(low)
    upstream_z = [part[:z_cut] for part in upstream_z] + [called("input_z", z_moves[-1], upstream_sent)]

    out_parts = called("w_out_y", at.scatter_steps, out_parts, moves[1:-1])
    out_parts = [part.reshape(2, -1, width) for part in out_parts]
    out_parts = called("w_out_x", at.scatter_steps, out_parts, moves[:1])
    out_parts[-1] = out_parts[-1]

    def joined(block, row, count):
        return block[row, :count].astype(wide) + block[row + 1, :count].astype(wide)

    received = called("grad_qkv_xy", at.scatter_xy, messages)
    fast = in_kernel and heads == 2 and head_dim == half_lanes
    if fast:
        sent = qkv_sum(at.z, z_size, received)
    else:
        summed = total(received)
        bias_sum = joined(summed[-16:], 0, bias_count)
        gain_sum = joined(summed[-16:], 2, gain_count).reshape(z_size, 2 * share)
        summed = summed[:-16].astype(low).reshape(z_size, 2 * share, 3 * padded)
        sent = []
        for d in range(z_size):
            block, gain = (
                lax.dynamic_index_in_dim(v, jnp.bitwise_xor(at.z, d), axis=0, keepdims=False)
                for v in (summed, gain_sum)
            )
            sent.append(with_extra(block, *halves(bias_sum), *halves(gain)))
    depth = grad_w_ffn.shape[0] // 2
    other = lax.dynamic_slice_in_dim(grad_w_ffn, (1 - at.x) * depth, depth, 0)
    other = called("grad_ffn_x", at.along_x, other)
    upstream_z[-1], other = tied(upstream_z[-1], other)
    upstream_z[-1], sent = tied(upstream_z[-1], sent)
    z_cut = z_cut // 2
    upstream_sent = total([part[z_cut:] for part in upstream_z]).astype(low)
    upstream_sent, sent = tied(upstream_sent, sent)
    upstream_z = [part[:z_cut] for part in upstream_z] + [called("input_z", z_moves[-2], upstream_sent)]
    grad_w_gate, grad_w_up, grad_w_down = finish_feed(at.x, grad_w_ffn, other)
    if grad_w_down.shape != w_down.shape:
        grad_w_down = grad_w_down.T
    upstream_z[-1] = after(upstream_z[-1], grad_w_gate)
    upstream_one = total(called("input_z", at.scatter_steps, upstream_z, z_moves[:-2]))[0]
    out_parts[-1] = out_parts[-1]
    output = middle + total(down)
    out_parts = [part.reshape(z_size, share, width) for part in out_parts]
    grad_w_out = total(called("w_out_z", at.scatter_steps, out_parts, z_moves))[0]
    received = called("grad_qkv_z", at.scatter_z, [sent[d] for d in range(z_size)])
    upstream_one, received[0] = tied(upstream_one, received[0])
    if fast:
        core_own, core_sent, extra_own = qkv_pack(at.c, share, bias_count, received)
    else:
        bias_z = jnp.concatenate([joined(block[-16:], 0, bias_count) for block in received])
        gain_sum = functools.reduce(jnp.add, [joined(block[-16:], 2, 2 * share) for block in received])
        received = jnp.stack([block[:-16] for block in received]).reshape(z_size, 2, share, 3 * padded)
        core_own = pick(at.c, received[:, 0], received[:, 1])
        core_sent = pick(at.c, received[:, 1], received[:, 0]).reshape(-1, 3 * padded)
        gain_own = pick(at.c, gain_sum[:share], gain_sum[share:])
        gain_sent = pick(at.c, gain_sum[share:], gain_sum[:share])
        core_sent = with_extra(core_sent, *halves(bias_z), *halves(gain_sent))
    upstream_one = upstream_one.astype(low)
    core_sent = core_sent
    upstream_one = called("input_turn", at.turn, upstream_one)
    grad_input = finish_input(inputs[0], upstream_one, grad_middle)
    core_got = called("grad_qkv_core", at.along_c, core_sent)
    if fast:
        grad_w_qkv, grad_gain_attn, grad_gain_ffn, full_bias = finish_qkv(
            bias_count, group, core_own, core_got, extra_own, w_qkv, gain_attn[:, None]
        )
        grad_gain_attn, grad_gain_ffn = grad_gain_attn[0], grad_gain_ffn[0, :share]
        full_bias = full_bias[0, : 2 * head_count].reshape(head_count, 2)
    else:
        core_other = core_got[:-16].reshape(z_size, share, 3 * padded)
        grad_gain_ffn = gain_own + joined(core_got[-16:], 2, share)
        biases = jnp.stack([bias_z, joined(core_got[-16:], 0, z_size * bias_count)])
        biases = list(biases.reshape(2, z_size, heads, 2).transpose(1, 0, 2, 3).reshape(groups, heads, 2))
        full_bias = jnp.concatenate(xor_list(biases, group), axis=0)
        by_group = jnp.stack([core_own, core_other], axis=1).reshape(groups, share, 3 * padded)
        by_group = place(by_group, group, list(range(groups))).astype(wide).reshape(groups, share, 3, padded)
        by_group = by_group[..., :group_width].reshape(groups, share, 3, heads, head_dim)
        raw = by_group.transpose(1, 0, 3, 2, 4).reshape(share, 3 * width)
        grad_w_qkv = raw * gain_one
        grad_gain_attn = jnp.sum(raw * w_qkv.astype(wide), axis=1)

    return (
        output.astype(low).reshape(1, rows, width),
        grad_input.reshape(1, rows, width),
        grad_gain_attn,
        grad_w_qkv,
        full_bias,
        grad_w_out,
        grad_gain_ffn,
        grad_w_gate,
        grad_w_up,
        grad_w_down,
    )


def solution(mesh):
    placed = (
        P("head", "seq", None),
        P(("seq", "head")),
        P(("seq", "head"), None),
        P(),
        P(("seq", "head"), None),
        P(("seq", "head")),
        P("seq", "head"),
        P("seq", "head"),
        P("head", "seq"),
        P(),
        P(),
        P(),
        P("head", "seq", None),
    )
    return jax.shard_map(
        shards,
        mesh=mesh,
        in_specs=placed,
        out_specs=(
            P("head", "seq", None),
            P("head", "seq", None),
            P(("seq", "head")),
            P(("seq", "head"), None),
            P(),
            P(("seq", "head"), None),
            P(("seq", "head")),
            P("seq", "head"),
            P("seq", "head"),
            P("head", "seq"),
        ),
        check_vma=False,
    )
```

```python
import functools
import math

import jax
import jax.numpy as jnp
from jax import lax
from jax.experimental import pallas as pl
from jax.experimental.layout import Layout, with_layout_constraint
from jax.experimental.pallas import tpu as pltpu
from jax.sharding import PartitionSpec as P


epsilon = 1e-05
masked_score = -1e30
low = jnp.bfloat16
wide = jnp.float32
lanes = 128
half_lanes = 64


def dot(a, b):
    return jnp.dot(a, b, preferred_element_type=wide)


def dot_t(a, b):
    return lax.dot_general(a, b, (((1,), (1,)), ((), ())), preferred_element_type=wide)


def t_dot(a, b):
    return lax.dot_general(a, b, (((0,), (0,)), ((), ())), preferred_element_type=wide)


class Place:
    def __init__(self):
        self.seq_size = lax.axis_size("seq")
        self.head_size = lax.axis_size("head")
        self.z_size = self.seq_size // 2
        self.y_size = self.head_size // 2
        self.seq = lax.axis_index("seq")
        self.head = lax.axis_index("head")
        self.z, self.x = self.seq // 2, self.seq % 2
        self.y, self.c = self.head // 2, self.head % 2

    def along_z(self, value, step):
        return lax.ppermute(value, "seq", [(i, i ^ (2 * step)) for i in range(self.seq_size)])

    def along_x(self, value):
        return lax.ppermute(value, "seq", [(i, i ^ 1) for i in range(self.seq_size)])

    def along_c(self, value):
        return lax.ppermute(value, "head", [(i, i ^ 1) for i in range(self.head_size)])

    def along_xy(self, value, dx, dy):
        if dy == 0:
            return self.along_x(value)
        if dx == 0:
            return lax.ppermute(
                value, "head", [(i, i ^ (2 * dy)) for i in range(self.head_size)]
            )
        return lax.ppermute(
            value,
            ("seq", "head"),
            [
                (s * self.head_size + h, (s ^ dx) * self.head_size + (h ^ (2 * dy)))
                for s in range(self.seq_size)
                for h in range(self.head_size)
            ],
        )

    def turn(self, value):
        return lax.ppermute(
            value,
            ("seq", "head"),
            [
                (s * self.head_size + h, ((s & ~1) | (h & 1)) * self.head_size + ((h & ~1) | (s & 1)))
                for s in range(self.seq_size)
                for h in range(self.head_size)
            ],
        )

    def pairs(self):
        return [(dx, dy) for dy in range(self.y_size) for dx in range(2)]

    def gather_xy(self, value):
        return [value if d == (0, 0) else self.along_xy(value, *d) for d in self.pairs()]

    def scatter_xy(self, blocks):
        return [
            block if d == (0, 0) else self.along_xy(block, *d)
            for d, block in zip(self.pairs(), blocks)
        ]

    def columns_z(self):
        return [[x + 2 * z for z in range(self.z_size)] for x in range(2)]

    def gather_z(self, value):
        return [value if d == 0 else self.along_z(value, d) for d in range(self.z_size)]

    def scatter_z(self, blocks):
        return [block if d == 0 else self.along_z(block, d) for d, block in enumerate(blocks)]

    def gather_steps(self, value, moves):
        held = value[None]
        for move in moves:
            held = jnp.concatenate([held, move(held)], axis=0)
        return held

    def scatter_steps(self, addends, moves):
        for move in reversed(moves):
            cut = addends[0].shape[0] // 2
            received = move(total([value[cut:] for value in addends]).astype(low))
            if len(addends) > 2:
                addends = [total([value[:cut] for value in addends])]
            else:
                addends = [value[:cut] for value in addends]
            addends = addends + [received]
        return addends

    def xy_moves(self):
        steps = [1 << i for i in range(self.y_size.bit_length() - 1)]
        return [self.along_x] + [functools.partial(self.along_xy, dx=0, dy=step) for step in steps]

    def z_moves(self):
        steps = [1 << i for i in reversed(range(self.z_size.bit_length() - 1))]
        return [functools.partial(self.along_z, step=step) for step in steps]

    def z_order(self):
        order = [0]
        for step in [1 << i for i in reversed(range(self.z_size.bit_length() - 1))]:
            order = order + [step ^ d for d in order]
        return order


def called(name, move, *operands):
    with jax.named_scope(name):
        return move(*operands)


def total(addends):
    return functools.reduce(jnp.add, [value.astype(wide) for value in addends])


def after(value, *others):
    return lax.optimization_barrier((value, others))[0]


def tied(*values):
    return lax.optimization_barrier(values)


def pick(bit, zero, one):
    return jnp.where(bit == 0, zero, one)


def xor_list(blocks, me):
    step = 1
    while step < len(blocks):
        on = (me // step) % 2
        blocks = [pick(on, blocks[i], blocks[i ^ step]) for i in range(len(blocks))]
        step *= 2
    return blocks


def place_kernel(masks, me_ref, in_ref, out_ref):
    for i, mask in enumerate(masks):
        out_ref[jnp.bitwise_xor(me_ref[0], mask)] = in_ref[i]


def fetch_kernel(masks, me_ref, in_ref, out_ref):
    for i, mask in enumerate(masks):
        out_ref[i] = in_ref[jnp.bitwise_xor(me_ref[0], mask)]


def move_blocks(kernel, blocks, me, masks):
    return pl.pallas_call(
        functools.partial(kernel, masks),
        out_shape=jax.ShapeDtypeStruct(blocks.shape, blocks.dtype),
        in_specs=[pl.BlockSpec(memory_space=pltpu.SMEM), pl.BlockSpec(memory_space=pltpu.VMEM)],
        out_specs=pl.BlockSpec(memory_space=pltpu.VMEM),
        compiler_params=pltpu.CompilerParams(vmem_limit_bytes=32 * 2**20),
        cost_estimate=pl.CostEstimate(flops=0, bytes_accessed=4 * blocks.size, transcendentals=0),
    )(me.reshape(1).astype(jnp.int32), blocks)


def place(blocks, me, masks):
    return move_blocks(place_kernel, blocks, me, masks)


def fetch(blocks, me, masks):
    return move_blocks(fetch_kernel, blocks, me, masks)


def join_kernel(first_ref, second_ref, out_ref):
    count = first_ref.shape[0]
    out_ref[:count] = first_ref[...]
    out_ref[count:] = second_ref[...]


def join(first, second):
    return pl.pallas_call(
        join_kernel,
        out_shape=jax.ShapeDtypeStruct((2 * first.shape[0],) + first.shape[1:], first.dtype),
        cost_estimate=pl.CostEstimate(flops=1 << 20, bytes_accessed=2**10, transcendentals=0),
    )(first, second)


def lane_ids(rows):
    return lax.broadcasted_iota(jnp.int32, (rows, lanes), 1)


def swap_halves(value):
    first = lane_ids(value.shape[0]) % half_lanes < half_lanes // 2
    return jnp.where(first, pltpu.roll(value, lanes - 32, 1), pltpu.roll(value, 32, 1))


def column_of(row):
    wide_row = jnp.broadcast_to(row.astype(wide), (8, row.shape[1]))
    return jnp.transpose(wide_row)[:, :1].astype(jnp.int32)


def three_pieces(value):
    one = value.astype(low).astype(wide)
    rest = value - one
    two = rest.astype(low).astype(wide)
    return one, two, (rest - two).astype(low).astype(wide)


def attend_kernel(
    heads,
    bias_ref,
    near_ref,
    far_ref,
    w_ref,
    cosine_ref,
    sine_ref,
    kinds_ref,
    docs_ref,
    query_ref,
    key_ref,
    value_ref,
    out_ref,
    docs_column_ref,
):
    rows = near_ref.shape[0]
    docs_column_ref[...] = column_of(docs_ref[...])
    length = 2 * rows
    step = min(rows, 256)
    padded = w_ref.shape[1] // 3
    for part, source in enumerate((near_ref, far_ref)):
        for start in range(0, rows, step):
            at = pl.ds(part * rows + start, step)
            packed = dot(source[start : start + step, :], w_ref[...])
            cosine, sine = cosine_ref[at, :], sine_ref[at, :]
            lane = lane_ids(step)
            kind = column_of(kinds_ref[:, at])
            own = (lane == 64 + kind).astype(wide)
            own_two = (lane == 68 + kind).astype(wide)
            extra_query = ((lane == 72 + kind) | (lane == 76)).astype(wide)
            extra_key = own + own_two + ((lane >= 77) & (lane < 80)).astype(wide)
            extra_value = ((lane >= 64) & (lane < 67)).astype(wide)
            for head in range(heads):
                base = head // 2 * lanes
                query = packed[:, base : base + lanes]
                key = packed[:, padded + base : padded + base + lanes]
                value = packed[:, 2 * padded + base : 2 * padded + base + lanes]
                query = (query * cosine + swap_halves(query) * sine).astype(low).astype(wide) * 0.125
                key = key * cosine + swap_halves(key) * sine
                if head % 2:
                    query, key, value = (pltpu.roll(v, half_lanes, 1) for v in (query, key, value))
                body = lane < half_lanes
                extra = extra_query + own * bias_ref[0, head] + own_two * bias_ref[1, head]
                query_ref[head, at, :] = jnp.where(body, query, extra).astype(low)
                key_ref[head, at, :] = jnp.where(body, key, extra_key).astype(low)
                value_ref[head, at, :] = jnp.where(body, value, extra_value).astype(low)
    block = min(length, 256)
    lane = lane_ids(block)

    @pl.loop(0, length // block)
    def _(i):
        at = pl.ds(pl.multiple_of(i * block, block), block)
        allowed = docs_column_ref[at, :] == docs_ref[...]
        done = []
        for head in range(heads):
            query = query_ref[head, at, :]
            scores = jnp.where(allowed, dot_t(query, key_ref[head]), masked_score)
            top = jnp.max(scores, axis=1, keepdims=True)
            weights = jnp.exp(scores - top).astype(low)
            summed = dot(weights, value_ref[head])
            total = summed[:, half_lanes : half_lanes + 1]
            one, two, three = three_pieces(-(top + jnp.log(total)))
            extra = jnp.where(lane == 77, one, jnp.where(lane == 78, two, jnp.where(lane == 79, three, 0.0)))
            query_ref[head, at, :] = jnp.where(lane < 77, query.astype(wide), extra).astype(low)
            done.append(summed / total)
        for base in range(0, heads, 2):
            both = done[base]
            if base + 1 < heads:
                both = jnp.where(lane < half_lanes, both, pltpu.roll(done[base + 1], half_lanes, 1))
            out_ref[at, base // 2 * lanes : (base // 2 + 1) * lanes] = both.astype(low)


def attend(bias, near, far, w, cosine, sine, ids, heads):
    length = 2 * near.shape[0]
    padded = w.shape[1] // 3
    vmem = pl.BlockSpec(memory_space=pltpu.VMEM)
    whole = jax.ShapeDtypeStruct((heads, length, lanes), low)
    return pl.pallas_call(
        functools.partial(attend_kernel, heads),
        out_shape=(whole, whole, whole, jax.ShapeDtypeStruct((length, padded), low)),
        in_specs=[pl.BlockSpec(memory_space=pltpu.SMEM)] + [vmem] * 7,
        out_specs=(vmem, vmem, vmem, vmem),
        scratch_shapes=[pltpu.VMEM((length, 1), jnp.int32)],
        compiler_params=pltpu.CompilerParams(vmem_limit_bytes=48 * 2**20),
        cost_estimate=pl.CostEstimate(
            flops=1 << 20, bytes_accessed=2**20, transcendentals=0
        ),
    )(bias, near, far, w, cosine, sine, *ids)


def attend_grad_kernel(
    heads,
    masks,
    *refs,
):
    if masks:
        place_ref, near_ref, far_ref, extra_ref, *refs = refs
        *refs, messages_ref, total_ref = refs
    attend_grad_body(heads, *refs)
    if not masks:
        return
    packed_ref, bias_ref = refs[12:14]
    half, width = near_ref.shape
    share = (messages_ref.shape[1] - 16) // len(masks[0])
    for start in range(0, width, 256):
        here = slice(start, start + 256)
        grads = t_dot(near_ref[:, here], packed_ref[:half, :]) + t_dot(far_ref[:, here], packed_ref[half:, :])
        total_ref[here, :] = grads.astype(low)
    columns = packed_ref.shape[1]
    row = lax.broadcasted_iota(jnp.int32, (16, columns), 0)
    lane = lax.broadcasted_iota(jnp.int32, (16, columns), 1)
    biases = jnp.zeros((16, columns), wide)
    for head in range(heads):
        for i in range(2):
            biases = jnp.where(lane == 2 * head + i, bias_ref[head, i], biases)
    high = biases.astype(low).astype(wide)
    biases = jnp.where(row == 0, high, jnp.where(row == 1, biases - high, 0.0))
    for i, part in enumerate(masks):
        for j, mask in enumerate(part):
            start = pl.multiple_of(jnp.bitwise_xor(place_ref[0], mask) * share, share)
            messages_ref[i, j * share : (j + 1) * share, :] = total_ref[pl.ds(start, share), :]
        messages_ref[i, len(part) * share :, :] = (extra_ref[i].astype(wide) + biases).astype(low)


def attend_grad_body(
    heads,
    query_ref,
    key_ref,
    value_ref,
    out_ref,
    grad_out_ref,
    cosine_ref,
    sine_ref,
    kinds_ref,
    docs_ref,
    w_ref,
    near_up_ref,
    far_up_ref,
    packed_ref,
    bias_ref,
    grad_query_ref,
    grad_key_ref,
    grad_value_ref,
    docs_column_ref,
):
    length = query_ref.shape[1]
    docs_column_ref[...] = column_of(docs_ref[...])
    padded = packed_ref.shape[1] // 3
    half = length // 2
    block = min(length, 256)
    lane = lane_ids(block)
    grad_key_ref[...] = jnp.zeros_like(grad_key_ref)
    grad_value_ref[...] = jnp.zeros_like(grad_value_ref)

    @pl.loop(0, length // block)
    def _(i):
        at = pl.ds(pl.multiple_of(i * block, block), block)
        allowed = docs_column_ref[...] == docs_ref[:, at]
        for head in range(heads):
            columns = slice(head // 2 * lanes, (head // 2 + 1) * lanes)
            grad_out = grad_out_ref[at, columns].astype(wide)
            product = grad_out * out_ref[at, columns].astype(wide)
            mine = (lane >= half_lanes) if head % 2 else (lane < half_lanes)
            row_dot = jnp.sum(jnp.where(mine, product, 0.0), axis=1, keepdims=True)
            one, two, three = three_pieces(-row_dot)
            if head % 2:
                grad_out = pltpu.roll(grad_out, half_lanes, 1)
            extra = jnp.where(lane == 64, one, jnp.where(lane == 65, two, jnp.where(lane == 66, three, 0.0)))
            grad_out = jnp.where(lane < half_lanes, grad_out, extra).astype(low)
            query, key = query_ref[head, at, :], key_ref[head]
            weights = jnp.exp(jnp.where(allowed, dot_t(key, query), masked_score))
            grad_scores = (weights * dot_t(value_ref[head], grad_out)).astype(low)
            grad_value_ref[head] += dot(weights.astype(low), grad_out)
            grad_key_ref[head] += dot(grad_scores, query)
            grad_query_ref[head, at, :] = t_dot(grad_scores, key)

    for start in range(0, length, block):
        at = slice(start, start + block)
        cosine, sine = cosine_ref[at, :], sine_ref[at, :]
        for base in range(0, heads, 2):

            def joined(ref):
                both = ref[base, at, :]
                if base + 1 < heads:
                    both = jnp.where(lane < half_lanes, both, pltpu.roll(ref[base + 1, at, :], half_lanes, 1))
                else:
                    both = jnp.where(lane < half_lanes, both, 0.0)
                return both

            columns = base // 2 * lanes
            query = joined(grad_query_ref) * 0.125
            key = joined(grad_key_ref)
            value = joined(grad_value_ref)
            query = query * cosine - swap_halves(query) * sine
            key = key * cosine - swap_halves(key) * sine
            for part, result in enumerate((query, key, value)):
                packed_ref[at, part * padded + columns : part * padded + columns + lanes] = result.astype(low)
    for start in range(0, half, block):
        here = slice(start, start + block)
        far_up_ref[here, :] = dot_t(packed_ref[half + start : half + start + block, :], w_ref[...]).astype(low)
        near_up_ref[here, :] = dot_t(packed_ref[here, :], w_ref[...]).astype(low)
    every = lane_ids(length)
    kinds = column_of(kinds_ref[...])
    for head in range(heads):
        grads = grad_key_ref[head]
        same = jnp.sum(jnp.where(every == 72 + kinds, grads, 0.0))
        total = jnp.sum(jnp.where(every == 76, grads, 0.0))
        bias_ref[head, 0] = same
        bias_ref[head, 1] = total - same


def attend_grad(query, key, value, out, grad_out, cosine, sine, ids, w, near, far, extra, place, masks):
    heads, length, _ = query.shape
    half, width = length // 2, w.shape[0]
    vmem, smem = pl.BlockSpec(memory_space=pltpu.VMEM), pl.BlockSpec(memory_space=pltpu.SMEM)
    columns = w.shape[1]
    out_shape = [
        jax.ShapeDtypeStruct((half, width), low),
        jax.ShapeDtypeStruct((half, width), low),
        jax.ShapeDtypeStruct((length, columns), low),
        jax.ShapeDtypeStruct((heads, 2), wide),
    ]
    scratch = [pltpu.VMEM((heads, length, lanes), wide)] * 3 + [pltpu.VMEM((length, 1), jnp.int32)]
    in_specs, out_specs = [vmem] * 10, [vmem] * 3 + [smem]
    operands = [query, key, value, out, grad_out, cosine, sine, *ids, w]
    kernel = functools.partial(attend_grad_kernel, heads, masks)
    if masks:
        share = width // sum(map(len, masks))
        in_specs = [smem, vmem, vmem, vmem] + in_specs
        operands = [place.reshape(1).astype(jnp.int32), near, far, extra] + operands
        out_shape.append(jax.ShapeDtypeStruct((len(masks), len(masks[0]) * share + 16, columns), low))
        out_specs = out_specs + [vmem]
        scratch = scratch + [pltpu.VMEM((width, columns), low)]

        def kernel(*refs):
            before, messages, after = refs[: len(in_specs) + 4], refs[len(in_specs) + 4], refs[len(in_specs) + 5 :]
            attend_grad_kernel(heads, masks, *before, *after[:-1], messages, after[-1])

    return pl.pallas_call(
        kernel,
        out_shape=out_shape,
        in_specs=in_specs,
        out_specs=out_specs,
        scratch_shapes=scratch,
        compiler_params=pltpu.CompilerParams(vmem_limit_bytes=48 * 2**20),
        cost_estimate=pl.CostEstimate(flops=4000 << 20, bytes_accessed=2**10, transcendentals=0),
    )(*operands)


def middle_grad_kernel(middle_ref, grad_out_ref, gain_ref, w_ref, *refs):
    *parts, grads_ref, branch_ref, merged_ref, gain_out_ref = refs
    middle = middle_ref[...]
    inverse = lax.rsqrt(jnp.mean(middle * middle, axis=-1, keepdims=True) + epsilon)
    unit = middle * inverse
    grads = total([part[...] for part in parts])
    gain_out_ref[...] = jnp.sum(grads * unit, axis=0, keepdims=True)
    grads = grads * gain_ref[...]
    mean = jnp.mean(grads * unit, axis=-1, keepdims=True)
    grads = grad_out_ref[...].astype(wide) + inverse * (grads - unit * mean)
    grads_ref[...] = grads
    branch = grads.astype(low)
    branch_ref[...] = branch
    merged_ref[...] = dot_t(branch, w_ref[...]).astype(low)


def middle_grad(middle, grad_out, gain, w, parts):
    return pl.pallas_call(
        middle_grad_kernel,
        out_shape=(
            jax.ShapeDtypeStruct(middle.shape, wide),
            jax.ShapeDtypeStruct(middle.shape, low),
            jax.ShapeDtypeStruct((middle.shape[0], w.shape[0]), low),
            jax.ShapeDtypeStruct((1, middle.shape[1]), wide),
        ),
        cost_estimate=pl.CostEstimate(flops=1 << 20, bytes_accessed=2**10, transcendentals=0),
    )(middle, grad_out, gain, w, *parts)


def feed_kernel(units, tokens_ref, grads_ref, w_ref, hidden_ref, grad_units_ref, up_ref, down_ref):
    gate_up = dot(tokens_ref[...], w_ref[:, : 2 * units])
    count = grads_ref.shape[0] * grads_ref.shape[1]
    grad_hidden = dot(grads_ref[...].reshape(count, -1), w_ref[:, 2 * units :])
    gate_values, up_values = gate_up[:, :units], gate_up[:, units:]
    sigmoid_gate = jax.nn.sigmoid(gate_values)
    activated = gate_values * sigmoid_gate
    hidden_ref[...] = (activated * up_values).astype(low)
    slope = sigmoid_gate + activated * (1.0 - sigmoid_gate)
    grad_units_ref[:, :units] = (grad_hidden * up_values * slope).astype(low)
    grad_units_ref[:, units:] = (grad_hidden * activated).astype(low)
    up_ref[...] = dot_t(grad_units_ref[...], w_ref[:, : 2 * units]).astype(low)
    down_ref[...] = dot_t(hidden_ref[...], w_ref[:, 2 * units :]).astype(low)


def feed(tokens, grads, w):
    count, width = tokens.shape
    rows = count // grads.shape[0]
    units = w.shape[1] // 3
    step = min(count, 512)
    return pl.pallas_call(
        functools.partial(feed_kernel, units),
        grid=(count // step,),
        out_shape=(
            jax.ShapeDtypeStruct((count, units), low),
            jax.ShapeDtypeStruct((count, 2 * units), low),
            jax.ShapeDtypeStruct((count, width), low),
            jax.ShapeDtypeStruct((count, width), low),
        ),
        in_specs=[
            pl.BlockSpec((step, width), lambda i: (i, 0)),
            pl.BlockSpec((step // rows, rows, width), lambda i: (i, 0, 0)),
            pl.BlockSpec(memory_space=pltpu.VMEM),
        ],
        out_specs=(
            pl.BlockSpec((step, units), lambda i: (i, 0)),
            pl.BlockSpec((step, 2 * units), lambda i: (i, 0)),
            pl.BlockSpec((step, width), lambda i: (i, 0)),
            pl.BlockSpec((step, width), lambda i: (i, 0)),
        ),
        compiler_params=pltpu.CompilerParams(vmem_limit_bytes=40 * 2**20),
        cost_estimate=pl.CostEstimate(
            flops=5000 << 20, bytes_accessed=2**10, transcendentals=0
        ),
    )(tokens, grads, w)


def feed_grad_kernel(units, *refs):
    *parts, out_ref = refs
    results = [0.0, 0.0]
    for tokens_ref, grads_ref, hidden_ref, grad_units_ref in (parts[:4], parts[4:]):
        grads = grads_ref[...]
        grads = grads.reshape(grads.shape[0] * grads.shape[1], -1)
        results[0] += t_dot(tokens_ref[...], grad_units_ref[...])
        results[1] += t_dot(grads, hidden_ref[...])
    out_ref[:, : 2 * units] = results[0].astype(low)
    out_ref[:, 2 * units :] = results[1].astype(low)


def feed_grad(near, far):
    tokens, grads, hidden, _ = near
    count, width = tokens.shape
    rows = count // grads.shape[0]
    units = hidden.shape[1]
    step = min(width, 256)
    whole = pl.BlockSpec(memory_space=pltpu.VMEM)
    part = [
        pl.BlockSpec((count, step), lambda i: (0, i)),
        pl.BlockSpec((grads.shape[0], rows, step), lambda i: (0, 0, i)),
        whole,
        whole,
    ]
    return pl.pallas_call(
        functools.partial(feed_grad_kernel, units),
        grid=(width // step,),
        out_shape=jax.ShapeDtypeStruct((width, 3 * units), low),
        in_specs=part + part,
        out_specs=pl.BlockSpec((step, 3 * units), lambda i: (i, 0)),
        compiler_params=pltpu.CompilerParams(vmem_limit_bytes=40 * 2**20),
        cost_estimate=pl.CostEstimate(
            flops=5000 << 20, bytes_accessed=2**10, transcendentals=0
        ),
    )(*near, *far)


def finish_input_kernel(tokens_ref, upstream_ref, grads_ref, out_ref):
    tokens = tokens_ref[...].astype(wide)
    upstream = upstream_ref[...].astype(wide)
    inverse = lax.rsqrt(jnp.mean(tokens * tokens, axis=-1, keepdims=True) + epsilon)
    unit = tokens * inverse
    mean = jnp.mean(upstream * unit, axis=-1, keepdims=True)
    out_ref[...] = (grads_ref[...] + inverse * (upstream - unit * mean)).astype(low)


def finish_input(tokens, upstream, grads):
    return pl.pallas_call(
        finish_input_kernel,
        out_shape=jax.ShapeDtypeStruct(tokens.shape, low),
        cost_estimate=pl.CostEstimate(flops=3000 << 20, bytes_accessed=2**20, transcendentals=0),
    )(tokens, upstream, grads)


def extra_rows(first, second):
    shape = (16, first.shape[1])
    row = lax.broadcasted_iota(jnp.int32, shape, 0)
    result = jnp.zeros(shape, wide)
    for i, value in enumerate((first, second)):
        high = value.astype(low).astype(wide)
        result = jnp.where(row == 2 * i, high, jnp.where(row == 2 * i + 1, value - high, result))
    return result.astype(low)


def moved(row, shift):
    rows = jnp.broadcast_to(row, (8, row.shape[1]))
    return pltpu.roll(rows, lax.rem(shift + row.shape[1], row.shape[1]), 1)[:1]


def first_lanes(row, count):
    return jnp.where(lax.broadcasted_iota(jnp.int32, row.shape, 1) < count, row, 0.0)


def qkv_sum_kernel(z_size, z_ref, *refs):
    *parts, out_ref, sum_ref = refs
    sum_ref[...] = total([part[...] for part in parts])
    count = (sum_ref.shape[0] - 16) // z_size
    extra = sum_ref[sum_ref.shape[0] - 16 :, :]
    bias, gain = extra[0:1] + extra[1:2], extra[2:3] + extra[3:4]
    for d in range(z_size):
        z = jnp.bitwise_xor(z_ref[0], d)
        out_ref[d, :count, :] = sum_ref[pl.ds(pl.multiple_of(z * count, count), count), :].astype(low)
        out_ref[d, count:, :] = extra_rows(bias, first_lanes(moved(gain, -z * count), count))


def qkv_sum(z, z_size, parts):
    rows, columns = parts[0].shape
    vmem = pl.BlockSpec(memory_space=pltpu.VMEM)
    return pl.pallas_call(
        functools.partial(qkv_sum_kernel, z_size),
        out_shape=jax.ShapeDtypeStruct((z_size, (rows - 16) // z_size + 16, columns), low),
        in_specs=[pl.BlockSpec(memory_space=pltpu.SMEM)] + [vmem] * len(parts),
        out_specs=vmem,
        scratch_shapes=[pltpu.VMEM((rows, columns), wide)],
        cost_estimate=pl.CostEstimate(flops=2**20, bytes_accessed=2**10, transcendentals=0),
    )(z.reshape(1).astype(jnp.int32), *parts)


def qkv_pack_kernel(biases, c_ref, *refs):
    *parts, own_ref, sent_ref, extra_ref = refs
    share = own_ref.shape[1]
    c = c_ref[0]
    bias, gain = 0.0, 0.0
    for d, part in enumerate(parts):
        own_ref[d] = part[pl.ds(pl.multiple_of(c * share, share), share), :]
        sent_ref[d * share : (d + 1) * share, :] = part[pl.ds(pl.multiple_of((1 - c) * share, share), share), :]
        extra = part[2 * share :, :].astype(wide)
        bias += moved(first_lanes(extra[0:1] + extra[1:2], biases), d * biases)
        gain += first_lanes(extra[2:3] + extra[3:4], 2 * share)
    gain_sent = first_lanes(moved(gain, -(1 - c) * share), share)
    sent_ref[len(parts) * share :, :] = extra_rows(bias, gain_sent)
    row = lax.broadcasted_iota(jnp.int32, extra_ref.shape, 0)
    gain_own = first_lanes(moved(gain, -c * share), share)
    extra_ref[...] = jnp.where(row == 0, bias, jnp.where(row == 1, gain_own, 0.0))


def qkv_pack(c, share, biases, parts):
    columns = parts[0].shape[1]
    vmem = pl.BlockSpec(memory_space=pltpu.VMEM)
    return pl.pallas_call(
        functools.partial(qkv_pack_kernel, biases),
        out_shape=(
            jax.ShapeDtypeStruct((len(parts), share, columns), low),
            jax.ShapeDtypeStruct((len(parts) * share + 16, columns), low),
            jax.ShapeDtypeStruct((8, columns), wide),
        ),
        in_specs=[pl.BlockSpec(memory_space=pltpu.SMEM)] + [vmem] * len(parts),
        out_specs=(vmem, vmem, vmem),
        cost_estimate=pl.CostEstimate(flops=2**20, bytes_accessed=2**10, transcendentals=0),
    )(c.reshape(1).astype(jnp.int32), *parts)


def finish_qkv_kernel(
    biases, group_ref, own_ref, got_ref, extra_ref, w_ref, gain_ref, out_ref, gain_out_ref, gain_two_ref, bias_ref
):
    count, share, _ = own_ref.shape
    low_half = lane_ids(share) < half_lanes
    gain = gain_ref[...].astype(wide)
    summed = jnp.zeros((share, lanes), wide)
    extra = got_ref[count * share :, :].astype(wide)
    bias_rows = extra_ref[0:1, :], extra[0:1] + extra[1:2]
    bias = jnp.zeros((1, bias_rows[0].shape[1]), wide)
    lane = lax.broadcasted_iota(jnp.int32, bias.shape, 1)
    for i in range(2 * count):
        d, e = i // 2, i % 2
        place = jnp.bitwise_xor(group_ref[0], i)
        parts = []
        for j in range(3):
            columns = slice(j * lanes, (j + 1) * lanes)
            part = got_ref[d * share : (d + 1) * share, columns] if e else own_ref[d, :, columns]
            parts.append(part.astype(wide))
        query, key, value = parts
        key = pltpu.roll(key, half_lanes, 1)
        parts = (
            jnp.where(low_half, query, key),
            jnp.where(low_half, value, query),
            jnp.where(low_half, key, value),
        )
        for j, part in enumerate(parts):
            at = pl.ds(pl.multiple_of(place * (3 * lanes) + j * lanes, lanes), lanes)
            summed += part * w_ref[:, at].astype(wide)
            out_ref[:, at] = part * gain
        here = (lane >= place * biases) & (lane < (place + 1) * biases)
        bias = jnp.where(here, moved(bias_rows[e], place * biases - d * biases), bias)
    column = jnp.broadcast_to(jnp.sum(summed, axis=1, keepdims=True), (share, lanes))
    gain_out_ref[...] = jnp.transpose(column)[:1, :]
    gain_two_ref[...] = (extra_ref[1:2, :] + extra[2:3] + extra[3:4])[:, :lanes]
    bias_ref[...] = bias[:, :lanes]


def finish_qkv(biases, group, own, got, extra, w, gain):
    vmem = pl.BlockSpec(memory_space=pltpu.VMEM)
    share = w.shape[0]
    return pl.pallas_call(
        functools.partial(finish_qkv_kernel, biases),
        out_shape=(
            jax.ShapeDtypeStruct(w.shape, wide),
            jax.ShapeDtypeStruct((1, share), wide),
            jax.ShapeDtypeStruct((1, lanes), wide),
            jax.ShapeDtypeStruct((1, lanes), wide),
        ),
        in_specs=[pl.BlockSpec(memory_space=pltpu.SMEM)] + [vmem] * 5,
        out_specs=(vmem,) * 4,
        cost_estimate=pl.CostEstimate(flops=3000 << 20, bytes_accessed=2**20, transcendentals=0),
    )(group.reshape(1).astype(jnp.int32), own, got, extra, w, gain)


def finish_feed_kernel(x_ref, both_ref, other_ref, gate_ref, up_ref, down_ref):
    depth, units = other_ref.shape[0], other_ref.shape[1] // 3
    mine = pl.ds(pl.multiple_of(x_ref[0] * depth, depth), depth)
    for value, x in ((both_ref[mine, :], x_ref[0]), (other_ref[...], 1 - x_ref[0])):
        at = pl.ds(pl.multiple_of(x * units, units), units)
        parts = [value[:, j * units : (j + 1) * units].astype(wide) for j in range(3)]
        gate_ref[:, at], up_ref[:, at] = parts[:2]
        if down_ref.shape[0] == 2 * units:
            down_ref[at, :] = jnp.transpose(parts[2])
        else:
            down_ref[:, at] = parts[2]


def finish_feed(x, both, other):
    vmem = pl.BlockSpec(memory_space=pltpu.VMEM)
    depth, units = other.shape[0], other.shape[1] // 3
    return pl.pallas_call(
        finish_feed_kernel,
        out_shape=(
            jax.ShapeDtypeStruct((depth, 2 * units), wide),
            jax.ShapeDtypeStruct((depth, 2 * units), wide),
            jax.ShapeDtypeStruct((2 * units, depth) if depth % lanes == 0 else (depth, 2 * units), wide),
        ),
        in_specs=[pl.BlockSpec(memory_space=pltpu.SMEM), vmem, vmem],
        out_specs=(vmem,) * 3,
        cost_estimate=pl.CostEstimate(flops=3000 << 20, bytes_accessed=2**20, transcendentals=0),
    )(x.reshape(1).astype(jnp.int32), both, other)


def rope_tables(stamps, dimension):
    halfway = dimension // 2
    frequency = jnp.exp(-math.log(10000.0) * jnp.arange(halfway, dtype=wide) / halfway)
    repeated = jnp.tile(frequency, lanes // halfway)
    angles = stamps.astype(wide)[:, None] * repeated[None, :]
    sign = jnp.where(jnp.arange(lanes) % dimension < halfway, -1.0, 1.0)
    return (jnp.cos(angles), jnp.sin(angles) * sign[None, :])


def shards(
    inputs,
    gain_attn,
    w_qkv,
    head_bias,
    w_out,
    gain_ffn,
    w_gate,
    w_up,
    w_down,
    time_ids,
    variate_ids,
    seq_ids,
    cotangent,
):
    at = Place()
    z_size, y_size = at.z_size, at.y_size
    tokens = inputs[0].astype(wide)
    rows, width = tokens.shape
    head_count = head_bias.shape[0]
    head_dim = width // head_count
    groups = at.seq_size
    heads = head_count // groups
    group_width = heads * head_dim
    padded = (heads + 1) // 2 * lanes
    share = width // (at.seq_size * at.head_size)
    group = 2 * at.z + at.c
    window = 2 * at.y + at.x
    device_id = at.seq * at.head_size + at.head

    inverse_one = lax.rsqrt(jnp.mean(tokens * tokens, axis=-1, keepdims=True) + epsilon)
    unit = tokens * inverse_one
    turned = called("tokens_turn", at.turn, unit.astype(low))

    depth, units = w_gate.shape[0], w_gate.shape[1] // 2
    gain_one = gain_attn.astype(wide)[:, None]
    scaled = (w_qkv.astype(wide) * gain_one).astype(low)

    def to_parts(columns):
        parts = columns.reshape(-1, groups, heads, 3, head_dim).transpose(0, 1, 3, 2, 4)
        parts = parts.reshape(-1, groups, 3, group_width)
        parts = jnp.pad(parts, ((0, 0), (0, 0), (0, 0), (0, padded - group_width)))
        return parts.reshape(-1, groups, 3 * padded)

    parts = to_parts(scaled).reshape(share, z_size, 2, 3 * padded)
    core_own = pick(at.c, parts[:, :, 0], parts[:, :, 1])
    core_sent = pick(at.c, parts[:, :, 1], parts[:, :, 0]).reshape(-1, 3 * padded)

    def with_extra(block, *values):
        extra = jnp.stack([jnp.pad(v.astype(low), (0, 3 * padded - v.shape[0])) for v in values])
        return jnp.concatenate([block, jnp.pad(extra, ((0, 16 - len(values)), (0, 0)))], axis=0)

    core_got = called("qkv_core", at.along_c, with_extra(core_sent, gain_ffn))
    both = jnp.stack([core_own, core_got[:-16].reshape(core_own.shape)])
    out_z = called("out_z", at.gather_steps, w_out, at.z_moves()).reshape(-1, width)
    gains = jnp.concatenate([gain_ffn, core_got[-16, :share]])
    sent = []
    for d in range(z_size):
        block = lax.dynamic_index_in_dim(both, jnp.bitwise_xor(at.z, d), axis=2, keepdims=False)
        sent.append(with_extra(block.reshape(-1, 3 * padded), gains))
    by_z = jnp.stack(called("qkv_z", at.scatter_z, sent))
    gains = by_z[:, -16, : 2 * share].reshape(-1)
    by_z = by_z[:, :-16].reshape(-1, 3 * padded)
    late_gate, late_up, late_down = w_gate, w_up, w_down
    by_z, late_gate, late_up, late_down = tied(by_z, w_gate, w_up, w_down)
    units = w_gate.shape[1] // 2
    down_t = with_layout_constraint(late_down.T, Layout(major_to_minor=(0, 1)))
    firsts = jnp.concatenate([v[:, :units] for v in (late_gate, late_up, down_t)], axis=1)
    seconds = jnp.concatenate([v[:, units:] for v in (late_gate, late_up, down_t)], axis=1)
    mine = pick(at.x, firsts, seconds)
    other = called("ffn_x", at.along_x, pick(at.x, seconds, firsts))
    z_block = jnp.concatenate([pick(at.x, mine, other), pick(at.x, other, mine)], axis=0)

    z_early = z_block
    near = called("tokens_z", at.gather_steps, turned, at.z_moves()[:-1])
    near = near
    near = join(near, called("tokens_z", at.z_moves()[-1], near)).reshape(-1, width)
    by_xy = jnp.stack(called("qkv_xy", at.gather_xy, with_extra(by_z, gains)))
    gains = by_xy[:, -16, : gains.shape[0]].reshape(y_size, 2, z_size, 2, share)
    gains = gains.transpose(2, 1, 0, 3, 4).reshape(-1, share)
    by_xy = by_xy[:, :-16]
    devices = jnp.arange(at.seq_size * at.head_size)
    from_device = (devices[None, :] == jnp.bitwise_xor(devices[:, None], device_id)).astype(low)
    gain_two = dot(from_device, gains).reshape(1, width)
    masks = [
        (2 * d + dx) * at.head_size + 2 * dy + e
        for dx, dy in at.pairs()
        for d in range(z_size)
        for e in range(2)
    ]
    w_heads = place(by_xy.reshape(-1, share, 3 * padded), device_id, masks).reshape(width, 3 * padded)

    out_xy = called("out_xy", at.gather_steps, out_z, at.xy_moves())

    grad_out = cotangent[0]
    grad_out_near = called("cotangent_x", at.gather_steps, grad_out, at.xy_moves()[:1])

    near, w_heads = tied(near, w_heads)
    near, out_xy = tied(near, out_xy)
    near, grad_out_near = tied(near, grad_out_near)
    w_ffn = lax.all_gather(z_block, "seq", axis=0, tiled=True, axis_index_groups=at.columns_z())

    time_ids, variate_ids, seq_ids, by_z = tied(time_ids, variate_ids, seq_ids, by_z)

    def of_window(ids):
        row = lax.dynamic_index_in_dim(ids, window, axis=0, keepdims=False).reshape(z_size, 2, rows)
        order = [
            lax.dynamic_slice(
                row, (jnp.bitwise_xor(at.z, d), jnp.bitwise_xor(at.c, e), 0), (1, 1, rows)
            ).reshape(rows)
            for e in range(2)
            for d in at.z_order()
        ]
        return jnp.concatenate(order)

    ids = (of_window(variate_ids).reshape(1, -1), of_window(seq_ids).reshape(1, -1))
    cosine, sine = rope_tables(of_window(time_ids), head_dim)
    local_bias = lax.dynamic_slice_in_dim(head_bias, group * heads, heads, 0)
    difference = local_bias[:, 0] - local_bias[:, 1]
    difference_high = difference.astype(low).astype(wide)
    bias = jnp.stack([difference_high, difference - difference_high])

    near, w_heads, cosine, sine, ids = tied(near, w_heads, cosine, sine, ids)
    far = called("tokens_core", at.along_c, near)
    query, key, value, attended = attend(bias, near, far, w_heads, cosine, sine, ids, heads)

    out_far = called("out_core", at.along_c, out_xy)
    out_blocks = jnp.stack([out_xy, out_far]).reshape(-1, share, width)
    out_masks = [
        (dx * z_size + d) * at.head_size + 2 * dy + e
        for e in range(2)
        for dx, dy in at.pairs()
        for d in range(z_size)
    ]
    out_rows = place(out_blocks, at.head, out_masks).reshape(width, width)

    sent = attended[:, :group_width].reshape(2, z_size, rows, group_width)
    places = {d: i for i, d in enumerate(at.z_order())}
    received = called("attended_z", at.scatter_z, [sent[:, places[d]] for d in range(z_size)])
    received = [received[d] for d in at.z_order()]
    kept = jnp.concatenate([block[0] for block in received], axis=1)
    passed = jnp.concatenate([block[1] for block in received], axis=1)
    held = grad_out_near[None]
    for move in at.xy_moves()[1:]:
        got = called("cotangent_y", move, held)
        got, passed = tied(got, passed)
        held = jnp.concatenate([held, got], axis=0)
    grad_out_near = held.reshape(2 * y_size, rows, width)
    grad_out_far = called("cotangent_core", at.along_c, grad_out_near)

    passed = called("attended_core", at.along_c, passed)

    merged = called("attended_turn", at.turn, jnp.concatenate([kept, passed], axis=1))

    middle = tokens + dot(merged, out_rows)
    inverse_two = lax.rsqrt(jnp.mean(middle * middle, axis=-1, keepdims=True) + epsilon)
    unit_two = middle * inverse_two
    normed_two = (unit_two * gain_two).astype(low)
    normed_near = jnp.concatenate(called("normed_xy", at.gather_xy, normed_two), axis=0)
    normed_far = called("normed_core", at.along_c, normed_near)

    hidden_far, units_far, up_far, down_far = feed(normed_far, grad_out_far, w_ffn)
    hidden_near, units_near, up_near, down_near = feed(normed_near, grad_out_near, w_ffn)

    blocks = (2 * y_size, rows, width)
    up = up_near.reshape(blocks), called("up_core", at.along_c, up_far).reshape(blocks)
    kept = [total([part[i] for part in up]).astype(low) for i in range(2 * y_size)]
    grad_w_ffn = feed_grad(
        (normed_near, grad_out_near, hidden_near, units_near),
        (normed_far, grad_out_far, hidden_far, units_far),
    )
    received = called("up_xy", at.scatter_xy, kept)
    down = [down_near.reshape(blocks), called("down_core", at.along_c, down_far).reshape(blocks)]
    moves = at.xy_moves()
    y_cut = y_size // 2
    down = [part.reshape(y_size, 2, rows, width) for part in down]
    down_sent = total([part[y_cut:] for part in down]).astype(low)
    received[0], down_sent = tied(received[0], down_sent)
    down = [part[:y_cut] for part in down] + [called("down_y", moves[-1], down_sent)]
    *received[1:], grad_w_ffn = tied(*received[1:], grad_w_ffn)
    grad_middle, grad_branch, grad_merged, gain_part = middle_grad(middle, grad_out, gain_two, out_rows, received)

    turned_back = called("merged_turn", at.turn, grad_merged)
    grad_w_ffn = lax.psum_scatter(
        grad_w_ffn, "seq", scatter_dimension=0, tiled=True, axis_index_groups=at.columns_z()
    )
    cut = width // 2
    kept, passed = turned_back[:, :cut], called("merged_core", at.along_c, turned_back[:, cut:])
    merged, grad_branch, passed = tied(merged, grad_branch, passed)
    sent = []
    for d in range(z_size):
        columns = slice(places[d] * group_width, (places[d] + 1) * group_width)
        sent.append(jnp.stack([part[:, columns] for part in (kept, passed)]))
    received_z = called("merged_z", at.scatter_z, sent)
    received_one = received_z[1]

    grad_out_rows = t_dot(merged, grad_branch).astype(low)
    grad_out_rows = fetch(grad_out_rows.reshape(-1, share, width), at.head, out_masks)
    grad_out_rows = grad_out_rows.reshape(2, y_size, 2, z_size * share, width)
    out_parts = [grad_out_rows[0], called("w_out_core", at.along_c, grad_out_rows[1])]
    out_sent = total([part[y_cut:] for part in out_parts]).astype(low)
    received_one, out_sent = tied(received_one, out_sent)
    received_z[1] = received_one
    received = jnp.stack([received_z[d] for d in at.z_order()], axis=1)
    grad_attended = received.reshape(2 * z_size * rows, group_width)
    if padded > group_width:
        grad_attended = jnp.pad(grad_attended, ((0, 0), (0, padded - group_width)))
    down = called("down_y", at.scatter_steps, down, moves[1:-1])
    down = [part.reshape(2, rows, width) for part in down]
    down_sent = total([part[1] for part in down]).astype(low)
    down = [part[0] for part in down] + [called("down_x", moves[0], down_sent)]
    grad_attended, out_sent = tied(grad_attended, out_sent)
    grad_attended, down[-1] = tied(grad_attended, down[-1])
    out_got = called("w_out_y", moves[-1], out_sent)
    out_parts = [part[:y_cut] for part in out_parts] + [out_got]

    def halves(values):
        high = values.astype(low)
        return high, (values - high.astype(wide)).astype(low)

    gain_part = gain_part.reshape(z_size, 2, y_size, 2, share)
    bias_count, gain_count = 2 * heads, 2 * z_size * share
    extra, device_masks = [], []
    for dx, dy in at.pairs():
        x, y = jnp.bitwise_xor(at.x, dx), jnp.bitwise_xor(at.y, dy)
        gain = lax.dynamic_slice(gain_part, (0, x, y, 0, 0), (z_size, 1, 1, 2, share)).reshape(-1)
        none = jnp.zeros((0, 3 * padded), low)
        extra.append(with_extra(none, *(jnp.zeros_like(v) for v in halves(gain)), *halves(gain)))
        device_masks.append([
            (2 * d + dx) * at.head_size + 2 * dy + e for d in range(z_size) for e in range(2)
        ])
    extra = jnp.stack(extra)
    place_xy = at.x * at.head_size + 2 * at.y
    in_kernel = share % 16 == 0
    upstream_near, upstream_far, grad_packed, bias_grad, *messages = attend_grad(
        query, key, value, attended, grad_attended, cosine, sine, ids, w_heads,
        near, far, extra, place_xy, device_masks if in_kernel else None,
    )
    half = near.shape[0]
    if in_kernel:
        messages = [messages[0][i] for i in range(2 * y_size)]
    else:
        grad_heads = t_dot(near, grad_packed[:half]) + t_dot(far, grad_packed[half:])
        grad_heads = grad_heads.astype(low).reshape(-1, share, 3 * padded)
        none = jnp.zeros((0, 3 * padded), low)
        biases = with_extra(none, *halves(bias_grad.reshape(-1)))
        messages = [
            jnp.concatenate([
                lax.dynamic_index_in_dim(grad_heads, jnp.bitwise_xor(place_xy, mask), 0, False)
                for mask in masks
            ] + [extra[i] + biases])
            for i, masks in enumerate(device_masks)
        ]

    upstream_far, out_parts[-1] = tied(upstream_far, out_parts[-1])
    upstream_far = called("input_core", at.along_c, upstream_far)
    z_moves = at.z_moves()
    blocks = (z_size, rows, width)
    upstream_z = [upstream_near.reshape(blocks), upstream_far.reshape(blocks)]
    z_cut = z_size // 2
    upstream_sent = total([part[z_cut:] for part in upstream_z]).astype(low)
    upstream_z = [part[:z_cut] for part in upstream_z] + [called("input_z", z_moves[-1], upstream_sent)]

    out_parts = called("w_out_y", at.scatter_steps, out_parts, moves[1:-1])
    out_parts = [part.reshape(2, -1, width) for part in out_parts]
    out_parts = called("w_out_x", at.scatter_steps, out_parts, moves[:1])
    out_parts[-1] = out_parts[-1]

    def joined(block, row, count):
        return block[row, :count].astype(wide) + block[row + 1, :count].astype(wide)

    received = called("grad_qkv_xy", at.scatter_xy, messages)
    fast = in_kernel and heads == 2 and head_dim == half_lanes
    if fast:
        sent = qkv_sum(at.z, z_size, received)
    else:
        summed = total(received)
        bias_sum = joined(summed[-16:], 0, bias_count)
        gain_sum = joined(summed[-16:], 2, gain_count).reshape(z_size, 2 * share)
        summed = summed[:-16].astype(low).reshape(z_size, 2 * share, 3 * padded)
        sent = []
        for d in range(z_size):
            block, gain = (
                lax.dynamic_index_in_dim(v, jnp.bitwise_xor(at.z, d), axis=0, keepdims=False)
                for v in (summed, gain_sum)
            )
            sent.append(with_extra(block, *halves(bias_sum), *halves(gain)))
    depth = grad_w_ffn.shape[0] // 2
    other = lax.dynamic_slice_in_dim(grad_w_ffn, (1 - at.x) * depth, depth, 0)
    other = called("grad_ffn_x", at.along_x, other)
    upstream_z[-1], other = tied(upstream_z[-1], other)
    upstream_z[-1], sent = tied(upstream_z[-1], sent)
    z_cut = z_cut // 2
    upstream_sent = total([part[z_cut:] for part in upstream_z]).astype(low)
    upstream_sent, sent = tied(upstream_sent, sent)
    upstream_z = [part[:z_cut] for part in upstream_z] + [called("input_z", z_moves[-2], upstream_sent)]
    grad_w_gate, grad_w_up, grad_w_down = finish_feed(at.x, grad_w_ffn, other)
    if grad_w_down.shape != w_down.shape:
        grad_w_down = grad_w_down.T
    upstream_z[-1] = after(upstream_z[-1], grad_w_gate)
    upstream_one = total(called("input_z", at.scatter_steps, upstream_z, z_moves[:-2]))[0]
    out_parts[-1] = out_parts[-1]
    output = middle + total(down)
    out_parts = [part.reshape(z_size, share, width) for part in out_parts]
    grad_w_out = total(called("w_out_z", at.scatter_steps, out_parts, z_moves))[0]
    received = called("grad_qkv_z", at.scatter_z, [sent[d] for d in range(z_size)])
    upstream_one, received[0] = tied(upstream_one, received[0])
    if fast:
        core_own, core_sent, extra_own = qkv_pack(at.c, share, bias_count, received)
    else:
        bias_z = jnp.concatenate([joined(block[-16:], 0, bias_count) for block in received])
        gain_sum = functools.reduce(jnp.add, [joined(block[-16:], 2, 2 * share) for block in received])
        received = jnp.stack([block[:-16] for block in received]).reshape(z_size, 2, share, 3 * padded)
        core_own = pick(at.c, received[:, 0], received[:, 1])
        core_sent = pick(at.c, received[:, 1], received[:, 0]).reshape(-1, 3 * padded)
        gain_own = pick(at.c, gain_sum[:share], gain_sum[share:])
        gain_sent = pick(at.c, gain_sum[share:], gain_sum[:share])
        core_sent = with_extra(core_sent, *halves(bias_z), *halves(gain_sent))
    upstream_one = upstream_one.astype(low)
    core_sent = core_sent
    upstream_one = called("input_turn", at.turn, upstream_one)
    grad_input = finish_input(inputs[0], upstream_one, grad_middle)
    core_got = called("grad_qkv_core", at.along_c, core_sent)
    if fast:
        grad_w_qkv, grad_gain_attn, grad_gain_ffn, full_bias = finish_qkv(
            bias_count, group, core_own, core_got, extra_own, w_qkv, gain_attn[:, None]
        )
        grad_gain_attn, grad_gain_ffn = grad_gain_attn[0], grad_gain_ffn[0, :share]
        full_bias = full_bias[0, : 2 * head_count].reshape(head_count, 2)
    else:
        core_other = core_got[:-16].reshape(z_size, share, 3 * padded)
        grad_gain_ffn = gain_own + joined(core_got[-16:], 2, share)
        biases = jnp.stack([bias_z, joined(core_got[-16:], 0, z_size * bias_count)])
        biases = list(biases.reshape(2, z_size, heads, 2).transpose(1, 0, 2, 3).reshape(groups, heads, 2))
        full_bias = jnp.concatenate(xor_list(biases, group), axis=0)
        by_group = jnp.stack([core_own, core_other], axis=1).reshape(groups, share, 3 * padded)
        by_group = place(by_group, group, list(range(groups))).astype(wide).reshape(groups, share, 3, padded)
        by_group = by_group[..., :group_width].reshape(groups, share, 3, heads, head_dim)
        raw = by_group.transpose(1, 0, 3, 2, 4).reshape(share, 3 * width)
        grad_w_qkv = raw * gain_one
        grad_gain_attn = jnp.sum(raw * w_qkv.astype(wide), axis=1)

    return (
        output.astype(low).reshape(1, rows, width),
        grad_input.reshape(1, rows, width),
        grad_gain_attn,
        grad_w_qkv,
        full_bias,
        grad_w_out,
        grad_gain_ffn,
        grad_w_gate,
        grad_w_up,
        grad_w_down,
    )


def solution(mesh):
    placed = (
        P("head", "seq", None),
        P(("seq", "head")),
        P(("seq", "head"), None),
        P(),
        P(("seq", "head"), None),
        P(("seq", "head")),
        P("seq", "head"),
        P("seq", "head"),
        P("head", "seq"),
        P(),
        P(),
        P(),
        P("head", "seq", None),
    )
    return jax.shard_map(
        shards,
        mesh=mesh,
        in_specs=placed,
        out_specs=(
            P("head", "seq", None),
            P("head", "seq", None),
            P(("seq", "head")),
            P(("seq", "head"), None),
            P(),
            P(("seq", "head"), None),
            P(("seq", "head")),
            P("seq", "head"),
            P("seq", "head"),
            P("head", "seq"),
        ),
        check_vma=False,
    )
```
